512 devices in a mesh: blocks: 64 (over y, z), octant: 8 (over x, core).
Axes of the slice: x: 4, y: 8, z: 8, core: 2. Of those that a mesh axis runs over, the one named last changes fastest.
Arguments:
- em_store: bfloat16 [8, 4096, 64], P('octant', 'blocks'), may hold values from 0 to 1, as said below
- route_block: int32 [8, 4096], P('octant', 'blocks'), may hold values from 0 to 63, as said below
- route_slot: int32 [8, 4096], P('octant', 'blocks'), may hold values from 0 to 63, as said below
- conv1_w: bfloat16 [32, 27], replicated, may hold values from -1.25 to 1.25
- conv1_b: float32 [32], replicated, may hold values from -3 to 3
- conv2_w: bfloat16 [27, 32, 32], replicated, may hold values from -0.21875 to 0.21875
- conv2_b: float32 [32], replicated, may hold values from -3 to 3
- head_w: bfloat16 [3, 32], replicated, may hold values from -1 to 1
- head_b: float32 [3], replicated, may hold values from -3 to 3
Outputs:
- affinities: float32 [8, 64, 3, 4096], P('octant', 'blocks')
The draws below stay inside these ranges and needn't reach their ends.
Inputs may be any that keep to these rules, and one draw needn't show every extreme that they name: For each octant index, the pairs (route_block, route_slot) are all distinct, so every tile receives exactly 64 sub-blocks; the sub-blocks that one storage device sends to one tissue block are at most 2, and every storage device sends exactly 2 to some tissue block. `route_slot`: slot s lies at sub-block coordinates (s // 4 ** 2, s // 4 % 4, s % 4) of the tile. `em_store`: the tiles of one tissue block are cut from one volume of that block: where two tiles cover the same voxel they hold the same intensity.
All inputs are finite; a program needn't handle non-finite values.
Results may differ from the reference program's by a relative error of at most 0.002.
Values may be sent and summed in bfloat16 or wider, within the bound.
A program may use at most 64 MiB of HBM per device.

```python
import jax
import jax.numpy as jnp
from jax import lax

C1 = 32
AFF = 3
SB = 4
TS = 4
TILE = 16
SUBS = 64
OVL = 6
STEP = 10
CAP = 2
BITS = 3
N_BLOCKS = 64
N_OCTANT = 8


def route_tables(key):

    def column(column_key):
        key_rho, key_shift, key_ticket, key_sigma = jax.random.split(column_key, 4)
        rho = jax.random.permutation(key_rho, N_BLOCKS).astype(jnp.int32)
        rank_of = jnp.argsort(rho).astype(jnp.int32)
        shifts = jax.random.permutation(key_shift, N_BLOCKS).astype(jnp.int32)
        rest = CAP + jax.random.permutation(key_ticket, N_BLOCKS * CAP - CAP)[:SUBS - CAP].astype(jnp.int32)
        tickets = jnp.concatenate([jnp.arange(CAP, dtype=jnp.int32), rest])
        groups = tickets // CAP
        order_key = groups * SUBS + jnp.arange(SUBS, dtype=jnp.int32)
        position = jnp.argsort(jnp.argsort(order_key)).astype(jnp.int32)
        sources = jnp.arange(N_BLOCKS, dtype=jnp.int32)
        targets = rho[(rank_of[sources][:, None] + shifts[groups][None, :]) % N_BLOCKS]
        sigma_keys = jax.random.split(key_sigma, N_BLOCKS)
        sigma = jax.vmap(lambda sigma_key: jax.random.permutation(sigma_key, SUBS).astype(jnp.int32))(sigma_keys)
        slots = sigma[targets, jnp.broadcast_to(position[None, :], targets.shape)]
        return (targets.reshape(-1).astype(jnp.int32), slots.reshape(-1).astype(jnp.int32))
    return jax.vmap(column)(jax.random.split(key, N_OCTANT))


def draw_route_block(key, part):
    tables = route_tables(key)
    return tables[0].astype(jnp.int32)


def draw_route_slot(key, part):
    tables = route_tables(key)
    return tables[1].astype(jnp.int32)


def draw_em_store(key, part):
    tables = route_tables(key)
    key = jax.random.fold_in(key, 7)
    extents = [TILE + STEP if axis_dim < BITS else TILE for axis_dim in range(3)]
    volume = jax.random.uniform(key, (N_BLOCKS, extents[0], extents[1], extents[2]), jnp.float32, 0.0, 1.0)
    stores = []
    for octant_index in range(N_OCTANT):
        starts = [(octant_index >> axis_dim & 1) * STEP if axis_dim < BITS else 0 for axis_dim in range(3)]
        tile = volume[:, starts[0]:starts[0] + TILE, starts[1]:starts[1] + TILE, starts[2]:starts[2] + TILE]
        tile = tile.reshape(N_BLOCKS, TS, SB, TS, SB, TS, SB).transpose(0, 1, 3, 5, 2, 4, 6)
        tile = tile.reshape(N_BLOCKS, SUBS, SB ** 3)
        stores.append(tile[tables[0][octant_index], tables[1][octant_index]])
    return jnp.stack(stores, 0).astype(jnp.bfloat16)


def gaussian(key, shape, deviation, limit, held_as=jnp.bfloat16):
    entries = deviation * jax.random.normal(key, shape, jnp.float32)
    return jnp.clip(entries, min=-limit, max=limit).astype(held_as)


def setup_inputs(seed: int = 0) -> dict:
    key_of = jax.random.split(jax.random.key(seed), 10)
    return {
        "em_store": draw_em_store(jax.random.fold_in(key_of[9], 71), 0),
        "route_block": draw_route_block(jax.random.fold_in(key_of[9], 71), 0),
        "route_slot": draw_route_slot(jax.random.fold_in(key_of[9], 71), 0),
        "conv1_w": gaussian(key_of[3], (C1, 27), 27 ** -0.5, 1.25),
        "conv1_b": gaussian(key_of[4], (C1,), 0.5, 3.0, jnp.float32),
        "conv2_w": gaussian(key_of[5], (27, C1, C1), (27 * C1) ** -0.5, 0.21875),
        "conv2_b": gaussian(key_of[6], (C1,), 0.5, 3.0, jnp.float32),
        "head_w": gaussian(key_of[7], (AFF, C1), C1 ** -0.5, 1.0),
        "head_b": gaussian(key_of[8], (AFF,), 1.0, 3.0, jnp.float32),
    }


def conv_same(volume, kernel):
    edge_len = volume.shape[1]
    padded = jnp.pad(volume, ((0, 0), (1, 1), (1, 1), (1, 1)))
    summed = jnp.zeros((kernel.shape[1], edge_len, edge_len, edge_len), jnp.float32)
    for tap_index in range(27):
        shift_x = tap_index // 9
        shift_y = (tap_index // 3) % 3
        shift_z = tap_index % 3
        window = padded[:, shift_x:shift_x + edge_len, shift_y:shift_y + edge_len, shift_z:shift_z + edge_len]
        summed = summed + jnp.einsum("oc,cxyz->oxyz", kernel[tap_index], window)
    return summed


def predict(tile_em, first_kernel, first_bias, second_kernel, second_bias, head_kernel, head_bias):
    volume = tile_em.reshape(TS, TS, TS, SB, SB, SB).transpose(0, 3, 1, 4, 2, 5)
    volume = volume.reshape(1, TILE, TILE, TILE).astype(jnp.float32)
    hidden_one = jax.nn.relu(conv_same(volume, first_kernel) + first_bias[:, None, None, None]).astype(jnp.bfloat16)
    hidden_one = lax.optimization_barrier(hidden_one)
    hidden_two = jax.nn.relu(conv_same(hidden_one.astype(jnp.float32), second_kernel) + second_bias[:, None, None, None]).astype(jnp.bfloat16)
    hidden_two = lax.optimization_barrier(hidden_two)
    logits = jnp.einsum("ac,cxyz->axyz", head_kernel, hidden_two.astype(jnp.float32)) + head_bias[:, None, None, None]
    return jax.nn.sigmoid(logits)


def ramp_for(own_bit):
    position = jnp.arange(TILE, dtype=jnp.float32)
    if own_bit == 1:
        return jnp.clip((position + 0.5) / OVL, 0.0, 1.0)
    return jnp.clip((TILE - position - 0.5) / OVL, 0.0, 1.0)


def blend_weights(octant_index):
    factors = []
    for axis_dim in range(3):
        if axis_dim < BITS:
            factors.append(ramp_for((octant_index >> axis_dim) & 1))
        else:
            factors.append(jnp.ones((TILE,), jnp.float32))
    return factors[0][:, None, None] * (factors[1][:, None] * factors[2][None, :])[None]


def reference(em_store, route_block, route_slot, conv1_w, conv1_b, conv2_w, conv2_b, head_w, head_b):
    octant_ids = jnp.broadcast_to(jnp.arange(N_OCTANT, dtype=jnp.int32)[:, None], route_block.shape).astype(jnp.int32)
    em_tiles = jnp.zeros((N_OCTANT, N_BLOCKS, SUBS, SB ** 3), jnp.bfloat16)
    em_tiles = em_tiles.at[octant_ids, route_block.astype(jnp.int32), route_slot.astype(jnp.int32)].set(em_store)
    first_kernel = conv1_w.astype(jnp.float32).T[:, :, None]
    second_kernel = conv2_w.astype(jnp.float32)
    head_kernel = head_w.astype(jnp.float32)

    def one_tile(tile_em):
        return predict(tile_em, first_kernel, conv1_b, second_kernel, conv2_b, head_kernel, head_b)

    predictions = lax.map(one_tile, em_tiles.reshape(N_OCTANT * N_BLOCKS, SUBS, SB ** 3))
    predictions = predictions.reshape(N_OCTANT, N_BLOCKS, AFF, TILE, TILE, TILE)
    extents = [TILE + STEP if axis_dim < BITS else TILE for axis_dim in range(3)]
    canvas = jnp.zeros((N_BLOCKS, AFF, extents[0], extents[1], extents[2]), jnp.float32)
    corners = []
    for octant_index in range(N_OCTANT):
        starts = [((octant_index >> axis_dim) & 1) * STEP if axis_dim < BITS else 0 for axis_dim in range(3)]
        blended = predictions[octant_index] * blend_weights(octant_index)[None, None]
        canvas = canvas.at[:, :, starts[0]:starts[0] + TILE, starts[1]:starts[1] + TILE, starts[2]:starts[2] + TILE].add(blended)
        corners.append(starts)
    outputs = []
    for starts in corners:
        region = canvas[:, :, starts[0]:starts[0] + TILE, starts[1]:starts[1] + TILE, starts[2]:starts[2] + TILE]
        outputs.append(region.reshape(N_BLOCKS, AFF, TILE ** 3))
    return jnp.stack(outputs, 0)
```

```python
import jax
import jax.numpy as jnp
from jax import lax
from jax.experimental import pallas as pl
from jax.experimental.pallas import tpu as pltpu
from jax.sharding import PartitionSpec as P

TILE = 16
OVL = 6
LANES = TILE * TILE
C1 = 32
AFF = 3
MESH = pl.DeviceIdType.MESH
F32 = jnp.float32
BF16 = jnp.bfloat16


def iota(shape, dim):
    return lax.broadcasted_iota(jnp.int32, shape, dim)


def dot(a, b):
    return jnp.dot(a, b, preferred_element_type=F32)


def column(row):
    n = row.shape[1]
    return jnp.sum(jnp.where(iota((n, n), 0) == iota((n, n), 1), row, 0.0), axis=1, keepdims=True)


def pack_rows(em, targets, slots):
    n = em.shape[0]
    target_row = targets.astype(F32)
    target_col = column(target_row)
    earlier = (target_col == target_row) & (iota((n, n), 0) < iota((n, n), 1))
    rank_row = jnp.sum(jnp.where(earlier, 1.0, 0.0), axis=0, keepdims=True)
    slot_row = slots
    i_col = column((slot_row // 16 + 1).astype(F32))
    jk_col = column((slot_row % 16).astype(F32))
    lane = iota((n, 128), 1)
    spread = iota((64, 128), 0) == iota((64, 128), 1)
    wide = dot(em, spread.astype(F32).astype(BF16))
    wide = jnp.where(lane == 64, i_col, jnp.where(lane == 65, jk_col, wide)).astype(BF16)
    here = iota((64, n), 0).astype(F32) == target_row
    parts = [
        dot((here & (rank_row == rank)).astype(F32).astype(BF16), wide) for rank in (0.0, 1.0)
    ]
    return jnp.concatenate(parts, axis=1)


def expander():
    row = iota((128, 4 * LANES), 0)
    col = iota((128, 4 * LANES), 1)
    wanted = (col // LANES) * 16 + (col // 16 % 4) * 4 + col % 4
    return (row == wanted).astype(F32).astype(BF16)


def unpack_volume(arrived, expand):
    rows = jnp.concatenate([arrived[:, :128], arrived[:, 128:]], axis=0)
    i_col = rows[:, 64:65]
    jk_col = rows[:, 65:66]
    eye = iota((128, 128), 0) == iota((128, 128), 1)
    i_row = jnp.sum(jnp.where(eye, i_col, 0.0), axis=0, keepdims=True)
    lane = iota((128, LANES), 1)
    lane_jk = (lane // 64 * 4 + lane // 4 % 4).astype(F32)
    inside = lane_jk == jk_col
    spread = dot(rows.astype(BF16), expand)
    x_row = iota((TILE, 128), 0)
    volume = jnp.zeros((TILE, LANES), F32)
    for a in range(4):
        masked = jnp.where(inside, spread[:, a * LANES : (a + 1) * LANES], 0.0).astype(BF16)
        wanted = (x_row % 4 == a) & ((x_row // 4 + 1).astype(F32) == i_row)
        volume = volume + dot(wanted.astype(F32).astype(BF16), masked)
    return volume


def first_matrix(conv1_w):
    tap = iota((27, LANES), 0)
    col = iota((27, LANES), 1)
    x_in = iota((TILE, C1, LANES), 2) % TILE
    x_out = iota((TILE, C1, LANES), 0)
    total = jnp.zeros((TILE, C1, LANES), F32)
    for dx in range(3):
        spread = ((tap == 9 * dx + col // TILE) & (col < 9 * TILE)).astype(F32).astype(BF16)
        rows = dot(conv1_w, spread)
        total = jnp.where(x_in == x_out + dx - 1, rows[None], total)
    return total.reshape(TILE * C1, LANES).astype(BF16)


def replicated(weights, count):
    shape = (C1, count * C1)
    return dot(weights, (iota(shape, 0) == iota(shape, 1) % C1).astype(F32).astype(BF16))


def shift_lanes(value, by, roll):
    return roll(value, (-by) % value.shape[-1], value.ndim - 1)


def conv1_columns(volume, roll):
    lane = iota((TILE, LANES), 1)
    y, z = lane // TILE, lane % TILE
    rows = []
    for dy in (-1, 0, 1):
        for dz in (-1, 0, 1):
            moved = volume
            if dy or dz:
                moved = shift_lanes(volume, dy * TILE + dz, roll)
                keep = (y + dy >= 0) & (y + dy < TILE) & (z + dz >= 0) & (z + dz < TILE)
                moved = jnp.where(keep, moved, 0.0)
            rows.append(moved)
    rows.append(jnp.zeros((LANES - 9 * TILE, LANES), F32))
    return jnp.concatenate(rows, axis=0).astype(BF16)


def z_shifted(half, roll):
    z = iota(half.shape, 1) % TILE
    before = jnp.where(z > 0, shift_lanes(half, -1, roll), 0.0)
    after = jnp.where(z < TILE - 1, shift_lanes(half, 1, roll), 0.0)
    return jnp.concatenate([before, half, after], axis=0).astype(BF16)


def head_matrix(head_w):
    wide = replicated(head_w, TILE)
    x_in = iota((TILE, TILE * C1), 1) // C1
    x_out = iota((TILE, TILE * C1), 0)
    rows = [jnp.where(x_in == x_out, wide[a : a + 1], 0.0) for a in range(AFF)]
    return jnp.concatenate(rows, axis=0).astype(BF16)


def ramp(position, bit):
    lower = jnp.minimum((TILE - position - 0.5) / OVL, 1.0)
    upper = jnp.minimum((position + 0.5) / OVL, 1.0)
    return jnp.where(bit == 1, upper, lower)


def blend_weights(bits):
    lane = iota((TILE, LANES), 1)
    x = iota((TILE, LANES), 0).astype(F32)
    y = (lane // TILE).astype(F32)
    z = (lane % TILE).astype(F32)
    return ramp(x, bits[0]) * (ramp(y, bits[1]) * ramp(z, bits[2]))


def move_x(low, high, bit, roll):
    row = iota(low.shape, 1)
    from_high = jnp.where(row < OVL, roll(high, 6, 1), 0.0)
    from_low = jnp.where(row >= 8 - OVL, roll(low, 2, 1), 0.0)
    return jnp.where(bit == 0, from_high, from_low)


def move_y(low, high, bit, roll):
    lane = iota(low.shape, 2)
    from_high = jnp.where(lane < OVL * TILE, roll(high, 96, 2), 0.0)
    from_low = jnp.where(lane >= 128 - OVL * TILE, roll(low, 32, 2), 0.0)
    return jnp.where(bit == 0, from_high, from_low)


def pack_z(first, second, bit, roll):
    z = iota(first.shape, 2) % TILE
    head = jnp.where(bit == 0, roll(first, 128 - 10, 2), first)
    tail = jnp.where(bit == 0, roll(second, 128 - 2, 2), roll(second, 8, 2))
    return jnp.where(z < 8, head, tail)


def unpack_z(packed, bit, roll):
    z = iota(packed.shape, 2) % TILE
    keep = jnp.where(bit == 0, z - 10, 5 - z) >= 0
    head = jnp.where(bit == 0, roll(packed, 10, 2), packed)
    tail = jnp.where(bit == 0, roll(packed, 2, 2), roll(packed, 128 - 8, 2))
    return jnp.where(keep, head, 0.0), jnp.where(keep, tail, 0.0)


def kernel(
    em_ref, block_ref, slot_ref, w1_ref, b1_ref, w2_ref, b2_ref, wh_ref, bh_ref,
    out_ref,
    em, block, slot, w1, b1, w2, b2, wh, bh,
    sent, arrived, expand, first, second, heads, hidden, partial,
    x_out, y_out, z_out, e_out, x_in, y_in, z_in, e_in,
    load_sems, route_send, route_recv, swap_send, swap_recv,
):
    roll = pltpu.roll
    blocks = 64
    me = lax.axis_index("blocks")
    own = lax.axis_index("octant")
    bits = [own % 2, own // 2 % 2, own // 4]

    def partner(mask):
        total = 0
        for d in range(3):
            total = total + (1 - bits[d] if mask >> d & 1 else bits[d]) * 2**d
        return total

    barrier = pltpu.get_barrier_semaphore()

    def greet(step, carry):
        pl.semaphore_signal(
            barrier, inc=1, device_id={"blocks": (me + step) % blocks}, device_id_type=MESH
        )
        return carry

    lax.fori_loop(1, blocks, greet, 0)
    for mask in range(1, 8):
        pl.semaphore_signal(
            barrier, inc=1, device_id={"octant": partner(mask)}, device_id_type=MESH
        )

    loads = [
        pltpu.make_async_copy(source, target, load_sems.at[index])
        for index, (source, target) in enumerate(
            [
                (em_ref, em), (block_ref, block), (slot_ref, slot),
                (w1_ref, w1), (b1_ref, b1), (w2_ref, w2), (b2_ref, b2), (wh_ref, wh), (bh_ref, bh),
            ]
        )
    ]
    for load in loads:
        load.start()
    for load in loads[:3]:
        load.wait()
    packed = pack_rows(em[0], block[...], slot[...])
    sent[:, 0, :] = packed
    pl.semaphore_wait(barrier, blocks - 1 + 7)

    def send(step, carry):
        target = (me + step) % blocks
        pltpu.make_async_remote_copy(
            src_ref=sent.at[target],
            dst_ref=arrived.at[me],
            send_sem=route_send,
            recv_sem=route_recv,
            device_id={"blocks": target},
            device_id_type=MESH,
        ).start()
        return carry

    lax.fori_loop(1, blocks, send, 0)
    arrived[me] = sent[me]

    for load in loads[3:]:
        load.wait()
    expand[...] = expander()
    first[...] = first_matrix(w1[...])
    wide = replicated(w2[...].reshape(27 * C1, C1), 8)
    x_inner = iota((C1, 8 * C1), 1) // C1
    for x in range(10):
        for dy in range(3):
            for dz in range(3):
                block_rows = jnp.zeros((C1, 8 * C1), F32)
                for dx in range(3):
                    if 0 <= x + dx - 2 < 8:
                        at = (9 * dx + 3 * dy + dz) * C1
                        block_rows = jnp.where(
                            x_inner == x + dx - 2, wide[at : at + C1], block_rows
                        )
                at = (x * 3 + dy) * C1
                second[at : at + C1, dz * 256 : dz * 256 + 256] = block_rows.astype(BF16)
    heads[...] = head_matrix(wh[...])
    b1_col = column(b1[...])
    b2_col = column(b2[...])
    weights = blend_weights(bits)

    whole = pltpu.make_async_remote_copy(
        src_ref=sent.at[pl.ds(0, blocks - 1)],
        dst_ref=arrived.at[pl.ds(0, blocks - 1)],
        send_sem=route_send,
        recv_sem=route_recv,
        device_id={"blocks": (me + 1) % blocks},
        device_id_type=MESH,
    )
    whole.wait_recv()
    volume = unpack_volume(arrived[:, 0, :], expand[...])
    one = dot(first[...], conv1_columns(volume, roll)).reshape(TILE, C1, LANES)
    one = jnp.maximum(one + b1_col[None], 0.0).reshape(TILE * C1, LANES)
    for h in range(2):
        hidden[h] = z_shifted(one[h * 256 : h * 256 + 256], roll)
    low = dot(second[3 * C1 : 30 * C1], hidden[0]).reshape(9, 3, C1, LANES)
    high = dot(second[: 27 * C1], hidden[1]).reshape(9, 3, C1, LANES)
    both = low[7:] + high[:2]
    partial[:7] = low[:7]
    partial[7:9] = both
    partial[9:] = high[2:]
    y = iota((1, 1, LANES), 2) // TILE
    total = partial[:, 1]
    total = total + jnp.where(y > 0, shift_lanes(partial[:, 0].reshape(512, LANES), -TILE, roll).reshape(TILE, C1, LANES), 0.0)
    total = total + jnp.where(y < TILE - 1, shift_lanes(partial[:, 2].reshape(512, LANES), TILE, roll).reshape(TILE, C1, LANES), 0.0)
    two = jnp.maximum(total + b2_col[None], 0.0).reshape(TILE * C1, LANES).astype(BF16)
    logits = dot(heads[...], two)
    pieces = []
    for a in range(AFF):
        pieces.append(jax.nn.sigmoid(logits[a * TILE : a * TILE + TILE] + bh[:, a : a + 1]) * weights)
    blended = jnp.stack(pieces, axis=0)

    tile = [[blended[:, 8 * hx : 8 * hx + 8, 128 * hy : 128 * hy + 128] for hy in range(2)] for hx in range(2)]
    at_x = [move_x(tile[0][hy], tile[1][hy], bits[0], roll) for hy in range(2)]
    at_y = [move_y(tile[hx][0], tile[hx][1], bits[1], roll) for hx in range(2)]
    at_xy = move_y(at_x[0], at_x[1], bits[1], roll)
    z_out[:, :8] = pack_z(tile[0][0], tile[0][1], bits[2], roll)
    z_out[:, 8:] = pack_z(tile[1][0], tile[1][1], bits[2], roll)
    x_out[:, :, :128] = at_x[0]
    x_out[:, :, 128:] = at_x[1]
    y_out[:, :8] = at_y[0]
    y_out[:, 8:] = at_y[1]
    e_out[0] = at_xy
    e_out[1] = pack_z(at_x[0], at_x[1], bits[2], roll)
    e_out[2] = pack_z(at_y[0], at_y[1], bits[2], roll)
    e_out[3] = pack_z(at_xy, at_xy, bits[2], roll)

    pairs = [
        (4, z_out, z_in), (2, y_out, y_in), (6, e_out.at[2], e_in.at[2]), (7, e_out.at[3], e_in.at[3]),
        (5, e_out.at[1], e_in.at[1]), (3, e_out.at[0], e_in.at[0]), (1, x_out, x_in),
    ]
    swaps = [
        pltpu.make_async_remote_copy(
            src_ref=source,
            dst_ref=target,
            send_sem=swap_send.at[mask - 1],
            recv_sem=swap_recv.at[mask - 1],
            device_id={"octant": partner(mask)},
            device_id_type=MESH,
        )
        for mask, source, target in pairs
    ]
    for swap in swaps:
        swap.start()
    for swap in swaps:
        swap.wait_recv()

    plane = [[tile[hx][hy] for hy in range(2)] for hx in range(2)]

    def add(hx, hy, value):
        plane[hx][hy] = plane[hx][hy] + value

    def is_half(bit, half, value):
        return jnp.where(bit == 1 - half, value, 0.0)

    for hy in range(2):
        value = x_in[:, :, 128 * hy : 128 * hy + 128]
        for hx in range(2):
            add(hx, hy, is_half(bits[0], hx, value))
    for hx in range(2):
        value = y_in[:, 8 * hx : 8 * hx + 8]
        for hy in range(2):
            add(hx, hy, is_half(bits[1], hy, value))
        parts = unpack_z(z_in[:, 8 * hx : 8 * hx + 8], bits[2], roll)
        for hy in range(2):
            add(hx, hy, parts[hy])
    corner = e_in[0] + unpack_z(e_in[3], bits[2], roll)[0]
    for hx in range(2):
        for hy in range(2):
            add(hx, hy, is_half(bits[0], hx, is_half(bits[1], hy, corner)))
    parts = unpack_z(e_in[1], bits[2], roll)
    for hx in range(2):
        for hy in range(2):
            add(hx, hy, is_half(bits[0], hx, parts[hy]))
    parts = unpack_z(e_in[2], bits[2], roll)
    for hx in range(2):
        for hy in range(2):
            add(hx, hy, is_half(bits[1], hy, parts[hx]))
    for hx in range(2):
        for hy in range(2):
            out_ref[:, 8 * hx : 8 * hx + 8, 128 * hy : 128 * hy + 128] = plane[hx][hy]
    for swap in swaps:
        swap.wait_send()
    whole.wait_send()


def shards(em_store, route_block, route_slot, conv1_w, conv1_b, conv2_w, conv2_b, head_w, head_b):
    operands = (
        em_store, route_block, route_slot, conv1_w, conv1_b.reshape(1, C1), conv2_w,
        conv2_b.reshape(1, C1), head_w, head_b.reshape(1, AFF),
    )
    vmem = pltpu.VMEM
    result = pl.pallas_call(
        kernel,
        out_shape=jax.ShapeDtypeStruct((AFF, TILE, LANES), F32),
        in_specs=[pl.BlockSpec(memory_space=pl.ANY)] * len(operands),
        out_specs=pl.BlockSpec(memory_space=vmem),
        scratch_shapes=[vmem(value.shape, value.dtype) for value in operands]
        + [
            vmem((64, 1, 256), F32),
            vmem((64, 1, 256), F32),
            vmem((128, 4 * LANES), BF16),
            vmem((TILE * C1, LANES), BF16),
            vmem((30 * C1, 3 * 256), BF16),
            vmem((AFF * TILE, TILE * C1), BF16),
            vmem((2, 768, LANES), BF16),
            vmem((TILE, 3, C1, LANES), F32),
        ]
        + [
            vmem((AFF, 8, 256), F32),
            vmem((AFF, 16, 128), F32),
            vmem((AFF, 16, 128), F32),
            vmem((4, AFF, 8, 128), F32),
        ]
        * 2
        + [
            pltpu.SemaphoreType.DMA((len(operands),)),
            pltpu.SemaphoreType.DMA,
            pltpu.SemaphoreType.DMA,
            pltpu.SemaphoreType.DMA((7,)),
            pltpu.SemaphoreType.DMA((7,)),
        ],
        compiler_params=pltpu.CompilerParams(
            collective_id=0, has_side_effects=True, vmem_limit_bytes=32 * 1024 * 1024
        ),
    )(*operands)
    return result.reshape(1, 1, AFF, TILE * LANES)


def solution(mesh):
    in_specs = (P("octant", "blocks", None), P("octant", "blocks"), P("octant", "blocks")) + (P(),) * 6
    out_specs = P("octant", "blocks", None, None)
    return jax.shard_map(shards, mesh=mesh, in_specs=in_specs, out_specs=out_specs, check_vma=False)
```

```python
import functools

import jax
import jax.numpy as jnp
from jax import lax
from jax.experimental import pallas as pl
from jax.experimental.pallas import tpu as pltpu
from jax.sharding import PartitionSpec as P

TILE = 16
OVL = 6
LANES = TILE * TILE
C1 = 32
SIDE = 8
HUBS = 4
AFF = 3
MESH = pl.DeviceIdType.MESH
F32 = jnp.float32
BF16 = jnp.bfloat16


def iota(shape, dim):
    return lax.broadcasted_iota(jnp.int32, shape, dim)


def dot(a, b):
    return jnp.dot(a, b, preferred_element_type=F32)


def column(row):
    n = row.shape[1]
    return jnp.sum(jnp.where(iota((n, n), 0) == iota((n, n), 1), row, 0.0), axis=1, keepdims=True)


def pack_rows(em, targets, slots):
    n = em.shape[0]
    target_row = targets.astype(F32)
    target_col = column(target_row)
    earlier = (target_col == target_row) & (iota((n, n), 0) < iota((n, n), 1))
    rank_row = jnp.sum(jnp.where(earlier, 1.0, 0.0), axis=0, keepdims=True)
    slot_row = slots
    i_col = column((slot_row // 16 + 1).astype(F32))
    jk_col = column((slot_row % 16).astype(F32))
    lane = iota((n, 128), 1)
    spread = iota((64, 128), 0) == iota((64, 128), 1)
    wide = dot(em, spread.astype(F32).astype(BF16))
    wide = jnp.where(lane == 64, i_col, jnp.where(lane == 65, jk_col, wide)).astype(BF16)
    here = iota((64, n), 0).astype(F32) == target_row
    parts = [
        dot((here & (rank_row == rank)).astype(F32).astype(BF16), wide) for rank in (0.0, 1.0)
    ]
    return jnp.concatenate(parts, axis=1)


def expander():
    row = iota((128, 4 * LANES), 0)
    col = iota((128, 4 * LANES), 1)
    wanted = (col // LANES) * 16 + (col // 16 % 4) * 4 + col % 4
    return (row == wanted).astype(F32).astype(BF16)


def unpack_volume(arrived, expand):
    rows = jnp.concatenate([arrived[:, :128], arrived[:, 128:]], axis=0)
    i_col = rows[:, 64:65]
    jk_col = rows[:, 65:66]
    eye = iota((128, 128), 0) == iota((128, 128), 1)
    i_row = jnp.sum(jnp.where(eye, i_col, 0.0), axis=0, keepdims=True)
    lane = iota((128, LANES), 1)
    lane_jk = (lane // 64 * 4 + lane // 4 % 4).astype(F32)
    inside = lane_jk == jk_col
    spread = dot(rows.astype(BF16), expand)
    x_row = iota((TILE, 128), 0)
    volume = jnp.zeros((TILE, LANES), F32)
    for a in range(4):
        masked = jnp.where(inside, spread[:, a * LANES : (a + 1) * LANES], 0.0).astype(BF16)
        wanted = (x_row % 4 == a) & ((x_row // 4 + 1).astype(F32) == i_row)
        volume = volume + dot(wanted.astype(F32).astype(BF16), masked)
    return volume


def first_matrix(conv1_w):
    tap = iota((27, LANES), 0)
    col = iota((27, LANES), 1)
    x_in = iota((TILE, C1, LANES), 2) % TILE
    x_out = iota((TILE, C1, LANES), 0)
    total = jnp.zeros((TILE, C1, LANES), F32)
    for dx in range(3):
        spread = ((tap == 9 * dx + col // TILE) & (col < 9 * TILE)).astype(F32).astype(BF16)
        rows = dot(conv1_w, spread)
        total = jnp.where(x_in == x_out + dx - 1, rows[None], total)
    return total.reshape(TILE * C1, LANES).astype(BF16)


def replicated(weights, count):
    shape = (C1, count * C1)
    return dot(weights, (iota(shape, 0) == iota(shape, 1) % C1).astype(F32).astype(BF16))


def shift_lanes(value, by, roll):
    return roll(value, (-by) % value.shape[-1], value.ndim - 1)


def conv1_columns(volume, roll):
    lane = iota((TILE, LANES), 1)
    y, z = lane // TILE, lane % TILE
    rows = []
    for dy in (-1, 0, 1):
        for dz in (-1, 0, 1):
            moved = volume
            if dy or dz:
                moved = shift_lanes(volume, dy * TILE + dz, roll)
                keep = (y + dy >= 0) & (y + dy < TILE) & (z + dz >= 0) & (z + dz < TILE)
                moved = jnp.where(keep, moved, 0.0)
            rows.append(moved)
    rows.append(jnp.zeros((LANES - 9 * TILE, LANES), F32))
    return jnp.concatenate(rows, axis=0).astype(BF16)


def z_shifted(half, roll):
    z = iota(half.shape, 1) % TILE
    before = jnp.where(z > 0, shift_lanes(half, -1, roll), 0.0)
    after = jnp.where(z < TILE - 1, shift_lanes(half, 1, roll), 0.0)
    return jnp.concatenate([before, half, after], axis=0).astype(BF16)


def head_matrix(head_w):
    wide = replicated(head_w, TILE)
    x_in = iota((TILE, TILE * C1), 1) // C1
    x_out = iota((TILE, TILE * C1), 0)
    rows = [jnp.where(x_in == x_out, wide[a : a + 1], 0.0) for a in range(AFF)]
    return jnp.concatenate(rows, axis=0).astype(BF16)


def ramp(position, bit):
    lower = jnp.minimum((TILE - position - 0.5) / OVL, 1.0)
    upper = jnp.minimum((position + 0.5) / OVL, 1.0)
    return jnp.where(bit == 1, upper, lower)


def blend_weights(bits):
    lane = iota((TILE, LANES), 1)
    x = iota((TILE, LANES), 0).astype(F32)
    y = (lane // TILE).astype(F32)
    z = (lane % TILE).astype(F32)
    return ramp(x, bits[0]) * (ramp(y, bits[1]) * ramp(z, bits[2]))


def move_x(low, high, bit, roll):
    row = iota(low.shape, 1)
    from_high = jnp.where(row < OVL, roll(high, 6, 1), 0.0)
    from_low = jnp.where(row >= 8 - OVL, roll(low, 2, 1), 0.0)
    return jnp.where(bit == 0, from_high, from_low)


def move_y(low, high, bit, roll):
    lane = iota(low.shape, 2)
    from_high = jnp.where(lane < OVL * TILE, roll(high, 96, 2), 0.0)
    from_low = jnp.where(lane >= 128 - OVL * TILE, roll(low, 32, 2), 0.0)
    return jnp.where(bit == 0, from_high, from_low)


def pack_z(first, second, bit, roll):
    z = iota(first.shape, 2) % TILE
    head = jnp.where(bit == 0, roll(first, 128 - 10, 2), first)
    tail = jnp.where(bit == 0, roll(second, 128 - 2, 2), roll(second, 8, 2))
    return jnp.where(z < 8, head, tail)


def unpack_z(packed, bit, roll):
    z = iota(packed.shape, 2) % TILE
    keep = jnp.where(bit == 0, z - 10, 5 - z) >= 0
    head = jnp.where(bit == 0, roll(packed, 10, 2), packed)
    tail = jnp.where(bit == 0, roll(packed, 2, 2), roll(packed, 128 - 8, 2))
    return jnp.where(keep, head, 0.0), jnp.where(keep, tail, 0.0)


def kernel(
    em_ref, block_ref, slot_ref, w1_ref, b1_ref, w2_ref, b2_ref, wh_ref, bh_ref,
    out_ref,
    em, block, slot, w1, b1, w2, b2, wh, bh,
    sent, arrived, expand, first, second, heads, hidden, partial,
    x_out, y_out, z_out, e_out, x_in, y_in, z_in, e_in,
    load_sems, route_send, route_recv, swap_send, swap_recv, late_ready, all_ready,
):
    roll = pltpu.roll
    blocks = SIDE * SIDE
    me = lax.axis_index("blocks")
    own = lax.axis_index("octant")
    bits = [own % 2, own // 2 % 2, own // 4]

    def partner(mask):
        total = 0
        for d in range(3):
            total = total + (1 - bits[d] if mask >> d & 1 else bits[d]) * 2**d
        return total

    my, mz = me // SIDE, me % SIDE
    early = mz < HUBS
    spans = (4, 3, 5, 2, 6, 1, 7, 0)

    def each_in(columns, visit):
        for span in spans:
            for z in columns:
                target = (my + span) % SIDE * SIDE + z
                if span:
                    visit(target)
                else:
                    pl.when(mz != z)(functools.partial(visit, target))

    def signal(semaphore, target):
        pl.semaphore_signal(
            semaphore, inc=1, device_id={"blocks": target}, device_id_type=MESH
        )

    def send(target):
        pltpu.make_async_remote_copy(
            src_ref=sent.at[target],
            dst_ref=arrived.at[me],
            send_sem=route_send,
            recv_sem=route_recv,
            device_id={"blocks": target},
            device_id_type=MESH,
        ).start()

    loads = [
        pltpu.make_async_copy(source, target, load_sems.at[index])
        for index, (source, target) in enumerate(
            [
                (block_ref, block), (slot_ref, slot), (em_ref, em),
                (w1_ref, w1), (b1_ref, b1), (w2_ref, w2), (b2_ref, b2), (wh_ref, wh), (bh_ref, bh),
            ]
        )
    ]
    for load in loads:
        load.start()
    barrier = pltpu.get_barrier_semaphore()
    for mask in range(1, 8):
        pl.semaphore_signal(
            barrier, inc=1, device_id={"octant": partner(mask)}, device_id_type=MESH
        )
    hub_columns, late_columns = range(HUBS), range(HUBS, SIDE)
    hub_count, late_count = HUBS * SIDE, (SIDE - HUBS) * SIDE

    @pl.when(early)
    def _():
        each_in(late_columns, functools.partial(signal, barrier))
        each_in(hub_columns, functools.partial(signal, barrier))

    @pl.when(jnp.logical_not(early))
    def _():
        pl.semaphore_wait(barrier, 7 + hub_count)
        each_in(hub_columns, functools.partial(signal, late_ready))

    for load in loads[:3]:
        load.wait()
    packed = pack_rows(em[0], block[...], slot[...])
    sent[:, 0, :] = packed

    @pl.when(early)
    def _():
        pl.semaphore_wait(barrier, 7 + hub_count - 1)

    each_in(hub_columns, send)
    arrived[me] = sent[me]

    for load in loads[3:]:
        load.wait()
    expand[...] = expander()
    first[...] = first_matrix(w1[...])
    wide = replicated(w2[...].reshape(27 * C1, C1), 8)
    x_inner = iota((C1, 8 * C1), 1) // C1
    for x in range(10):
        for dy in range(3):
            for dz in range(3):
                block_rows = jnp.zeros((C1, 8 * C1), F32)
                for dx in range(3):
                    if 0 <= x + dx - 2 < 8:
                        at = (9 * dx + 3 * dy + dz) * C1
                        block_rows = jnp.where(
                            x_inner == x + dx - 2, wide[at : at + C1], block_rows
                        )
                at = (x * 3 + dy) * C1
                second[at : at + C1, dz * 256 : dz * 256 + 256] = block_rows.astype(BF16)
    heads[...] = head_matrix(wh[...])
    b1_col = column(b1[...])
    b2_col = column(b2[...])
    weights = blend_weights(bits)

    @pl.when(early)
    def _():
        pl.semaphore_wait(late_ready, late_count)

        @pl.when((mz == 0) | (mz == HUBS - 1))
        def _():
            first_told = my * SIDE + jnp.where(mz == 0, SIDE - 2, HUBS)
            signal(all_ready, first_told)
            signal(all_ready, first_told + 1)

    @pl.when(jnp.logical_not(early))
    def _():
        pl.semaphore_wait(all_ready, 1)

    each_in(late_columns, send)
    whole = pltpu.make_async_remote_copy(
        src_ref=sent.at[pl.ds(0, blocks - 1)],
        dst_ref=arrived.at[pl.ds(0, blocks - 1)],
        send_sem=route_send,
        recv_sem=route_recv,
        device_id={"blocks": (me + 1) % blocks},
        device_id_type=MESH,
    )
    whole.wait_recv()
    volume = unpack_volume(arrived[:, 0, :], expand[...])
    one = dot(first[...], conv1_columns(volume, roll)).reshape(TILE, C1, LANES)
    one = jnp.maximum(one + b1_col[None], 0.0).reshape(TILE * C1, LANES)
    for h in range(2):
        hidden[h] = z_shifted(one[h * 256 : h * 256 + 256], roll)
    low = dot(second[3 * C1 : 30 * C1], hidden[0]).reshape(9, 3, C1, LANES)
    high = dot(second[: 27 * C1], hidden[1]).reshape(9, 3, C1, LANES)
    both = low[7:] + high[:2]
    partial[:7] = low[:7]
    partial[7:9] = both
    partial[9:] = high[2:]
    y = iota((1, 1, LANES), 2) // TILE
    total = partial[:, 1]
    total = total + jnp.where(y > 0, shift_lanes(partial[:, 0].reshape(512, LANES), -TILE, roll).reshape(TILE, C1, LANES), 0.0)
    total = total + jnp.where(y < TILE - 1, shift_lanes(partial[:, 2].reshape(512, LANES), TILE, roll).reshape(TILE, C1, LANES), 0.0)
    two = jnp.maximum(total + b2_col[None], 0.0).reshape(TILE * C1, LANES).astype(BF16)
    logits = dot(heads[...], two)
    pieces = []
    for a in range(AFF):
        pieces.append(jax.nn.sigmoid(logits[a * TILE : a * TILE + TILE] + bh[:, a : a + 1]) * weights)
    blended = jnp.stack(pieces, axis=0)

    tile = [[blended[:, 8 * hx : 8 * hx + 8, 128 * hy : 128 * hy + 128] for hy in range(2)] for hx in range(2)]
    swaps = {}

    def swap(mask, source, target):
        swaps[mask] = pltpu.make_async_remote_copy(
            src_ref=source,
            dst_ref=target,
            send_sem=swap_send.at[mask - 1],
            recv_sem=swap_recv.at[mask - 1],
            device_id={"octant": partner(mask)},
            device_id_type=MESH,
        )
        swaps[mask].start()

    z_out[:, :8] = pack_z(tile[0][0], tile[0][1], bits[2], roll)
    z_out[:, 8:] = pack_z(tile[1][0], tile[1][1], bits[2], roll)
    swap(4, z_out, z_in)
    at_x = [move_x(tile[0][hy], tile[1][hy], bits[0], roll) for hy in range(2)]
    e_out[1] = pack_z(at_x[0], at_x[1], bits[2], roll)
    swap(5, e_out.at[1], e_in.at[1])
    at_y = [move_y(tile[hx][0], tile[hx][1], bits[1], roll) for hx in range(2)]
    y_out[:, :8] = at_y[0]
    y_out[:, 8:] = at_y[1]
    swap(2, y_out, y_in)
    e_out[2] = pack_z(at_y[0], at_y[1], bits[2], roll)
    swap(6, e_out.at[2], e_in.at[2])
    at_xy = move_y(at_x[0], at_x[1], bits[1], roll)
    e_out[0] = at_xy
    swap(3, e_out.at[0], e_in.at[0])
    e_out[3] = pack_z(at_xy, at_xy, bits[2], roll)
    swap(7, e_out.at[3], e_in.at[3])
    x_out[:, :, :128] = at_x[0]
    x_out[:, :, 128:] = at_x[1]
    swap(1, x_out, x_in)

    plane = [[tile[hx][hy] for hy in range(2)] for hx in range(2)]

    def add(hx, hy, value):
        plane[hx][hy] = plane[hx][hy] + value

    def is_half(bit, half, value):
        return jnp.where(bit == 1 - half, value, 0.0)

    swaps[1].wait_recv()
    for hy in range(2):
        value = x_in[:, :, 128 * hy : 128 * hy + 128]
        for hx in range(2):
            add(hx, hy, is_half(bits[0], hx, value))
    swaps[2].wait_recv()
    for hx in range(2):
        value = y_in[:, 8 * hx : 8 * hx + 8]
        for hy in range(2):
            add(hx, hy, is_half(bits[1], hy, value))
    swaps[3].wait_recv()
    swaps[7].wait_recv()
    corner = e_in[0] + unpack_z(e_in[3], bits[2], roll)[0]
    for hx in range(2):
        for hy in range(2):
            add(hx, hy, is_half(bits[0], hx, is_half(bits[1], hy, corner)))
    swaps[6].wait_recv()
    parts = unpack_z(e_in[2], bits[2], roll)
    for hx in range(2):
        for hy in range(2):
            add(hx, hy, is_half(bits[1], hy, parts[hx]))
    swaps[5].wait_recv()
    parts = unpack_z(e_in[1], bits[2], roll)
    for hx in range(2):
        for hy in range(2):
            add(hx, hy, is_half(bits[0], hx, parts[hy]))
    swaps[4].wait_recv()
    for hx in range(2):
        parts = unpack_z(z_in[:, 8 * hx : 8 * hx + 8], bits[2], roll)
        for hy in range(2):
            add(hx, hy, parts[hy])
    for hx in range(2):
        for hy in range(2):
            out_ref[:, 8 * hx : 8 * hx + 8, 128 * hy : 128 * hy + 128] = plane[hx][hy]
    for copy in swaps.values():
        copy.wait_send()
    whole.wait_send()


def shards(em_store, route_block, route_slot, conv1_w, conv1_b, conv2_w, conv2_b, head_w, head_b):
    operands = (
        em_store, route_block, route_slot, conv1_w, conv1_b.reshape(1, C1), conv2_w,
        conv2_b.reshape(1, C1), head_w, head_b.reshape(1, AFF),
    )
    vmem = pltpu.VMEM
    result = pl.pallas_call(
        kernel,
        out_shape=jax.ShapeDtypeStruct((AFF, TILE, LANES), F32),
        in_specs=[pl.BlockSpec(memory_space=pl.ANY)] * len(operands),
        out_specs=pl.BlockSpec(memory_space=vmem),
        scratch_shapes=[vmem(value.shape, value.dtype) for value in operands]
        + [
            vmem((64, 1, 256), F32),
            vmem((64, 1, 256), F32),
            vmem((128, 4 * LANES), BF16),
            vmem((TILE * C1, LANES), BF16),
            vmem((30 * C1, 3 * 256), BF16),
            vmem((AFF * TILE, TILE * C1), BF16),
            vmem((2, 768, LANES), BF16),
            vmem((TILE, 3, C1, LANES), F32),
        ]
        + [
            vmem((AFF, 8, 256), F32),
            vmem((AFF, 16, 128), F32),
            vmem((AFF, 16, 128), F32),
            vmem((4, AFF, 8, 128), F32),
        ]
        * 2
        + [
            pltpu.SemaphoreType.DMA((len(operands),)),
            pltpu.SemaphoreType.DMA,
            pltpu.SemaphoreType.DMA,
            pltpu.SemaphoreType.DMA((7,)),
            pltpu.SemaphoreType.DMA((7,)),
            pltpu.SemaphoreType.REGULAR,
            pltpu.SemaphoreType.REGULAR,
        ],
        compiler_params=pltpu.CompilerParams(
            collective_id=0, has_side_effects=True, vmem_limit_bytes=60 * 1024 * 1024
        ),
    )(*operands)
    return result.reshape(1, 1, AFF, TILE * LANES)


def solution(mesh):
    in_specs = (P("octant", "blocks", None), P("octant", "blocks"), P("octant", "blocks")) + (P(),) * 6
    out_specs = P("octant", "blocks", None, None)
    return jax.shard_map(shards, mesh=mesh, in_specs=in_specs, out_specs=out_specs, check_vma=False)
```

```python
import functools

import jax
import jax.numpy as jnp
from jax import lax
from jax.experimental import pallas as pl
from jax.experimental.pallas import tpu as pltpu
from jax.sharding import PartitionSpec as P

TILE = 16
OVL = 6
LANES = TILE * TILE
C1 = 32
SIDE = 8
HUBS = 4
AFF = 3
MESH = pl.DeviceIdType.MESH
F32 = jnp.float32
BF16 = jnp.bfloat16


def iota(shape, dim):
    return lax.broadcasted_iota(jnp.int32, shape, dim)


def dot(a, b):
    return jnp.dot(a, b, preferred_element_type=F32)


def column(row):
    n = row.shape[1]
    return jnp.sum(jnp.where(iota((n, n), 0) == iota((n, n), 1), row, 0.0), axis=1, keepdims=True)


def pack_rows(em, targets, slots):
    n = em.shape[0]
    target_row = targets.astype(F32)
    target_col = column(target_row)
    earlier = (target_col == target_row) & (iota((n, n), 0) < iota((n, n), 1))
    rank_row = jnp.sum(jnp.where(earlier, 1.0, 0.0), axis=0, keepdims=True)
    slot_row = slots
    i_col = column((slot_row // 16 + 1).astype(F32))
    jk_col = column((slot_row % 16).astype(F32))
    lane = iota((n, 128), 1)
    spread = iota((64, 128), 0) == iota((64, 128), 1)
    wide = dot(em, spread.astype(F32).astype(BF16))
    wide = jnp.where(lane == 64, i_col, jnp.where(lane == 65, jk_col, wide)).astype(BF16)
    here = iota((64, n), 0).astype(F32) == target_row
    parts = [
        dot((here & (rank_row == rank)).astype(F32).astype(BF16), wide) for rank in (0.0, 1.0)
    ]
    return jnp.concatenate(parts, axis=1)


def expander():
    row = iota((128, 4 * LANES), 0)
    col = iota((128, 4 * LANES), 1)
    wanted = (col // LANES) * 16 + (col // 16 % 4) * 4 + col % 4
    return (row == wanted).astype(F32).astype(BF16)


def unpack_volume(arrived, expand):
    rows = jnp.concatenate([arrived[:, :128], arrived[:, 128:]], axis=0)
    i_col = rows[:, 64:65]
    jk_col = rows[:, 65:66]
    eye = iota((128, 128), 0) == iota((128, 128), 1)
    i_row = jnp.sum(jnp.where(eye, i_col, 0.0), axis=0, keepdims=True)
    lane = iota((128, LANES), 1)
    lane_jk = (lane // 64 * 4 + lane // 4 % 4).astype(F32)
    inside = lane_jk == jk_col
    spread = dot(rows.astype(BF16), expand)
    x_row = iota((TILE, 128), 0)
    volume = jnp.zeros((TILE, LANES), F32)
    for a in range(4):
        masked = jnp.where(inside, spread[:, a * LANES : (a + 1) * LANES], 0.0).astype(BF16)
        wanted = (x_row % 4 == a) & ((x_row // 4 + 1).astype(F32) == i_row)
        volume = volume + dot(wanted.astype(F32).astype(BF16), masked)
    return volume


def first_matrix(conv1_w):
    tap = iota((27, LANES), 0)
    col = iota((27, LANES), 1)
    x_in = iota((TILE, C1, LANES), 2) % TILE
    x_out = iota((TILE, C1, LANES), 0)
    total = jnp.zeros((TILE, C1, LANES), F32)
    for dx in range(3):
        spread = ((tap == 9 * dx + col // TILE) & (col < 9 * TILE)).astype(F32).astype(BF16)
        rows = dot(conv1_w, spread)
        total = jnp.where(x_in == x_out + dx - 1, rows[None], total)
    return total.reshape(TILE * C1, LANES).astype(BF16)


def replicated(weights, count):
    shape = (C1, count * C1)
    return dot(weights, (iota(shape, 0) == iota(shape, 1) % C1).astype(F32).astype(BF16))


def shift_lanes(value, by, roll):
    return roll(value, (-by) % value.shape[-1], value.ndim - 1)


def conv1_columns(volume, roll):
    lane = iota((TILE, LANES), 1)
    y, z = lane // TILE, lane % TILE
    rows = []
    for dy in (-1, 0, 1):
        for dz in (-1, 0, 1):
            moved = volume
            if dy or dz:
                moved = shift_lanes(volume, dy * TILE + dz, roll)
                keep = (y + dy >= 0) & (y + dy < TILE) & (z + dz >= 0) & (z + dz < TILE)
                moved = jnp.where(keep, moved, 0.0)
            rows.append(moved)
    rows.append(jnp.zeros((LANES - 9 * TILE, LANES), F32))
    return jnp.concatenate(rows, axis=0).astype(BF16)


def z_shifted(half, roll):
    z = iota(half.shape, 1) % TILE
    before = jnp.where(z > 0, shift_lanes(half, -1, roll), 0.0)
    after = jnp.where(z < TILE - 1, shift_lanes(half, 1, roll), 0.0)
    return jnp.concatenate([before, half, after], axis=0).astype(BF16)


def head_matrix(head_w):
    wide = replicated(head_w, TILE)
    x_in = iota((TILE, TILE * C1), 1) // C1
    x_out = iota((TILE, TILE * C1), 0)
    rows = [jnp.where(x_in == x_out, wide[a : a + 1], 0.0) for a in range(AFF)]
    return jnp.concatenate(rows, axis=0).astype(BF16)


def ramp(position, bit):
    lower = jnp.minimum((TILE - position - 0.5) / OVL, 1.0)
    upper = jnp.minimum((position + 0.5) / OVL, 1.0)
    return jnp.where(bit == 1, upper, lower)


def blend_weights(bits):
    lane = iota((TILE, LANES), 1)
    x = iota((TILE, LANES), 0).astype(F32)
    y = (lane // TILE).astype(F32)
    z = (lane % TILE).astype(F32)
    return ramp(x, bits[0]) * (ramp(y, bits[1]) * ramp(z, bits[2]))


def move_x(low, high, bit, roll):
    row = iota(low.shape, 1)
    from_high = jnp.where(row < OVL, roll(high, 6, 1), 0.0)
    from_low = jnp.where(row >= 8 - OVL, roll(low, 2, 1), 0.0)
    return jnp.where(bit == 0, from_high, from_low)


def move_y(low, high, bit, roll):
    lane = iota(low.shape, 2)
    from_high = jnp.where(lane < OVL * TILE, roll(high, 96, 2), 0.0)
    from_low = jnp.where(lane >= 128 - OVL * TILE, roll(low, 32, 2), 0.0)
    return jnp.where(bit == 0, from_high, from_low)


def pack_z(first, second, bit, roll):
    z = iota(first.shape, 2) % TILE
    head = jnp.where(bit == 0, roll(first, 128 - 10, 2), first)
    tail = jnp.where(bit == 0, roll(second, 128 - 2, 2), roll(second, 8, 2))
    return jnp.where(z < 8, head, tail)


def unpack_z(packed, bit, roll):
    z = iota(packed.shape, 2) % TILE
    keep = jnp.where(bit == 0, z - 10, 5 - z) >= 0
    head = jnp.where(bit == 0, roll(packed, 10, 2), packed)
    tail = jnp.where(bit == 0, roll(packed, 2, 2), roll(packed, 128 - 8, 2))
    return jnp.where(keep, head, 0.0), jnp.where(keep, tail, 0.0)


def kernel(
    em_ref, block_ref, slot_ref, w1_ref, b1_ref, w2_ref, b2_ref, wh_ref, bh_ref,
    out_ref,
    em, block, slot, w1, b1, w2, b2, wh, bh,
    sent, arrived, expand, first, second, heads, hidden, partial,
    x_out, y_out, z_out, e_out, x_in, y_in, z_in, e_in,
    load_sems, route_send, route_recv, swap_send, swap_recv,
    relayed, relay_send, relay_recv, mate_ready,
):
    roll = pltpu.roll
    blocks = SIDE * SIDE
    me = lax.axis_index("blocks")
    own = lax.axis_index("octant")
    bits = [own % 2, own // 2 % 2, own // 4]

    def partner(mask):
        total = 0
        for d in range(3):
            total = total + (1 - bits[d] if mask >> d & 1 else bits[d]) * 2**d
        return total

    my, mz = me // SIDE, me % SIDE
    early = mz < HUBS
    half = HUBS * SIDE
    slot_me = jnp.where(early, my * HUBS + mz, half + my * HUBS + mz - HUBS)
    group_me = jnp.where(early, SIDE, my)
    mate = my * SIDE + SIDE - 1 - mz
    spans = (4, 3, 5, 2, 6, 1, 7, 0)

    def signal(semaphore, target):
        pl.semaphore_signal(
            semaphore, inc=1, device_id={"blocks": target}, device_id_type=MESH
        )

    def unless(condition, visit):
        if condition is None:
            visit()
        else:
            pl.when(jnp.logical_not(condition))(visit)

    def greet(span, z):
        target = (my + span) % SIDE * SIDE + z
        unless(mz == z if span == 0 and z < HUBS else None, lambda: signal(barrier, target))

    def rows(source, target, semaphores, device):
        return pltpu.make_async_remote_copy(
            src_ref=source,
            dst_ref=target,
            send_sem=semaphores[0],
            recv_sem=semaphores[1],
            device_id={"blocks": device},
            device_id_type=MESH,
        )

    def send(span, z):
        row = (my + span) % SIDE * SIDE
        target = row + z
        if z < HUBS:
            device, place, semaphore = target, arrived, route_recv
        else:
            device, place, semaphore = row + SIDE - 1 - z, relayed, relay_recv.at[group_me]
        copy = rows(sent.at[target], place.at[slot_me], (route_send, semaphore), device)
        here = mz == (z if z < HUBS else SIDE - 1 - z)
        unless(here if span == 0 else None, copy.start)

    def landed(count, place, semaphores):
        return rows(place.at[pl.ds(0, count)], place.at[pl.ds(0, count)], semaphores, mate)

    loads = [
        pltpu.make_async_copy(source, target, load_sems.at[index])
        for index, (source, target) in enumerate(
            [
                (block_ref, block), (slot_ref, slot), (em_ref, em),
                (w1_ref, w1), (b1_ref, b1), (w2_ref, w2), (b2_ref, b2), (wh_ref, wh), (bh_ref, bh),
            ]
        )
    ]
    for load in loads:
        load.start()
    barrier = pltpu.get_barrier_semaphore()
    for mask in range(1, 8):
        pl.semaphore_signal(
            barrier, inc=1, device_id={"octant": partner(mask)}, device_id_type=MESH
        )

    @pl.when(early)
    def _():
        for span in spans:
            for z in range(SIDE):
                greet(span, z)

    @pl.when(jnp.logical_not(early))
    def _():
        pl.semaphore_wait(barrier, 7 + half)
        signal(mate_ready, mate)

    for load in loads[:3]:
        load.wait()
    packed = pack_rows(em[0], block[...], slot[...])
    sent[:, 0, :] = packed

    @pl.when(early)
    def _():
        pl.semaphore_wait(barrier, 7 + half - 1)
        arrived[slot_me] = sent[me]
        relayed[slot_me] = sent[mate]

    for span in spans:
        for z in range(SIDE):
            send(span, z)

    for load in loads[3:]:
        load.wait()
    expand[...] = expander()
    first[...] = first_matrix(w1[...])
    wide = replicated(w2[...].reshape(27 * C1, C1), 8)
    x_inner = iota((C1, 8 * C1), 1) // C1
    for x in range(10):
        for dy in range(3):
            for dz in range(3):
                block_rows = jnp.zeros((C1, 8 * C1), F32)
                for dx in range(3):
                    if 0 <= x + dx - 2 < 8:
                        at = (9 * dx + 3 * dy + dz) * C1
                        block_rows = jnp.where(
                            x_inner == x + dx - 2, wide[at : at + C1], block_rows
                        )
                at = (x * 3 + dy) * C1
                second[at : at + C1, dz * 256 : dz * 256 + 256] = block_rows.astype(BF16)
    heads[...] = head_matrix(wh[...])
    b1_col = column(b1[...])
    b2_col = column(b2[...])
    weights = blend_weights(bits)

    @pl.when(early)
    def _():
        def forward(start, count, awaited, group):
            landed(awaited, relayed, (relay_send, relay_recv.at[group])).wait_recv()
            part = pl.ds(start, count)
            rows(relayed.at[part], arrived.at[part], (relay_send, route_recv), mate).start()

        pl.semaphore_wait(mate_ready, 1)
        forward(0, half, half - 1, SIDE)
        for y in (0, 1, 7, 2, 6, 3, 5, 4):
            forward(half + y * HUBS, HUBS, HUBS, y)
        landed(blocks - 1, arrived, (route_send, route_recv)).wait_recv()

    @pl.when(jnp.logical_not(early))
    def _():
        landed(blocks, arrived, (route_send, route_recv)).wait_recv()

    volume = unpack_volume(arrived[:, 0, :], expand[...])
    one = dot(first[...], conv1_columns(volume, roll)).reshape(TILE, C1, LANES)
    one = jnp.maximum(one + b1_col[None], 0.0).reshape(TILE * C1, LANES)
    for h in range(2):
        hidden[h] = z_shifted(one[h * 256 : h * 256 + 256], roll)
    low = dot(second[3 * C1 : 30 * C1], hidden[0]).reshape(9, 3, C1, LANES)
    high = dot(second[: 27 * C1], hidden[1]).reshape(9, 3, C1, LANES)
    both = low[7:] + high[:2]
    partial[:7] = low[:7]
    partial[7:9] = both
    partial[9:] = high[2:]
    y = iota((1, 1, LANES), 2) // TILE
    total = partial[:, 1]
    total = total + jnp.where(y > 0, shift_lanes(partial[:, 0].reshape(512, LANES), -TILE, roll).reshape(TILE, C1, LANES), 0.0)
    total = total + jnp.where(y < TILE - 1, shift_lanes(partial[:, 2].reshape(512, LANES), TILE, roll).reshape(TILE, C1, LANES), 0.0)
    two = jnp.maximum(total + b2_col[None], 0.0).reshape(TILE * C1, LANES).astype(BF16)
    logits = dot(heads[...], two)
    pieces = []
    for a in range(AFF):
        pieces.append(jax.nn.sigmoid(logits[a * TILE : a * TILE + TILE] + bh[:, a : a + 1]) * weights)
    blended = jnp.stack(pieces, axis=0)

    tile = [[blended[:, 8 * hx : 8 * hx + 8, 128 * hy : 128 * hy + 128] for hy in range(2)] for hx in range(2)]
    swaps = {}

    def swap(mask, source, target):
        swaps[mask] = pltpu.make_async_remote_copy(
            src_ref=source,
            dst_ref=target,
            send_sem=swap_send.at[mask - 1],
            recv_sem=swap_recv.at[mask - 1],
            device_id={"octant": partner(mask)},
            device_id_type=MESH,
        )
        swaps[mask].start()

    z_out[:, :8] = pack_z(tile[0][0], tile[0][1], bits[2], roll)
    z_out[:, 8:] = pack_z(tile[1][0], tile[1][1], bits[2], roll)
    swap(4, z_out, z_in)
    at_x = [move_x(tile[0][hy], tile[1][hy], bits[0], roll) for hy in range(2)]
    e_out[1] = pack_z(at_x[0], at_x[1], bits[2], roll)
    swap(5, e_out.at[1], e_in.at[1])
    at_y = [move_y(tile[hx][0], tile[hx][1], bits[1], roll) for hx in range(2)]
    y_out[:, :8] = at_y[0]
    y_out[:, 8:] = at_y[1]
    swap(2, y_out, y_in)
    e_out[2] = pack_z(at_y[0], at_y[1], bits[2], roll)
    swap(6, e_out.at[2], e_in.at[2])
    at_xy = move_y(at_x[0], at_x[1], bits[1], roll)
    e_out[0] = at_xy
    swap(3, e_out.at[0], e_in.at[0])
    e_out[3] = pack_z(at_xy, at_xy, bits[2], roll)
    swap(7, e_out.at[3], e_in.at[3])
    x_out[:, :, :128] = at_x[0]
    x_out[:, :, 128:] = at_x[1]
    swap(1, x_out, x_in)

    plane = [[tile[hx][hy] for hy in range(2)] for hx in range(2)]

    def add(hx, hy, value):
        plane[hx][hy] = plane[hx][hy] + value

    def is_half(bit, half, value):
        return jnp.where(bit == 1 - half, value, 0.0)

    swaps[1].wait_recv()
    for hy in range(2):
        value = x_in[:, :, 128 * hy : 128 * hy + 128]
        for hx in range(2):
            add(hx, hy, is_half(bits[0], hx, value))
    swaps[2].wait_recv()
    for hx in range(2):
        value = y_in[:, 8 * hx : 8 * hx + 8]
        for hy in range(2):
            add(hx, hy, is_half(bits[1], hy, value))
    swaps[3].wait_recv()
    swaps[7].wait_recv()
    corner = e_in[0] + unpack_z(e_in[3], bits[2], roll)[0]
    for hx in range(2):
        for hy in range(2):
            add(hx, hy, is_half(bits[0], hx, is_half(bits[1], hy, corner)))
    swaps[6].wait_recv()
    parts = unpack_z(e_in[2], bits[2], roll)
    for hx in range(2):
        for hy in range(2):
            add(hx, hy, is_half(bits[1], hy, parts[hx]))
    swaps[5].wait_recv()
    parts = unpack_z(e_in[1], bits[2], roll)
    for hx in range(2):
        for hy in range(2):
            add(hx, hy, is_half(bits[0], hx, parts[hy]))
    swaps[4].wait_recv()
    for hx in range(2):
        parts = unpack_z(z_in[:, 8 * hx : 8 * hx + 8], bits[2], roll)
        for hy in range(2):
            add(hx, hy, parts[hy])
    for hx in range(2):
        for hy in range(2):
            out_ref[:, pl.ds(TILE * hx + hy, 8, stride=2), :] = plane[hx][hy]
    for copy in swaps.values():
        copy.wait_send()

    @pl.when(early)
    def _():
        landed(blocks - 2, arrived, (route_send, route_recv)).wait_send()
        landed(blocks, arrived, (relay_send, route_recv)).wait_send()

    @pl.when(jnp.logical_not(early))
    def _():
        landed(blocks, arrived, (route_send, route_recv)).wait_send()


def shards(em_store, route_block, route_slot, conv1_w, conv1_b, conv2_w, conv2_b, head_w, head_b):
    operands = (
        em_store, route_block, route_slot, conv1_w, conv1_b.reshape(1, C1), conv2_w,
        conv2_b.reshape(1, C1), head_w, head_b.reshape(1, AFF),
    )
    operands = tuple(pltpu.with_memory_space_constraint(value, pltpu.HBM) for value in operands)
    vmem = pltpu.VMEM
    result = pl.pallas_call(
        kernel,
        out_shape=jax.ShapeDtypeStruct((AFF, 2 * TILE, 128), F32),
        in_specs=[pl.BlockSpec(memory_space=pltpu.HBM)] * len(operands),
        out_specs=pl.BlockSpec(memory_space=vmem),
        scratch_shapes=[vmem(value.shape, value.dtype) for value in operands]
        + [
            vmem((64, 1, 256), F32),
            vmem((64, 1, 256), F32),
            vmem((128, 4 * LANES), BF16),
            vmem((TILE * C1, LANES), BF16),
            vmem((30 * C1, 3 * 256), BF16),
            vmem((AFF * TILE, TILE * C1), BF16),
            vmem((2, 768, LANES), BF16),
            vmem((TILE, 3, C1, LANES), F32),
        ]
        + [
            vmem((AFF, 8, 256), F32),
            vmem((AFF, 16, 128), F32),
            vmem((AFF, 16, 128), F32),
            vmem((4, AFF, 8, 128), F32),
        ]
        * 2
        + [
            pltpu.SemaphoreType.DMA((len(operands),)),
            pltpu.SemaphoreType.DMA,
            pltpu.SemaphoreType.DMA,
            pltpu.SemaphoreType.DMA((7,)),
            pltpu.SemaphoreType.DMA((7,)),
        ]
        + [
            vmem((64, 1, 256), F32),
            pltpu.SemaphoreType.DMA,
            pltpu.SemaphoreType.DMA((SIDE + 1,)),
            pltpu.SemaphoreType.REGULAR,
        ],
        compiler_params=pltpu.CompilerParams(
            collective_id=0, has_side_effects=True, vmem_limit_bytes=32 * 1024 * 1024
        ),
    )(*operands)
    return result.reshape(1, 1, AFF, TILE * LANES)


def solution(mesh):
    in_specs = (P("octant", "blocks", None), P("octant", "blocks"), P("octant", "blocks")) + (P(),) * 6
    out_specs = P("octant", "blocks", None, None)
    return jax.shard_map(shards, mesh=mesh, in_specs=in_specs, out_specs=out_specs, check_vma=False)
```

```python
import functools

import jax
import jax.numpy as jnp
from jax import lax
from jax.experimental import pallas as pl
from jax.experimental.pallas import tpu as pltpu
from jax.sharding import PartitionSpec as P

TILE = 16
OVL = 6
LANES = TILE * TILE
C1 = 32
SIDE = 8
HUBS = 4
AFF = 3
MESH = pl.DeviceIdType.MESH
F32 = jnp.float32
BF16 = jnp.bfloat16


def iota(shape, dim):
    return lax.broadcasted_iota(jnp.int32, shape, dim)


def dot(a, b):
    return jnp.dot(a, b, preferred_element_type=F32)


def column(row):
    n = row.shape[1]
    return jnp.sum(jnp.where(iota((n, n), 0) == iota((n, n), 1), row, 0.0), axis=1, keepdims=True)


def pack_rows(em, targets, slots):
    n = em.shape[0]
    target_row = targets.astype(F32)
    target_col = column(target_row)
    earlier = (target_col == target_row) & (iota((n, n), 0) < iota((n, n), 1))
    rank_row = jnp.sum(jnp.where(earlier, 1.0, 0.0), axis=0, keepdims=True)
    slot_row = slots
    i_col = column((slot_row // 16 + 1).astype(F32))
    jk_col = column((slot_row % 16).astype(F32))
    lane = iota((n, 64), 1)
    labels = jnp.where(lane == 0, i_col, jnp.where(lane == 1, jk_col, 0.0)).astype(BF16)
    wide = jnp.concatenate([em, labels], axis=1)
    here = iota((64, n), 0).astype(F32) == target_row
    parts = [
        dot((here & (rank_row == rank)).astype(F32).astype(BF16), wide) for rank in (0.0, 1.0)
    ]
    return jnp.concatenate(parts, axis=1)


def expander():
    row = iota((128, 4 * LANES), 0)
    col = iota((128, 4 * LANES), 1)
    wanted = (col // LANES) * 16 + (col // 16 % 4) * 4 + col % 4
    return (row == wanted).astype(F32).astype(BF16)


def unpack_volume(arrived, expand):
    rows = jnp.concatenate([arrived[:, :128], arrived[:, 128:]], axis=0)
    i_col = rows[:, 64:65]
    jk_col = rows[:, 65:66]
    eye = iota((128, 128), 0) == iota((128, 128), 1)
    i_row = jnp.sum(jnp.where(eye, i_col, 0.0), axis=0, keepdims=True)
    lane = iota((128, LANES), 1)
    lane_jk = (lane // 64 * 4 + lane // 4 % 4).astype(F32)
    inside = lane_jk == jk_col
    spread = dot(rows.astype(BF16), expand)
    x_row = iota((TILE, 128), 0)
    volume = jnp.zeros((TILE, LANES), F32)
    for a in range(4):
        masked = jnp.where(inside, spread[:, a * LANES : (a + 1) * LANES], 0.0).astype(BF16)
        wanted = (x_row % 4 == a) & ((x_row // 4 + 1).astype(F32) == i_row)
        volume = volume + dot(wanted.astype(F32).astype(BF16), masked)
    return volume


def first_matrix(conv1_w):
    tap = iota((27, LANES), 0)
    col = iota((27, LANES), 1)
    x_in = iota((TILE, C1, LANES), 2) % TILE
    x_out = iota((TILE, C1, LANES), 0)
    total = jnp.zeros((TILE, C1, LANES), F32)
    for dx in range(3):
        spread = ((tap == 9 * dx + col // TILE) & (col < 9 * TILE)).astype(F32).astype(BF16)
        rows = dot(conv1_w, spread)
        total = jnp.where(x_in == x_out + dx - 1, rows[None], total)
    return total.reshape(TILE * C1, LANES).astype(BF16)


def replicated(weights, count):
    shape = (C1, count * C1)
    return dot(weights, (iota(shape, 0) == iota(shape, 1) % C1).astype(F32).astype(BF16))


def shift_lanes(value, by, roll):
    return roll(value, (-by) % value.shape[-1], value.ndim - 1)


def conv1_columns(volume, roll):
    lane = iota((TILE, LANES), 1)
    y, z = lane // TILE, lane % TILE
    rows = []
    for dy in (-1, 0, 1):
        for dz in (-1, 0, 1):
            moved = volume
            if dy or dz:
                moved = shift_lanes(volume, dy * TILE + dz, roll)
                keep = (y + dy >= 0) & (y + dy < TILE) & (z + dz >= 0) & (z + dz < TILE)
                moved = jnp.where(keep, moved, 0.0)
            rows.append(moved)
    rows.append(jnp.zeros((LANES - 9 * TILE, LANES), F32))
    return jnp.concatenate(rows, axis=0).astype(BF16)


def z_shifted(half, roll):
    z = iota(half.shape, 1) % TILE
    before = jnp.where(z > 0, shift_lanes(half, -1, roll), 0.0)
    after = jnp.where(z < TILE - 1, shift_lanes(half, 1, roll), 0.0)
    return jnp.concatenate([before, half, after], axis=0).astype(BF16)


def head_matrix(head_w):
    wide = replicated(head_w, TILE)
    x_in = iota((TILE, TILE * C1), 1) // C1
    x_out = iota((TILE, TILE * C1), 0)
    rows = [jnp.where(x_in == x_out, wide[a : a + 1], 0.0) for a in range(AFF)]
    return jnp.concatenate(rows, axis=0).astype(BF16)


def ramp(position, bit):
    lower = jnp.minimum((TILE - position - 0.5) / OVL, 1.0)
    upper = jnp.minimum((position + 0.5) / OVL, 1.0)
    return jnp.where(bit == 1, upper, lower)


def blend_weights(bits):
    lane = iota((TILE, LANES), 1)
    x = iota((TILE, LANES), 0).astype(F32)
    y = (lane // TILE).astype(F32)
    z = (lane % TILE).astype(F32)
    return ramp(x, bits[0]) * (ramp(y, bits[1]) * ramp(z, bits[2]))


def move_x(low, high, bit, roll):
    row = iota(low.shape, 1)
    from_high = jnp.where(row < OVL, roll(high, 6, 1), 0.0)
    from_low = jnp.where(row >= 8 - OVL, roll(low, 2, 1), 0.0)
    return jnp.where(bit == 0, from_high, from_low)


def move_y(low, high, bit, roll):
    lane = iota(low.shape, 2)
    from_high = jnp.where(lane < OVL * TILE, roll(high, 96, 2), 0.0)
    from_low = jnp.where(lane >= 128 - OVL * TILE, roll(low, 32, 2), 0.0)
    return jnp.where(bit == 0, from_high, from_low)


def pack_z(first, second, bit, roll):
    z = iota(first.shape, 2) % TILE
    head = jnp.where(bit == 0, roll(first, 128 - 10, 2), first)
    tail = jnp.where(bit == 0, roll(second, 128 - 2, 2), roll(second, 8, 2))
    return jnp.where(z < 8, head, tail)


def unpack_z(packed, bit, roll):
    z = iota(packed.shape, 2) % TILE
    keep = jnp.where(bit == 0, z - 10, 5 - z) >= 0
    head = jnp.where(bit == 0, roll(packed, 10, 2), packed)
    tail = jnp.where(bit == 0, roll(packed, 2, 2), roll(packed, 128 - 8, 2))
    return jnp.where(keep, head, 0.0), jnp.where(keep, tail, 0.0)


def two_halves(first, second):
    return jnp.concatenate([first, second], axis=1).astype(BF16)


def edge(value):
    upper = two_halves(value[0:1], value[1:2])
    return jnp.concatenate([upper, two_halves(value[2:3], jnp.zeros_like(value[2:3]))], axis=0)


def from_edge(ref):
    value = ref[...].astype(F32)
    return jnp.concatenate([value[0:1, :8], value[0:1, 8:], value[1:2, :8]], axis=0)


def kernel(
    em_ref, block_ref, slot_ref, w1_ref, b1_ref, w2_ref, b2_ref, wh_ref, bh_ref,
    out_ref,
    em, block, slot, w1, b1, w2, b2, wh, bh,
    sent, arrived, expand, first, second, heads, hidden, partial,
    x_out, y_out, z_out, e_out, x_in, y_in, z_in, e_in,
    load_sems, route_send, route_recv, swap_send, swap_recv,
    relayed, relay_send, relay_recv, mate_ready,
):
    roll = pltpu.roll
    blocks = SIDE * SIDE
    me = lax.axis_index("blocks")
    own = lax.axis_index("octant")
    bits = [own % 2, own // 2 % 2, own // 4]

    def partner(mask):
        total = 0
        for d in range(3):
            total = total + (1 - bits[d] if mask >> d & 1 else bits[d]) * 2**d
        return total

    my, mz = me // SIDE, me % SIDE
    early = mz < HUBS
    half = HUBS * SIDE
    slot_me = jnp.where(early, my * HUBS + mz, half + my * HUBS + mz - HUBS)
    group_me = jnp.where(early, SIDE, my)
    mate = my * SIDE + SIDE - 1 - mz
    spans = (4, 3, 5, 2, 6, 1, 7, 0)

    def signal(semaphore, target):
        pl.semaphore_signal(
            semaphore, inc=1, device_id={"blocks": target}, device_id_type=MESH
        )

    def unless(condition, visit):
        if condition is None:
            visit()
        else:
            pl.when(jnp.logical_not(condition))(visit)

    def greet(span, z):
        target = (my + span) % SIDE * SIDE + z
        unless(mz == z if span == 0 and z < HUBS else None, lambda: signal(barrier, target))

    def rows(source, target, semaphores, device):
        return pltpu.make_async_remote_copy(
            src_ref=source,
            dst_ref=target,
            send_sem=semaphores[0],
            recv_sem=semaphores[1],
            device_id={"blocks": device},
            device_id_type=MESH,
        )

    def send(span, z):
        row = (my + span) % SIDE * SIDE
        target = row + z
        if z < HUBS:
            device, place, semaphore = target, arrived, route_recv
        else:
            device, place, semaphore = row + SIDE - 1 - z, relayed, relay_recv.at[group_me]
        copy = rows(sent.at[target], place.at[slot_me], (route_send, semaphore), device)
        here = mz == (z if z < HUBS else SIDE - 1 - z)
        unless(here if span == 0 else None, copy.start)

    def landed(count, place, semaphores):
        return rows(place.at[pl.ds(0, count)], place.at[pl.ds(0, count)], semaphores, mate)

    loads = [
        pltpu.make_async_copy(source, target, load_sems.at[index])
        for index, (source, target) in enumerate(
            [
                (block_ref, block), (slot_ref, slot), (em_ref, em),
                (w1_ref, w1), (b1_ref, b1), (w2_ref, w2), (b2_ref, b2), (wh_ref, wh), (bh_ref, bh),
            ]
        )
    ]
    for load in loads[:3]:
        load.start()
    barrier = pltpu.get_barrier_semaphore()
    for mask in range(1, 8):
        pl.semaphore_signal(
            barrier, inc=1, device_id={"octant": partner(mask)}, device_id_type=MESH
        )

    @pl.when(early)
    def _():
        for span in spans:
            for z in range(SIDE):
                greet(span, z)

    @pl.when(jnp.logical_not(early))
    def _():
        pl.semaphore_wait(barrier, 7 + half)
        signal(mate_ready, mate)

    for load in loads[:3]:
        load.wait()
    packed = pack_rows(em[0], block[...], slot[...])
    sent[:, 0, :] = packed

    @pl.when(early)
    def _():
        pl.semaphore_wait(barrier, 7 + half - 1)
        arrived[slot_me] = sent[me]
        relayed[slot_me] = sent[mate]

    for span in spans:
        for z in range(SIDE):
            send(span, z)

    for load in loads[3:]:
        load.start()
    for load in loads[3:]:
        load.wait()
    expand[...] = expander()
    first[...] = first_matrix(w1[...])
    wide = replicated(w2[...].reshape(27 * C1, C1), 8)
    x_inner = iota((C1, 8 * C1), 1) // C1
    for x in range(10):
        for dy in range(3):
            for dz in range(3):
                block_rows = jnp.zeros((C1, 8 * C1), F32)
                for dx in range(3):
                    if 0 <= x + dx - 2 < 8:
                        at = (9 * dx + 3 * dy + dz) * C1
                        block_rows = jnp.where(
                            x_inner == x + dx - 2, wide[at : at + C1], block_rows
                        )
                at = (x * 3 + dy) * C1
                second[at : at + C1, dz * 256 : dz * 256 + 256] = block_rows.astype(BF16)
    heads[...] = head_matrix(wh[...])
    b1_col = column(b1[...])
    b2_col = column(b2[...])
    weights = blend_weights(bits)

    @pl.when(early)
    def _():
        def forward(start, count, awaited, group):
            landed(awaited, relayed, (relay_send, relay_recv.at[group])).wait_recv()
            part = pl.ds(start, count)
            rows(relayed.at[part], arrived.at[part], (relay_send, route_recv), mate).start()

        pl.semaphore_wait(mate_ready, 1)
        forward(0, half, half - 1, SIDE)
        for y in (0, 1, 7, 2, 6, 3, 5, 4):
            forward(half + y * HUBS, HUBS, HUBS, y)
        landed(blocks - 1, arrived, (route_send, route_recv)).wait_recv()

    @pl.when(jnp.logical_not(early))
    def _():
        landed(blocks, arrived, (route_send, route_recv)).wait_recv()

    volume = unpack_volume(arrived[:, 0, :], expand[...])
    one = dot(first[...], conv1_columns(volume, roll)).reshape(TILE, C1, LANES)
    one = jnp.maximum(one + b1_col[None], 0.0).reshape(TILE * C1, LANES)
    for h in range(2):
        hidden[h] = z_shifted(one[h * 256 : h * 256 + 256], roll)
    low = dot(second[3 * C1 : 30 * C1], hidden[0]).reshape(9, 3, C1, LANES)
    high = dot(second[: 27 * C1], hidden[1]).reshape(9, 3, C1, LANES)
    both = low[7:] + high[:2]
    partial[:7] = low[:7]
    partial[7:9] = both
    partial[9:] = high[2:]
    y = iota((1, 1, LANES), 2) // TILE
    total = partial[:, 1]
    total = total + jnp.where(y > 0, shift_lanes(partial[:, 0].reshape(512, LANES), -TILE, roll).reshape(TILE, C1, LANES), 0.0)
    total = total + jnp.where(y < TILE - 1, shift_lanes(partial[:, 2].reshape(512, LANES), TILE, roll).reshape(TILE, C1, LANES), 0.0)
    two = jnp.maximum(total + b2_col[None], 0.0).reshape(TILE * C1, LANES).astype(BF16)
    logits = dot(heads[...], two)
    pieces = []
    for a in range(AFF):
        pieces.append(jax.nn.sigmoid(logits[a * TILE : a * TILE + TILE] + bh[:, a : a + 1]) * weights)
    blended = jnp.stack(pieces, axis=0)

    tile = [[blended[:, 8 * hx : 8 * hx + 8, 128 * hy : 128 * hy + 128] for hy in range(2)] for hx in range(2)]
    swaps = {}

    def swap(mask, source, target):
        swaps[mask] = pltpu.make_async_remote_copy(
            src_ref=source,
            dst_ref=target,
            send_sem=swap_send.at[mask - 1],
            recv_sem=swap_recv.at[mask - 1],
            device_id={"octant": partner(mask)},
            device_id_type=MESH,
        )
        swaps[mask].start()

    z_out[...] = two_halves(
        pack_z(tile[0][0], tile[0][1], bits[2], roll), pack_z(tile[1][0], tile[1][1], bits[2], roll)
    )
    swap(4, z_out, z_in)
    at_x = [move_x(tile[0][hy], tile[1][hy], bits[0], roll) for hy in range(2)]
    e_out[1] = edge(pack_z(at_x[0], at_x[1], bits[2], roll))
    swap(5, e_out.at[1], e_in.at[1])
    at_y = [move_y(tile[hx][0], tile[hx][1], bits[1], roll) for hx in range(2)]
    y_out[...] = two_halves(at_y[0], at_y[1])
    swap(2, y_out, y_in)
    e_out[2] = edge(pack_z(at_y[0], at_y[1], bits[2], roll))
    swap(6, e_out.at[2], e_in.at[2])
    at_xy = move_y(at_x[0], at_x[1], bits[1], roll)
    e_out[0] = edge(at_xy)
    swap(3, e_out.at[0], e_in.at[0])
    e_out[3] = edge(pack_z(at_xy, at_xy, bits[2], roll))
    swap(7, e_out.at[3], e_in.at[3])
    x_out[...] = two_halves(at_x[0], at_x[1])
    swap(1, x_out, x_in)

    plane = [[tile[hx][hy] for hy in range(2)] for hx in range(2)]

    def add(hx, hy, value):
        plane[hx][hy] = plane[hx][hy] + value

    def is_half(bit, half, value):
        return jnp.where(bit == 1 - half, value, 0.0)

    swaps[1].wait_recv()
    face = x_in[...].astype(F32)
    for hy in range(2):
        value = face[:, 8 * hy : 8 * hy + 8]
        for hx in range(2):
            add(hx, hy, is_half(bits[0], hx, value))
    swaps[2].wait_recv()
    face = y_in[...].astype(F32)
    for hx in range(2):
        value = face[:, 8 * hx : 8 * hx + 8]
        for hy in range(2):
            add(hx, hy, is_half(bits[1], hy, value))
    swaps[3].wait_recv()
    swaps[7].wait_recv()
    corner = from_edge(e_in.at[0]) + unpack_z(from_edge(e_in.at[3]), bits[2], roll)[0]
    for hx in range(2):
        for hy in range(2):
            add(hx, hy, is_half(bits[0], hx, is_half(bits[1], hy, corner)))
    swaps[6].wait_recv()
    parts = unpack_z(from_edge(e_in.at[2]), bits[2], roll)
    for hx in range(2):
        for hy in range(2):
            add(hx, hy, is_half(bits[1], hy, parts[hx]))
    swaps[5].wait_recv()
    parts = unpack_z(from_edge(e_in.at[1]), bits[2], roll)
    for hx in range(2):
        for hy in range(2):
            add(hx, hy, is_half(bits[0], hx, parts[hy]))
    swaps[4].wait_recv()
    face = z_in[...].astype(F32)
    for hx in range(2):
        parts = unpack_z(face[:, 8 * hx : 8 * hx + 8], bits[2], roll)
        for hy in range(2):
            add(hx, hy, parts[hy])
    for hx in range(2):
        for hy in range(2):
            out_ref[:, pl.ds(TILE * hx + hy, 8, stride=2), :] = plane[hx][hy]
    for copy in swaps.values():
        copy.wait_send()

    @pl.when(early)
    def _():
        landed(blocks - 2, arrived, (route_send, route_recv)).wait_send()
        landed(blocks, arrived, (relay_send, route_recv)).wait_send()

    @pl.when(jnp.logical_not(early))
    def _():
        landed(blocks, arrived, (route_send, route_recv)).wait_send()


def shards(em_store, route_block, route_slot, conv1_w, conv1_b, conv2_w, conv2_b, head_w, head_b):
    operands = (
        em_store, route_block, route_slot, conv1_w, conv1_b.reshape(1, C1), conv2_w,
        conv2_b.reshape(1, C1), head_w, head_b.reshape(1, AFF),
    )
    operands = tuple(pltpu.with_memory_space_constraint(value, pltpu.HBM) for value in operands)
    vmem = pltpu.VMEM
    result = pl.pallas_call(
        kernel,
        out_shape=jax.ShapeDtypeStruct((AFF, 2 * TILE, 128), F32),
        in_specs=[pl.BlockSpec(memory_space=pltpu.HBM)] * len(operands),
        out_specs=pl.BlockSpec(memory_space=vmem),
        scratch_shapes=[vmem(value.shape, value.dtype) for value in operands]
        + [
            vmem((64, 1, 256), F32),
            vmem((64, 1, 256), F32),
            vmem((128, 4 * LANES), BF16),
            vmem((TILE * C1, LANES), BF16),
            vmem((30 * C1, 3 * 256), BF16),
            vmem((AFF * TILE, TILE * C1), BF16),
            vmem((2, 768, LANES), BF16),
            vmem((TILE, 3, C1, LANES), F32),
        ]
        + [
            vmem((AFF, 16, 128), BF16),
            vmem((AFF, 16, 128), BF16),
            vmem((AFF, 16, 128), BF16),
            vmem((4, 2, 16, 128), BF16),
        ]
        * 2
        + [
            pltpu.SemaphoreType.DMA((len(operands),)),
            pltpu.SemaphoreType.DMA,
            pltpu.SemaphoreType.DMA,
            pltpu.SemaphoreType.DMA((7,)),
            pltpu.SemaphoreType.DMA((7,)),
        ]
        + [
            vmem((64, 1, 256), F32),
            pltpu.SemaphoreType.DMA,
            pltpu.SemaphoreType.DMA((SIDE + 1,)),
            pltpu.SemaphoreType.REGULAR,
        ],
        compiler_params=pltpu.CompilerParams(
            collective_id=0, has_side_effects=True, vmem_limit_bytes=32 * 1024 * 1024
        ),
    )(*operands)
    return result.reshape(1, 1, AFF, TILE * LANES)


def solution(mesh):
    in_specs = (P("octant", "blocks", None), P("octant", "blocks"), P("octant", "blocks")) + (P(),) * 6
    out_specs = P("octant", "blocks", None, None)
    return jax.shard_map(shards, mesh=mesh, in_specs=in_specs, out_specs=out_specs, check_vma=False)
```

```python
import functools

import jax
import jax.numpy as jnp
from jax import lax
from jax.experimental import pallas as pl
from jax.experimental.pallas import tpu as pltpu
from jax.sharding import PartitionSpec as P

TILE = 16
OVL = 6
LANES = TILE * TILE
C1 = 32
SIDE = 8
HUBS = 3
RELAYS = {7: (0, 0), 6: (1, 0), 5: (2, 0), 4: (1, 1), 3: (0, 1)}
AFF = 3
MESH = pl.DeviceIdType.MESH
F32 = jnp.float32
BF16 = jnp.bfloat16


def iota(shape, dim):
    return lax.broadcasted_iota(jnp.int32, shape, dim)


def dot(a, b):
    return jnp.dot(a, b, preferred_element_type=F32)


def column(row):
    n = row.shape[1]
    return jnp.sum(jnp.where(iota((n, n), 0) == iota((n, n), 1), row, 0.0), axis=1, keepdims=True)


def pack_rows(em, targets, slots):
    n = em.shape[0]
    target_row = targets.astype(F32)
    target_col = column(target_row)
    earlier = (target_col == target_row) & (iota((n, n), 0) < iota((n, n), 1))
    rank_row = jnp.sum(jnp.where(earlier, 1.0, 0.0), axis=0, keepdims=True)
    slot_row = slots
    i_col = column((slot_row // 16 + 1).astype(F32))
    jk_col = column((slot_row % 16).astype(F32))
    lane = iota((n, 64), 1)
    labels = jnp.where(lane == 0, i_col, jnp.where(lane == 1, jk_col, 0.0)).astype(BF16)
    wide = jnp.concatenate([em, labels], axis=1)
    here = iota((64, n), 0).astype(F32) == target_row
    parts = [
        dot((here & (rank_row == rank)).astype(F32).astype(BF16), wide) for rank in (0.0, 1.0)
    ]
    return jnp.concatenate(parts, axis=1)


def expander():
    row = iota((128, 4 * LANES), 0)
    col = iota((128, 4 * LANES), 1)
    wanted = (col // LANES) * 16 + (col // 16 % 4) * 4 + col % 4
    return (row == wanted).astype(F32).astype(BF16)


def unpack_volume(arrived, expand):
    rows = jnp.concatenate([arrived[:, :128], arrived[:, 128:]], axis=0)
    i_col = rows[:, 64:65]
    jk_col = rows[:, 65:66]
    eye = iota((128, 128), 0) == iota((128, 128), 1)
    i_row = jnp.sum(jnp.where(eye, i_col, 0.0), axis=0, keepdims=True)
    lane = iota((128, LANES), 1)
    lane_jk = (lane // 64 * 4 + lane // 4 % 4).astype(F32)
    inside = lane_jk == jk_col
    spread = dot(rows.astype(BF16), expand)
    x_row = iota((TILE, 128), 0)
    volume = jnp.zeros((TILE, LANES), F32)
    for a in range(4):
        masked = jnp.where(inside, spread[:, a * LANES : (a + 1) * LANES], 0.0).astype(BF16)
        wanted = (x_row % 4 == a) & ((x_row // 4 + 1).astype(F32) == i_row)
        volume = volume + dot(wanted.astype(F32).astype(BF16), masked)
    return volume


def first_matrix(conv1_w):
    tap = iota((27, LANES), 0)
    col = iota((27, LANES), 1)
    x_in = iota((TILE, C1, LANES), 2) % TILE
    x_out = iota((TILE, C1, LANES), 0)
    total = jnp.zeros((TILE, C1, LANES), F32)
    for dx in range(3):
        spread = ((tap == 9 * dx + col // TILE) & (col < 9 * TILE)).astype(F32).astype(BF16)
        rows = dot(conv1_w, spread)
        total = jnp.where(x_in == x_out + dx - 1, rows[None], total)
    return total.reshape(TILE * C1, LANES).astype(BF16)


def replicated(weights, count):
    shape = (C1, count * C1)
    return dot(weights, (iota(shape, 0) == iota(shape, 1) % C1).astype(F32).astype(BF16))


def shift_lanes(value, by, roll):
    return roll(value, (-by) % value.shape[-1], value.ndim - 1)


def conv1_columns(volume, roll):
    lane = iota((TILE, LANES), 1)
    y, z = lane // TILE, lane % TILE
    rows = []
    for dy in (-1, 0, 1):
        for dz in (-1, 0, 1):
            moved = volume
            if dy or dz:
                moved = shift_lanes(volume, dy * TILE + dz, roll)
                keep = (y + dy >= 0) & (y + dy < TILE) & (z + dz >= 0) & (z + dz < TILE)
                moved = jnp.where(keep, moved, 0.0)
            rows.append(moved)
    rows.append(jnp.zeros((LANES - 9 * TILE, LANES), F32))
    return jnp.concatenate(rows, axis=0).astype(BF16)


def z_shifted(half, roll):
    z = iota(half.shape, 1) % TILE
    before = jnp.where(z > 0, shift_lanes(half, -1, roll), 0.0)
    after = jnp.where(z < TILE - 1, shift_lanes(half, 1, roll), 0.0)
    return jnp.concatenate([before, half, after], axis=0).astype(BF16)


def head_matrix(head_w):
    wide = replicated(head_w, TILE)
    x_in = iota((TILE, TILE * C1), 1) // C1
    x_out = iota((TILE, TILE * C1), 0)
    rows = [jnp.where(x_in == x_out, wide[a : a + 1], 0.0) for a in range(AFF)]
    return jnp.concatenate(rows, axis=0).astype(BF16)


def ramp(position, bit):
    lower = jnp.minimum((TILE - position - 0.5) / OVL, 1.0)
    upper = jnp.minimum((position + 0.5) / OVL, 1.0)
    return jnp.where(bit == 1, upper, lower)


def blend_weights(bits):
    lane = iota((TILE, LANES), 1)
    x = iota((TILE, LANES), 0).astype(F32)
    y = (lane // TILE).astype(F32)
    z = (lane % TILE).astype(F32)
    return ramp(x, bits[0]) * (ramp(y, bits[1]) * ramp(z, bits[2]))


def move_x(low, high, bit, roll):
    row = iota(low.shape, 1)
    from_high = jnp.where(row < OVL, roll(high, 6, 1), 0.0)
    from_low = jnp.where(row >= 8 - OVL, roll(low, 2, 1), 0.0)
    return jnp.where(bit == 0, from_high, from_low)


def move_y(low, high, bit, roll):
    lane = iota(low.shape, 2)
    from_high = jnp.where(lane < OVL * TILE, roll(high, 96, 2), 0.0)
    from_low = jnp.where(lane >= 128 - OVL * TILE, roll(low, 32, 2), 0.0)
    return jnp.where(bit == 0, from_high, from_low)


def pack_z(first, second, bit, roll):
    z = iota(first.shape, 2) % TILE
    head = jnp.where(bit == 0, roll(first, 128 - 10, 2), first)
    tail = jnp.where(bit == 0, roll(second, 128 - 2, 2), roll(second, 8, 2))
    return jnp.where(z < 8, head, tail)


def unpack_z(packed, bit, roll):
    z = iota(packed.shape, 2) % TILE
    keep = jnp.where(bit == 0, z - 10, 5 - z) >= 0
    head = jnp.where(bit == 0, roll(packed, 10, 2), packed)
    tail = jnp.where(bit == 0, roll(packed, 2, 2), roll(packed, 128 - 8, 2))
    return jnp.where(keep, head, 0.0), jnp.where(keep, tail, 0.0)


def kernel(
    em_ref, block_ref, slot_ref, w1_ref, b1_ref, w2_ref, b2_ref, wh_ref, bh_ref,
    out_ref,
    em, block, slot, w1, b1, w2, b2, wh, bh,
    sent, arrived, expand, first, second, heads, hidden, partial,
    x_out, y_out, z_out, e_out, x_in, y_in, z_in, e_in,
    load_sems, route_send, route_recv, swap_send, swap_recv,
    relayed, relay_send, relay_recv, mate_ready, mates_ready, partners_told,
):
    roll = pltpu.roll
    blocks = SIDE * SIDE
    me = lax.axis_index("blocks")
    own = lax.axis_index("octant")
    bits = [own % 2, own // 2 % 2, own // 4]

    def partner(mask):
        total = 0
        for d in range(3):
            total = total + (1 - bits[d] if mask >> d & 1 else bits[d]) * 2**d
        return total

    my, mz = me // SIDE, me % SIDE
    early = mz < HUBS
    twice = mz < 2
    hubs, others = HUBS * SIDE, SIDE - HUBS
    slot_me = jnp.where(early, my * HUBS + mz, hubs + my * others + mz - HUBS)
    group_me = jnp.where(early, SIDE, my)
    pupils = [my * SIDE + SIDE - 1 - mz, my * SIDE + HUBS + mz]
    relay = my * SIDE + jnp.where(mz >= SIDE - HUBS, SIDE - 1 - mz, mz - HUBS)
    lane_me = jnp.where(mz >= SIDE - HUBS, 0, 1)
    spans = (4, 3, 5, 2, 6, 1, 7, 0)
    rows_first = (0, 1, 7, 2, 6, 3, 5, 4)

    def signal(semaphore, target):
        pl.semaphore_signal(
            semaphore, inc=1, device_id={"blocks": target}, device_id_type=MESH
        )

    def unless(condition, visit):
        if condition is None:
            visit()
        else:
            pl.when(jnp.logical_not(condition))(visit)

    def greet(span, z):
        target = (my + span) % SIDE * SIDE + z
        unless(mz == z if span == 0 and z < HUBS else None, lambda: signal(barrier, target))

    def rows(source, target, semaphores, device):
        return pltpu.make_async_remote_copy(
            src_ref=source,
            dst_ref=target,
            send_sem=semaphores[0],
            recv_sem=semaphores[1],
            device_id={"blocks": device},
            device_id_type=MESH,
        )

    def send(y, z):
        target = y * SIDE + z
        if z < HUBS:
            device, place, semaphore = target, arrived, route_recv
        else:
            hub, lane = RELAYS[z]
            device, place = y * SIDE + hub, relayed.at[lane]
            semaphore = relay_recv.at[lane, group_me]
        copy = rows(sent.at[target], place.at[slot_me], (route_send, semaphore), device)
        unless(me == device, copy.start)

    def landed(count, place, semaphores):
        return rows(place.at[pl.ds(0, count)], place.at[pl.ds(0, count)], semaphores, (me + 1) % blocks)

    loads = [
        pltpu.make_async_copy(source, target, load_sems.at[index])
        for index, (source, target) in enumerate(
            [
                (block_ref, block), (slot_ref, slot), (em_ref, em),
                (w1_ref, w1), (b1_ref, b1), (w2_ref, w2), (b2_ref, b2), (wh_ref, wh), (bh_ref, bh),
            ]
        )
    ]
    for load in loads[:3]:
        load.start()
    barrier = pltpu.get_barrier_semaphore()

    def greet_partners(semaphore):
        for mask in range(1, 8):
            pl.semaphore_signal(
                semaphore, inc=1, device_id={"octant": partner(mask)}, device_id_type=MESH
            )


    @pl.when(early)
    def _():
        greet_partners(barrier)
        for span in spans:
            for z in range(SIDE):
                greet(span, z)

    for load in loads[:3]:
        load.wait()
    packed = pack_rows(em[0], block[...], slot[...])
    sent[:, 0, :] = packed

    @pl.when(early)
    def _():
        pl.semaphore_wait(barrier, 7 + hubs - 1)
        arrived[slot_me] = sent[me]
        relayed[0, slot_me] = sent[pupils[0]]
        relayed[1, slot_me] = sent[pupils[1]]

    @pl.when(jnp.logical_not(early))
    def _():
        pl.semaphore_wait(barrier, hubs)
        signal(mate_ready.at[lane_me], relay)

    for y in rows_first:
        for z in range(SIDE):
            send(y, z)

    for load in loads[3:]:
        load.start()
    for load in loads[3:]:
        load.wait()
    expand[...] = expander()
    first[...] = first_matrix(w1[...])
    wide = replicated(w2[...].reshape(27 * C1, C1), 8)
    x_inner = iota((C1, 8 * C1), 1) // C1
    for x in range(10):
        for dy in range(3):
            for dz in range(3):
                block_rows = jnp.zeros((C1, 8 * C1), F32)
                for dx in range(3):
                    if 0 <= x + dx - 2 < 8:
                        at = (9 * dx + 3 * dy + dz) * C1
                        block_rows = jnp.where(
                            x_inner == x + dx - 2, wide[at : at + C1], block_rows
                        )
                at = (x * 3 + dy) * C1
                second[at : at + C1, dz * 256 : dz * 256 + 256] = block_rows.astype(BF16)
    heads[...] = head_matrix(wh[...])
    b1_col = column(b1[...])
    b2_col = column(b2[...])
    weights = blend_weights(bits)

    def forward(lane, start, count, awaited, group):
        landed(awaited, relayed.at[lane], (relay_send, relay_recv.at[lane, group])).wait_recv()
        part = pl.ds(start, count)
        rows(
            relayed.at[lane, part], arrived.at[part], (relay_send, route_recv), pupils[lane]
        ).start()

    def begin(lane):
        pl.semaphore_wait(mate_ready.at[lane], 1)
        greet_partners(mates_ready.at[lane])
        forward(lane, 0, hubs, hubs - 1, SIDE)

    def finish(lane):
        pl.semaphore_wait(mates_ready.at[lane], 7)
        signal(partners_told, pupils[lane])

    def also(visit, *numbers):
        pl.when(twice)(functools.partial(visit, 1, *numbers))

    @pl.when(early)
    def _():
        also(begin)
        begin(0)
        for y in rows_first:
            group = (hubs + y * others, others, others, y)
            forward(0, *group)
            also(forward, *group)
        finish(0)
        also(finish)
        landed(blocks - 1, arrived, (route_send, route_recv)).wait_recv()

    @pl.when(jnp.logical_not(early))
    def _():
        landed(blocks, arrived, (route_send, route_recv)).wait_recv()

    volume = unpack_volume(arrived[:, 0, :], expand[...])
    one = dot(first[...], conv1_columns(volume, roll)).reshape(TILE, C1, LANES)
    one = jnp.maximum(one + b1_col[None], 0.0).reshape(TILE * C1, LANES)
    for h in range(2):
        hidden[h] = z_shifted(one[h * 256 : h * 256 + 256], roll)
    low = dot(second[3 * C1 : 30 * C1], hidden[0]).reshape(9, 3, C1, LANES)
    high = dot(second[: 27 * C1], hidden[1]).reshape(9, 3, C1, LANES)
    both = low[7:] + high[:2]
    partial[:7] = low[:7]
    partial[7:9] = both
    partial[9:] = high[2:]
    y = iota((1, 1, LANES), 2) // TILE
    total = partial[:, 1]
    total = total + jnp.where(y > 0, shift_lanes(partial[:, 0].reshape(512, LANES), -TILE, roll).reshape(TILE, C1, LANES), 0.0)
    total = total + jnp.where(y < TILE - 1, shift_lanes(partial[:, 2].reshape(512, LANES), TILE, roll).reshape(TILE, C1, LANES), 0.0)
    two = jnp.maximum(total + b2_col[None], 0.0).reshape(TILE * C1, LANES).astype(BF16)
    logits = dot(heads[...], two)
    pieces = []
    for a in range(AFF):
        pieces.append(jax.nn.sigmoid(logits[a * TILE : a * TILE + TILE] + bh[:, a : a + 1]) * weights)
    blended = jnp.stack(pieces, axis=0)

    tile = [[blended[:, 8 * hx : 8 * hx + 8, 128 * hy : 128 * hy + 128] for hy in range(2)] for hx in range(2)]
    @pl.when(jnp.logical_not(early))
    def _():
        pl.semaphore_wait(partners_told, 1)

    swaps = {}

    def swap(mask, source, target):
        swaps[mask] = pltpu.make_async_remote_copy(
            src_ref=source,
            dst_ref=target,
            send_sem=swap_send.at[mask - 1],
            recv_sem=swap_recv.at[mask - 1],
            device_id={"octant": partner(mask)},
            device_id_type=MESH,
        )
        swaps[mask].start()

    z_out[:, :8] = pack_z(tile[0][0], tile[0][1], bits[2], roll)
    z_out[:, 8:] = pack_z(tile[1][0], tile[1][1], bits[2], roll)
    swap(4, z_out, z_in)
    at_x = [move_x(tile[0][hy], tile[1][hy], bits[0], roll) for hy in range(2)]
    e_out[1] = pack_z(at_x[0], at_x[1], bits[2], roll)
    swap(5, e_out.at[1], e_in.at[1])
    at_y = [move_y(tile[hx][0], tile[hx][1], bits[1], roll) for hx in range(2)]
    y_out[:, :8] = at_y[0]
    y_out[:, 8:] = at_y[1]
    swap(2, y_out, y_in)
    e_out[2] = pack_z(at_y[0], at_y[1], bits[2], roll)
    swap(6, e_out.at[2], e_in.at[2])
    at_xy = move_y(at_x[0], at_x[1], bits[1], roll)
    e_out[0] = at_xy
    swap(3, e_out.at[0], e_in.at[0])
    e_out[3] = pack_z(at_xy, at_xy, bits[2], roll)
    swap(7, e_out.at[3], e_in.at[3])
    x_out[:, :, :128] = at_x[0]
    x_out[:, :, 128:] = at_x[1]
    swap(1, x_out, x_in)

    plane = [[tile[hx][hy] for hy in range(2)] for hx in range(2)]

    def add(hx, hy, value):
        plane[hx][hy] = plane[hx][hy] + value

    def is_half(bit, half, value):
        return jnp.where(bit == 1 - half, value, 0.0)

    swaps[1].wait_recv()
    for hy in range(2):
        value = x_in[:, :, 128 * hy : 128 * hy + 128]
        for hx in range(2):
            add(hx, hy, is_half(bits[0], hx, value))
    swaps[2].wait_recv()
    for hx in range(2):
        value = y_in[:, 8 * hx : 8 * hx + 8]
        for hy in range(2):
            add(hx, hy, is_half(bits[1], hy, value))
    swaps[3].wait_recv()
    swaps[7].wait_recv()
    corner = e_in[0] + unpack_z(e_in[3], bits[2], roll)[0]
    for hx in range(2):
        for hy in range(2):
            add(hx, hy, is_half(bits[0], hx, is_half(bits[1], hy, corner)))
    swaps[6].wait_recv()
    parts = unpack_z(e_in[2], bits[2], roll)
    for hx in range(2):
        for hy in range(2):
            add(hx, hy, is_half(bits[1], hy, parts[hx]))
    swaps[5].wait_recv()
    parts = unpack_z(e_in[1], bits[2], roll)
    for hx in range(2):
        for hy in range(2):
            add(hx, hy, is_half(bits[0], hx, parts[hy]))
    swaps[4].wait_recv()
    for hx in range(2):
        parts = unpack_z(z_in[:, 8 * hx : 8 * hx + 8], bits[2], roll)
        for hy in range(2):
            add(hx, hy, parts[hy])
    for hx in range(2):
        for hy in range(2):
            out_ref[:, pl.ds(TILE * hx + hy, 8, stride=2), :] = plane[hx][hy]
    for copy in swaps.values():
        copy.wait_send()

    @pl.when(early)
    def _():
        landed(blocks - 3, arrived, (route_send, route_recv)).wait_send()
        landed(blocks, arrived, (relay_send, route_recv)).wait_send()

    @pl.when(twice)
    def _():
        landed(blocks, arrived, (relay_send, route_recv)).wait_send()

    @pl.when(mz == HUBS - 1)
    def _():
        landed(1, arrived, (route_send, route_recv)).wait_send()

    @pl.when(jnp.logical_not(early))
    def _():
        landed(blocks, arrived, (route_send, route_recv)).wait_send()


def shards(em_store, route_block, route_slot, conv1_w, conv1_b, conv2_w, conv2_b, head_w, head_b):
    operands = (
        em_store, route_block, route_slot, conv1_w, conv1_b.reshape(1, C1), conv2_w,
        conv2_b.reshape(1, C1), head_w, head_b.reshape(1, AFF),
    )
    operands = tuple(pltpu.with_memory_space_constraint(value, pltpu.HBM) for value in operands)
    vmem = pltpu.VMEM
    result = pl.pallas_call(
        kernel,
        out_shape=jax.ShapeDtypeStruct((AFF, 2 * TILE, 128), F32),
        in_specs=[pl.BlockSpec(memory_space=pltpu.HBM)] * len(operands),
        out_specs=pl.BlockSpec(memory_space=vmem),
        scratch_shapes=[vmem(value.shape, value.dtype) for value in operands]
        + [
            vmem((64, 1, 256), F32),
            vmem((64, 1, 256), F32),
            vmem((128, 4 * LANES), BF16),
            vmem((TILE * C1, LANES), BF16),
            vmem((30 * C1, 3 * 256), BF16),
            vmem((AFF * TILE, TILE * C1), BF16),
            vmem((2, 768, LANES), BF16),
            vmem((TILE, 3, C1, LANES), F32),
        ]
        + [
            vmem((AFF, 8, 256), F32),
            vmem((AFF, 16, 128), F32),
            vmem((AFF, 16, 128), F32),
            vmem((4, AFF, 8, 128), F32),
        ]
        * 2
        + [
            pltpu.SemaphoreType.DMA((len(operands),)),
            pltpu.SemaphoreType.DMA,
            pltpu.SemaphoreType.DMA,
            pltpu.SemaphoreType.DMA((7,)),
            pltpu.SemaphoreType.DMA((7,)),
        ]
        + [
            vmem((2, 64, 1, 256), F32),
            pltpu.SemaphoreType.DMA,
            pltpu.SemaphoreType.DMA((2, SIDE + 1)),
            pltpu.SemaphoreType.REGULAR((2,)),
            pltpu.SemaphoreType.REGULAR((2,)),
            pltpu.SemaphoreType.REGULAR,
        ],
        compiler_params=pltpu.CompilerParams(
            collective_id=0, has_side_effects=True, vmem_limit_bytes=32 * 1024 * 1024
        ),
    )(*operands)
    return result.reshape(1, 1, AFF, TILE * LANES)


def solution(mesh):
    in_specs = (P("octant", "blocks", None), P("octant", "blocks"), P("octant", "blocks")) + (P(),) * 6
    out_specs = P("octant", "blocks", None, None)
    return jax.shard_map(shards, mesh=mesh, in_specs=in_specs, out_specs=out_specs, check_vma=False)
```

```python
import functools

import jax
import jax.numpy as jnp
from jax import lax
from jax.experimental import pallas as pl
from jax.experimental.pallas import tpu as pltpu
from jax.sharding import PartitionSpec as P

TILE = 16
OVL = 6
LANES = TILE * TILE
C1 = 32
SIDE = 8
HUBS = 3
RELAYS = {7: (0, 0), 6: (1, 0), 5: (2, 0), 4: (1, 1), 3: (0, 1)}
AFF = 3
MESH = pl.DeviceIdType.MESH
F32 = jnp.float32
BF16 = jnp.bfloat16


def iota(shape, dim):
    return lax.broadcasted_iota(jnp.int32, shape, dim)


def dot(a, b):
    return jnp.dot(a, b, preferred_element_type=F32)


def column(row):
    n = row.shape[1]
    return jnp.sum(jnp.where(iota((n, n), 0) == iota((n, n), 1), row, 0.0), axis=1, keepdims=True)


def pack_rows(em, targets, slots):
    n = em.shape[0]
    target_row = targets.astype(F32)
    target_col = column(target_row)
    earlier = (target_col == target_row) & (iota((n, n), 0) < iota((n, n), 1))
    rank_row = jnp.sum(jnp.where(earlier, 1.0, 0.0), axis=0, keepdims=True)
    slot_row = slots
    i_col = column((slot_row // 16 + 1).astype(F32))
    jk_col = column((slot_row % 16).astype(F32))
    lane = iota((n, 64), 1)
    labels = jnp.where(lane == 0, i_col, jnp.where(lane == 1, jk_col, 0.0)).astype(BF16)
    wide = jnp.concatenate([em, labels], axis=1)
    here = iota((64, n), 0).astype(F32) == target_row
    parts = [
        dot((here & (rank_row == rank)).astype(F32).astype(BF16), wide) for rank in (0.0, 1.0)
    ]
    return jnp.concatenate(parts, axis=1)


def expander():
    row = iota((128, 4 * 128), 0)
    col = iota((128, 4 * 128), 1)
    wanted = (col // 128) * 16 + (col // 16 % 4) * 4 + col % 4
    return (row == wanted).astype(F32).astype(BF16)


def unpack_volume(arrived, expand):
    rows = jnp.concatenate([arrived[:, :128], arrived[:, 128:]], axis=0)
    i_col = rows[:, 64:65]
    jk_col = rows[:, 65:66]
    eye = iota((128, 128), 0) == iota((128, 128), 1)
    i_row = jnp.sum(jnp.where(eye, i_col, 0.0), axis=0, keepdims=True)
    lane = iota((128, LANES), 1)
    lane_jk = (lane // 64 * 4 + lane // 4 % 4).astype(F32)
    inside = lane_jk == jk_col
    spread = dot(rows.astype(BF16), expand)
    x_row = iota((TILE, 128), 0)
    volume = jnp.zeros((TILE, LANES), F32)
    for a in range(4):
        part = spread[:, a * 128 : a * 128 + 128]
        masked = jnp.where(inside, jnp.concatenate([part, part], axis=1), 0.0).astype(BF16)
        wanted = (x_row % 4 == a) & ((x_row // 4 + 1).astype(F32) == i_row)
        volume = volume + dot(wanted.astype(F32).astype(BF16), masked)
    return volume


def first_matrix(conv1_w):
    tap = iota((27, LANES), 0)
    col = iota((27, LANES), 1)
    x_in = iota((TILE, C1, LANES), 2) % TILE
    x_out = iota((TILE, C1, LANES), 0)
    total = jnp.zeros((TILE, C1, LANES), F32)
    for dx in range(3):
        spread = ((tap == 9 * dx + col // TILE) & (col < 9 * TILE)).astype(F32).astype(BF16)
        rows = dot(conv1_w, spread)
        total = jnp.where(x_in == x_out + dx - 1, rows[None], total)
    return total.reshape(TILE * C1, LANES).astype(BF16)


def replicated(weights, count):
    shape = (C1, count * C1)
    return dot(weights, (iota(shape, 0) == iota(shape, 1) % C1).astype(F32).astype(BF16))


def shift_lanes(value, by, roll):
    return roll(value, (-by) % value.shape[-1], value.ndim - 1)


def conv1_columns(volume, roll):
    lane = iota((TILE, LANES), 1)
    y, z = lane // TILE, lane % TILE
    rows = []
    for dy in (-1, 0, 1):
        for dz in (-1, 0, 1):
            moved = volume
            if dy or dz:
                moved = shift_lanes(volume, dy * TILE + dz, roll)
                keep = (y + dy >= 0) & (y + dy < TILE) & (z + dz >= 0) & (z + dz < TILE)
                moved = jnp.where(keep, moved, 0.0)
            rows.append(moved)
    rows.append(jnp.zeros((LANES - 9 * TILE, LANES), F32))
    return jnp.concatenate(rows, axis=0).astype(BF16)


def z_shifted(value, roll):
    z = iota(value.shape, 1) % TILE
    before = jnp.where(z > 0, shift_lanes(value, -1, roll), 0.0)
    after = jnp.where(z < TILE - 1, shift_lanes(value, 1, roll), 0.0)
    return [part.astype(BF16) for part in (before, value, after)]


def head_matrix(head_w):
    wide = replicated(head_w, TILE)
    x_in = iota((TILE, TILE * C1), 1) // C1
    x_out = iota((TILE, TILE * C1), 0)
    rows = [jnp.where(x_in == x_out, wide[a : a + 1], 0.0) for a in range(AFF)]
    return jnp.concatenate(rows, axis=0).astype(BF16)


def ramp(position, bit):
    lower = jnp.minimum((TILE - position - 0.5) / OVL, 1.0)
    upper = jnp.minimum((position + 0.5) / OVL, 1.0)
    return jnp.where(bit == 1, upper, lower)


def blend_weights(bits):
    lane = iota((TILE, LANES), 1)
    x = iota((TILE, LANES), 0).astype(F32)
    y = (lane // TILE).astype(F32)
    z = (lane % TILE).astype(F32)
    return ramp(x, bits[0]) * (ramp(y, bits[1]) * ramp(z, bits[2]))


def move_x(low, high, bit, roll):
    row = iota(low.shape, 1)
    from_high = jnp.where(row < OVL, roll(high, 6, 1), 0.0)
    from_low = jnp.where(row >= 8 - OVL, roll(low, 2, 1), 0.0)
    return jnp.where(bit == 0, from_high, from_low)


def move_y(low, high, bit, roll):
    lane = iota(low.shape, 2)
    from_high = jnp.where(lane < OVL * TILE, roll(high, 96, 2), 0.0)
    from_low = jnp.where(lane >= 128 - OVL * TILE, roll(low, 32, 2), 0.0)
    return jnp.where(bit == 0, from_high, from_low)


def pack_z(first, second, bit, roll):
    z = iota(first.shape, 2) % TILE
    head = jnp.where(bit == 0, roll(first, 128 - 10, 2), first)
    tail = jnp.where(bit == 0, roll(second, 128 - 2, 2), roll(second, 8, 2))
    return jnp.where(z < 8, head, tail)


def unpack_z(packed, bit, roll):
    z = iota(packed.shape, 2) % TILE
    keep = jnp.where(bit == 0, z - 10, 5 - z) >= 0
    head = jnp.where(bit == 0, roll(packed, 10, 2), packed)
    tail = jnp.where(bit == 0, roll(packed, 2, 2), roll(packed, 128 - 8, 2))
    return jnp.where(keep, head, 0.0), jnp.where(keep, tail, 0.0)


def kernel(
    em_ref, block_ref, slot_ref, w1_ref, b1_ref, w2_ref, b2_ref, wh_ref, bh_ref,
    out_ref,
    em, block, slot, w1, b1, w2, b2, wh, bh,
    sent, arrived, expand, first, second, heads, hidden, partial,
    x_out, y_out, z_out, e_out, x_in, y_in, z_in, e_in,
    load_sems, route_send, route_recv, swap_send, swap_recv,
    relayed, relay_send, relay_recv, mate_ready, mates_ready, partners_told,
):
    roll = pltpu.roll
    blocks = SIDE * SIDE
    me = lax.axis_index("blocks")
    own = lax.axis_index("octant")
    bits = [own % 2, own // 2 % 2, own // 4]

    def partner(mask):
        total = 0
        for d in range(3):
            total = total + (1 - bits[d] if mask >> d & 1 else bits[d]) * 2**d
        return total

    my, mz = me // SIDE, me % SIDE
    early = mz < HUBS
    twice = mz < 2
    hubs, others = HUBS * SIDE, SIDE - HUBS
    slot_me = jnp.where(early, my * HUBS + mz, hubs + my * others + mz - HUBS)
    group_me = jnp.where(early, SIDE, my)
    pupils = [my * SIDE + SIDE - 1 - mz, my * SIDE + HUBS + mz]
    relay = my * SIDE + jnp.where(mz >= SIDE - HUBS, SIDE - 1 - mz, mz - HUBS)
    lane_me = jnp.where(mz >= SIDE - HUBS, 0, 1)
    spans = (4, 3, 5, 2, 6, 1, 7, 0)
    rows_first = (0, 1, 7, 2, 6, 3, 5, 4)

    def signal(semaphore, target):
        pl.semaphore_signal(
            semaphore, inc=1, device_id={"blocks": target}, device_id_type=MESH
        )

    def unless(condition, visit):
        if condition is None:
            visit()
        else:
            pl.when(jnp.logical_not(condition))(visit)

    def greet(span, z):
        target = (my + span) % SIDE * SIDE + z
        unless(mz == z if span == 0 and z < HUBS else None, lambda: signal(barrier, target))

    def rows(source, target, semaphores, device):
        return pltpu.make_async_remote_copy(
            src_ref=source,
            dst_ref=target,
            send_sem=semaphores[0],
            recv_sem=semaphores[1],
            device_id={"blocks": device},
            device_id_type=MESH,
        )

    def send(y, z):
        target = y * SIDE + z
        if z < HUBS:
            device, place, semaphore = target, arrived, route_recv
        else:
            hub, lane = RELAYS[z]
            device, place = y * SIDE + hub, relayed.at[lane]
            semaphore = relay_recv.at[lane, group_me]
        copy = rows(sent.at[target], place.at[slot_me], (route_send, semaphore), device)
        unless(me == device, copy.start)

    def landed(count, place, semaphores):
        return rows(place.at[pl.ds(0, count)], place.at[pl.ds(0, count)], semaphores, (me + 1) % blocks)

    loads = [
        pltpu.make_async_copy(source, target, load_sems.at[index])
        for index, (source, target) in enumerate(
            [
                (block_ref, block), (slot_ref, slot), (em_ref, em),
                (w1_ref, w1), (b1_ref, b1), (w2_ref, w2), (b2_ref, b2), (wh_ref, wh), (bh_ref, bh),
            ]
        )
    ]
    for load in loads[:3]:
        load.start()
    barrier = pltpu.get_barrier_semaphore()

    def greet_partners(semaphore):
        for mask in range(1, 8):
            pl.semaphore_signal(
                semaphore, inc=1, device_id={"octant": partner(mask)}, device_id_type=MESH
            )


    @pl.when(early)
    def _():
        greet_partners(barrier)
        for span in spans:
            for z in range(SIDE):
                greet(span, z)

    for load in loads[:3]:
        load.wait()
    packed = pack_rows(em[0], block[...], slot[...])
    sent[:, 0, :] = packed

    @pl.when(early)
    def _():
        pl.semaphore_wait(barrier, 7 + hubs - 1)
        arrived[slot_me] = sent[me]
        relayed[0, slot_me] = sent[pupils[0]]
        relayed[1, slot_me] = sent[pupils[1]]

    @pl.when(jnp.logical_not(early))
    def _():
        pl.semaphore_wait(barrier, hubs)
        signal(mate_ready.at[lane_me], relay)

    for y in rows_first:
        for z in range(SIDE):
            send(y, z)

    for load in loads[3:]:
        load.start()
    for load in loads[3:]:
        load.wait()
    expand[...] = expander()
    first[...] = first_matrix(w1[...])
    wide = replicated(w2[...].reshape(27 * C1, C1), 2)
    x_inner = iota((C1, 2 * C1), 1) // C1
    for x in range(4):
        for dy in range(3):
            columns = []
            for dz in range(3):
                block_rows = jnp.zeros((C1, 2 * C1), F32)
                for dx in range(3):
                    if 0 <= x + dx - 2 < 2:
                        at = (9 * dx + 3 * dy + dz) * C1
                        block_rows = jnp.where(
                            x_inner == x + dx - 2, wide[at : at + C1], block_rows
                        )
                columns.append(block_rows)
            at = (x * 3 + dy) * C1
            second[at : at + C1, :] = jnp.concatenate(columns, axis=1).astype(BF16)
    heads[...] = head_matrix(wh[...])
    b1_col = column(b1[...])
    b2_col = column(b2[...])
    weights = blend_weights(bits)

    def forward(lane, start, count, awaited, group):
        landed(awaited, relayed.at[lane], (relay_send, relay_recv.at[lane, group])).wait_recv()
        part = pl.ds(start, count)
        rows(
            relayed.at[lane, part], arrived.at[part], (relay_send, route_recv), pupils[lane]
        ).start()

    def begin(lane):
        pl.semaphore_wait(mate_ready.at[lane], 1)
        greet_partners(mates_ready.at[lane])
        forward(lane, 0, hubs, hubs - 1, SIDE)

    def finish(lane):
        pl.semaphore_wait(mates_ready.at[lane], 7)
        signal(partners_told, pupils[lane])

    def also(visit, *numbers):
        pl.when(twice)(functools.partial(visit, 1, *numbers))

    @pl.when(early)
    def _():
        also(begin)
        begin(0)
        for y in rows_first:
            group = (hubs + y * others, others, others, y)
            forward(0, *group)
            also(forward, *group)
        finish(0)
        also(finish)
        landed(blocks - 1, arrived, (route_send, route_recv)).wait_recv()

    @pl.when(jnp.logical_not(early))
    def _():
        landed(blocks, arrived, (route_send, route_recv)).wait_recv()

    volume = unpack_volume(arrived[:, 0, :], expand[...])
    one = dot(first[...], conv1_columns(volume, roll)).reshape(TILE, C1, LANES)
    one = jnp.maximum(one + b1_col[None], 0.0).reshape(TILE * C1, LANES)
    for dz, part in enumerate(z_shifted(one, roll)):
        hidden[:, dz] = part.reshape(8, 2 * C1, LANES)
    held = None
    for group in range(8):
        sums = dot(second[...], hidden[group].reshape(6 * C1, LANES)).reshape(4, 3, C1, LANES)
        if held is None:
            partial[0] = sums[1]
        else:
            partial[2 * group - 1] = held[0] + sums[0]
            partial[2 * group] = held[1] + sums[1]
        held = sums[2:]
    partial[TILE - 1] = held[0]
    y = iota((1, 1, LANES), 2) // TILE
    total = partial[:, 1]
    total = total + jnp.where(y > 0, shift_lanes(partial[:, 0].reshape(512, LANES), -TILE, roll).reshape(TILE, C1, LANES), 0.0)
    total = total + jnp.where(y < TILE - 1, shift_lanes(partial[:, 2].reshape(512, LANES), TILE, roll).reshape(TILE, C1, LANES), 0.0)
    two = jnp.maximum(total + b2_col[None], 0.0).reshape(TILE * C1, LANES).astype(BF16)
    logits = dot(heads[...], two)
    pieces = []
    for a in range(AFF):
        pieces.append(jax.nn.sigmoid(logits[a * TILE : a * TILE + TILE] + bh[:, a : a + 1]) * weights)
    blended = jnp.stack(pieces, axis=0)

    tile = [[blended[:, 8 * hx : 8 * hx + 8, 128 * hy : 128 * hy + 128] for hy in range(2)] for hx in range(2)]
    @pl.when(jnp.logical_not(early))
    def _():
        pl.semaphore_wait(partners_told, 1)

    swaps = {}

    def swap(mask, source, target):
        swaps[mask] = pltpu.make_async_remote_copy(
            src_ref=source,
            dst_ref=target,
            send_sem=swap_send.at[mask - 1],
            recv_sem=swap_recv.at[mask - 1],
            device_id={"octant": partner(mask)},
            device_id_type=MESH,
        )
        swaps[mask].start()

    z_out[:, :8] = pack_z(tile[0][0], tile[0][1], bits[2], roll)
    z_out[:, 8:] = pack_z(tile[1][0], tile[1][1], bits[2], roll)
    swap(4, z_out, z_in)
    at_x = [move_x(tile[0][hy], tile[1][hy], bits[0], roll) for hy in range(2)]
    e_out[1] = pack_z(at_x[0], at_x[1], bits[2], roll)
    swap(5, e_out.at[1], e_in.at[1])
    at_y = [move_y(tile[hx][0], tile[hx][1], bits[1], roll) for hx in range(2)]
    y_out[:, :8] = at_y[0]
    y_out[:, 8:] = at_y[1]
    swap(2, y_out, y_in)
    e_out[2] = pack_z(at_y[0], at_y[1], bits[2], roll)
    swap(6, e_out.at[2], e_in.at[2])
    at_xy = move_y(at_x[0], at_x[1], bits[1], roll)
    e_out[0] = at_xy
    swap(3, e_out.at[0], e_in.at[0])
    e_out[3] = pack_z(at_xy, at_xy, bits[2], roll)
    swap(7, e_out.at[3], e_in.at[3])
    x_out[:, :, :128] = at_x[0]
    x_out[:, :, 128:] = at_x[1]
    swap(1, x_out, x_in)

    plane = [[tile[hx][hy] for hy in range(2)] for hx in range(2)]

    def add(hx, hy, value):
        plane[hx][hy] = plane[hx][hy] + value

    def is_half(bit, half, value):
        return jnp.where(bit == 1 - half, value, 0.0)

    swaps[1].wait_recv()
    for hy in range(2):
        value = x_in[:, :, 128 * hy : 128 * hy + 128]
        for hx in range(2):
            add(hx, hy, is_half(bits[0], hx, value))
    swaps[2].wait_recv()
    for hx in range(2):
        value = y_in[:, 8 * hx : 8 * hx + 8]
        for hy in range(2):
            add(hx, hy, is_half(bits[1], hy, value))
    swaps[3].wait_recv()
    swaps[7].wait_recv()
    corner = e_in[0] + unpack_z(e_in[3], bits[2], roll)[0]
    for hx in range(2):
        for hy in range(2):
            add(hx, hy, is_half(bits[0], hx, is_half(bits[1], hy, corner)))
    swaps[6].wait_recv()
    parts = unpack_z(e_in[2], bits[2], roll)
    for hx in range(2):
        for hy in range(2):
            add(hx, hy, is_half(bits[1], hy, parts[hx]))
    swaps[5].wait_recv()
    parts = unpack_z(e_in[1], bits[2], roll)
    for hx in range(2):
        for hy in range(2):
            add(hx, hy, is_half(bits[0], hx, parts[hy]))
    swaps[4].wait_recv()
    for hx in range(2):
        parts = unpack_z(z_in[:, 8 * hx : 8 * hx + 8], bits[2], roll)
        for hy in range(2):
            add(hx, hy, parts[hy])
    for hx in range(2):
        for hy in range(2):
            out_ref[:, pl.ds(TILE * hx + hy, 8, stride=2), :] = plane[hx][hy]
    for copy in swaps.values():
        copy.wait_send()

    @pl.when(early)
    def _():
        landed(blocks - 3, arrived, (route_send, route_recv)).wait_send()
        landed(blocks, arrived, (relay_send, route_recv)).wait_send()

    @pl.when(twice)
    def _():
        landed(blocks, arrived, (relay_send, route_recv)).wait_send()

    @pl.when(mz == HUBS - 1)
    def _():
        landed(1, arrived, (route_send, route_recv)).wait_send()

    @pl.when(jnp.logical_not(early))
    def _():
        landed(blocks, arrived, (route_send, route_recv)).wait_send()


def shards(em_store, route_block, route_slot, conv1_w, conv1_b, conv2_w, conv2_b, head_w, head_b):
    operands = (
        em_store, route_block, route_slot, conv1_w, conv1_b.reshape(1, C1), conv2_w,
        conv2_b.reshape(1, C1), head_w, head_b.reshape(1, AFF),
    )
    operands = tuple(pltpu.with_memory_space_constraint(value, pltpu.HBM) for value in operands)
    vmem = pltpu.VMEM
    result = pl.pallas_call(
        kernel,
        out_shape=jax.ShapeDtypeStruct((AFF, 2 * TILE, 128), F32),
        in_specs=[pl.BlockSpec(memory_space=pltpu.HBM)] * len(operands),
        out_specs=pl.BlockSpec(memory_space=vmem),
        scratch_shapes=[vmem(value.shape, value.dtype) for value in operands]
        + [
            vmem((64, 1, 256), F32),
            vmem((64, 1, 256), F32),
            vmem((128, 4 * 128), BF16),
            vmem((TILE * C1, LANES), BF16),
            vmem((12 * C1, 6 * C1), BF16),
            vmem((AFF * TILE, TILE * C1), BF16),
            vmem((8, 3, 2 * C1, LANES), BF16),
            vmem((TILE, 3, C1, LANES), F32),
        ]
        + [
            vmem((AFF, 8, 256), F32),
            vmem((AFF, 16, 128), F32),
            vmem((AFF, 16, 128), F32),
            vmem((4, AFF, 8, 128), F32),
        ]
        * 2
        + [
            pltpu.SemaphoreType.DMA((len(operands),)),
            pltpu.SemaphoreType.DMA,
            pltpu.SemaphoreType.DMA,
            pltpu.SemaphoreType.DMA((7,)),
            pltpu.SemaphoreType.DMA((7,)),
        ]
        + [
            vmem((2, 64, 1, 256), F32),
            pltpu.SemaphoreType.DMA,
            pltpu.SemaphoreType.DMA((2, SIDE + 1)),
            pltpu.SemaphoreType.REGULAR((2,)),
            pltpu.SemaphoreType.REGULAR((2,)),
            pltpu.SemaphoreType.REGULAR,
        ],
        compiler_params=pltpu.CompilerParams(
            collective_id=0, has_side_effects=True, vmem_limit_bytes=32 * 1024 * 1024
        ),
    )(*operands)
    return result.reshape(1, 1, AFF, TILE * LANES)


def solution(mesh):
    in_specs = (P("octant", "blocks", None), P("octant", "blocks"), P("octant", "blocks")) + (P(),) * 6
    out_specs = P("octant", "blocks", None, None)
    return jax.shard_map(shards, mesh=mesh, in_specs=in_specs, out_specs=out_specs, check_vma=False)
```

```python
import functools

import jax
import jax.numpy as jnp
from jax import lax
from jax.experimental import pallas as pl
from jax.experimental.pallas import tpu as pltpu
from jax.sharding import PartitionSpec as P

TILE = 16
OVL = 6
LANES = TILE * TILE
C1 = 32
SIDE = 8
HUBS = 3
RELAYS = {7: (0, 0), 6: (1, 0), 5: (2, 0), 4: (1, 1), 3: (0, 1)}
AFF = 3
MESH = pl.DeviceIdType.MESH
F32 = jnp.float32
BF16 = jnp.bfloat16


def iota(shape, dim):
    return lax.broadcasted_iota(jnp.int32, shape, dim)


def dot(a, b):
    return jnp.dot(a, b, preferred_element_type=F32)


def column(row):
    n = row.shape[1]
    return jnp.sum(jnp.where(iota((n, n), 0) == iota((n, n), 1), row, 0.0), axis=1, keepdims=True)


def pack_rows(em, targets, slots):
    n = em.shape[0]
    target_row = targets.astype(F32)
    target_col = column(target_row)
    earlier = (target_col == target_row) & (iota((n, n), 0) < iota((n, n), 1))
    rank_row = jnp.sum(jnp.where(earlier, 1.0, 0.0), axis=0, keepdims=True)
    slot_row = slots
    i_col = column((slot_row // 16 + 1).astype(F32))
    jk_col = column((slot_row % 16).astype(F32))
    lane = iota((n, 64), 1)
    labels = jnp.where(lane == 0, i_col, jnp.where(lane == 1, jk_col, 0.0)).astype(BF16)
    wide = jnp.concatenate([em, labels], axis=1)
    here = iota((64, n), 0).astype(F32) == target_row
    parts = [
        dot((here & (rank_row == rank)).astype(F32).astype(BF16), wide) for rank in (0.0, 1.0)
    ]
    return jnp.concatenate(parts, axis=1)


def expander():
    row = iota((128, 4 * 128), 0)
    col = iota((128, 4 * 128), 1)
    wanted = (col // 128) * 16 + (col // 16 % 4) * 4 + col % 4
    return (row == wanted).astype(F32).astype(BF16)


def unpack_volume(arrived, expand):
    rows = jnp.concatenate([arrived[:, :128], arrived[:, 128:]], axis=0)
    i_col = rows[:, 64:65]
    jk_col = rows[:, 65:66]
    eye = iota((128, 128), 0) == iota((128, 128), 1)
    i_row = jnp.sum(jnp.where(eye, i_col, 0.0), axis=0, keepdims=True)
    lane = iota((128, LANES), 1)
    lane_jk = (lane // 64 * 4 + lane // 4 % 4).astype(F32)
    inside = lane_jk == jk_col
    spread = dot(rows.astype(BF16), expand)
    x_row = iota((TILE, 128), 0)
    volume = jnp.zeros((TILE, LANES), F32)
    for a in range(4):
        part = spread[:, a * 128 : a * 128 + 128]
        masked = jnp.where(inside, jnp.concatenate([part, part], axis=1), 0.0).astype(BF16)
        wanted = (x_row % 4 == a) & ((x_row // 4 + 1).astype(F32) == i_row)
        volume = volume + dot(wanted.astype(F32).astype(BF16), masked)
    return volume


def first_matrix(conv1_w):
    tap = iota((27, LANES), 0)
    col = iota((27, LANES), 1)
    x_in = iota((TILE, C1, LANES), 2) % TILE
    x_out = iota((TILE, C1, LANES), 0)
    total = jnp.zeros((TILE, C1, LANES), F32)
    for dx in range(3):
        spread = ((tap == 9 * dx + col // TILE) & (col < 9 * TILE)).astype(F32).astype(BF16)
        rows = dot(conv1_w, spread)
        total = jnp.where(x_in == x_out + dx - 1, rows[None], total)
    return total.reshape(TILE * C1, LANES).astype(BF16)


def replicated(weights, count):
    shape = (C1, count * C1)
    return dot(weights, (iota(shape, 0) == iota(shape, 1) % C1).astype(F32).astype(BF16))


def shift_lanes(value, by, roll):
    return roll(value, (-by) % value.shape[-1], value.ndim - 1)


def conv1_columns(volume, roll):
    lane = iota((TILE, LANES), 1)
    y, z = lane // TILE, lane % TILE
    rows = []
    for dy in (-1, 0, 1):
        for dz in (-1, 0, 1):
            moved = volume
            if dy or dz:
                moved = shift_lanes(volume, dy * TILE + dz, roll)
                keep = (y + dy >= 0) & (y + dy < TILE) & (z + dz >= 0) & (z + dz < TILE)
                moved = jnp.where(keep, moved, 0.0)
            rows.append(moved)
    rows.append(jnp.zeros((LANES - 9 * TILE, LANES), F32))
    return jnp.concatenate(rows, axis=0).astype(BF16)


def z_shifted(value, roll):
    z = iota((1, LANES), 1) % TILE
    value = value.astype(BF16)
    before = shift_lanes(value, -1, roll) * jnp.where(z > 0, 1.0, 0.0).astype(BF16)
    after = shift_lanes(value, 1, roll) * jnp.where(z < TILE - 1, 1.0, 0.0).astype(BF16)
    return [before, value, after]


def head_matrix(head_w):
    wide = replicated(head_w, TILE)
    x_in = iota((TILE, TILE * C1), 1) // C1
    x_out = iota((TILE, TILE * C1), 0)
    rows = [jnp.where(x_in == x_out, wide[a : a + 1], 0.0) for a in range(AFF)]
    return jnp.concatenate(rows, axis=0).astype(BF16)


def ramp(position, bit):
    lower = jnp.minimum((TILE - position - 0.5) / OVL, 1.0)
    upper = jnp.minimum((position + 0.5) / OVL, 1.0)
    return jnp.where(bit == 1, upper, lower)


def blend_weights(bits):
    lane = iota((TILE, LANES), 1)
    x = iota((TILE, LANES), 0).astype(F32)
    y = (lane // TILE).astype(F32)
    z = (lane % TILE).astype(F32)
    return ramp(x, bits[0]) * (ramp(y, bits[1]) * ramp(z, bits[2]))


def move_x(low, high, bit, roll):
    row = iota(low.shape, 1)
    from_high = jnp.where(row < OVL, roll(high, 6, 1), 0.0)
    from_low = jnp.where(row >= 8 - OVL, roll(low, 2, 1), 0.0)
    return jnp.where(bit == 0, from_high, from_low)


def move_y(low, high, bit, roll):
    lane = iota(low.shape, 2)
    from_high = jnp.where(lane < OVL * TILE, roll(high, 96, 2), 0.0)
    from_low = jnp.where(lane >= 128 - OVL * TILE, roll(low, 32, 2), 0.0)
    return jnp.where(bit == 0, from_high, from_low)


def pack_z(first, second, bit, roll):
    z = iota(first.shape, 2) % TILE
    head = jnp.where(bit == 0, roll(first, 128 - 10, 2), first)
    tail = jnp.where(bit == 0, roll(second, 128 - 2, 2), roll(second, 8, 2))
    return jnp.where(z < 8, head, tail)


def unpack_z(packed, bit, roll):
    z = iota(packed.shape, 2) % TILE
    keep = jnp.where(bit == 0, z - 10, 5 - z) >= 0
    head = jnp.where(bit == 0, roll(packed, 10, 2), packed)
    tail = jnp.where(bit == 0, roll(packed, 2, 2), roll(packed, 128 - 8, 2))
    return jnp.where(keep, head, 0.0), jnp.where(keep, tail, 0.0)


def kernel(
    em_ref, block_ref, slot_ref, w1_ref, b1_ref, w2_ref, b2_ref, wh_ref, bh_ref,
    out_ref,
    em, block, slot, w1, b1, w2, b2, wh, bh,
    sent, arrived, expand, first, second, heads, hidden, partial,
    x_out, y_out, z_out, e_out, x_in, y_in, z_in, e_in,
    load_sems, route_send, route_recv, swap_send, swap_recv,
    relayed, relay_send, relay_recv, mate_ready, mates_ready, partners_told,
):
    roll = pltpu.roll
    blocks = SIDE * SIDE
    me = lax.axis_index("blocks")
    own = lax.axis_index("octant")
    bits = [own % 2, own // 2 % 2, own // 4]

    def partner(mask):
        total = 0
        for d in range(3):
            total = total + (1 - bits[d] if mask >> d & 1 else bits[d]) * 2**d
        return total

    my, mz = me // SIDE, me % SIDE
    early = mz < HUBS
    twice = mz < 2
    hubs, others = HUBS * SIDE, SIDE - HUBS
    slot_me = jnp.where(early, my * HUBS + mz, hubs + my * others + mz - HUBS)
    group_me = jnp.where(early, SIDE, my)
    pupils = [my * SIDE + SIDE - 1 - mz, my * SIDE + HUBS + mz]
    relay = my * SIDE + jnp.where(mz >= SIDE - HUBS, SIDE - 1 - mz, mz - HUBS)
    lane_me = jnp.where(mz >= SIDE - HUBS, 0, 1)
    spans = (4, 3, 5, 2, 6, 1, 7, 0)
    rows_first = (0, 1, 7, 2, 6, 3, 5, 4)

    def signal(semaphore, target):
        pl.semaphore_signal(
            semaphore, inc=1, device_id={"blocks": target}, device_id_type=MESH
        )

    def unless(condition, visit):
        if condition is None:
            visit()
        else:
            pl.when(jnp.logical_not(condition))(visit)

    def greet(span, z):
        target = (my + span) % SIDE * SIDE + z
        unless(mz == z if span == 0 and z < HUBS else None, lambda: signal(barrier, target))

    def rows(source, target, semaphores, device):
        return pltpu.make_async_remote_copy(
            src_ref=source,
            dst_ref=target,
            send_sem=semaphores[0],
            recv_sem=semaphores[1],
            device_id={"blocks": device},
            device_id_type=MESH,
        )

    def send(y, z):
        target = y * SIDE + z
        if z < HUBS:
            device, place, semaphore = target, arrived, route_recv
        else:
            hub, lane = RELAYS[z]
            device, place = y * SIDE + hub, relayed.at[lane]
            semaphore = relay_recv.at[lane, group_me]
        copy = rows(sent.at[target], place.at[slot_me], (route_send, semaphore), device)
        unless(me == device, copy.start)

    def landed(count, place, semaphores):
        return rows(place.at[pl.ds(0, count)], place.at[pl.ds(0, count)], semaphores, (me + 1) % blocks)

    loads = [
        pltpu.make_async_copy(source, target, load_sems.at[index])
        for index, (source, target) in enumerate(
            [
                (block_ref, block), (slot_ref, slot), (em_ref, em),
                (w1_ref, w1), (b1_ref, b1), (w2_ref, w2), (b2_ref, b2), (wh_ref, wh), (bh_ref, bh),
            ]
        )
    ]
    barrier = pltpu.get_barrier_semaphore()

    def greet_partners(semaphore):
        for mask in range(1, 8):
            pl.semaphore_signal(
                semaphore, inc=1, device_id={"octant": partner(mask)}, device_id_type=MESH
            )


    @pl.when(early)
    def _():
        for span in spans:
            for z in (6, 5, 7, 4, 0, 3, 1, 2):
                greet(span, z)
        greet_partners(barrier)

    for load in loads[:3]:
        load.start()
    for load in loads[:3]:
        load.wait()
    packed = pack_rows(em[0], block[...], slot[...])
    sent[:, 0, :] = packed

    @pl.when(early)
    def _():
        pl.semaphore_wait(barrier, 7 + hubs - 1)
        arrived[slot_me] = sent[me]
        relayed[0, slot_me] = sent[pupils[0]]
        relayed[1, slot_me] = sent[pupils[1]]

    @pl.when(jnp.logical_not(early))
    def _():
        pl.semaphore_wait(barrier, hubs)
        signal(mate_ready.at[lane_me], relay)

    for y in rows_first:
        for z in range(SIDE):
            send(y, z)

    for load in loads[3:]:
        load.start()
    for load in loads[3:]:
        load.wait()
    expand[...] = expander()
    first[...] = first_matrix(w1[...])
    wide = replicated(w2[...].reshape(27 * C1, C1), 2)
    x_inner = iota((C1, 2 * C1), 1) // C1
    for x in range(4):
        for dy in range(3):
            columns = []
            for dz in range(3):
                block_rows = jnp.zeros((C1, 2 * C1), F32)
                for dx in range(3):
                    if 0 <= x + dx - 2 < 2:
                        at = (9 * dx + 3 * dy + dz) * C1
                        block_rows = jnp.where(
                            x_inner == x + dx - 2, wide[at : at + C1], block_rows
                        )
                columns.append(block_rows)
            at = (x * 3 + dy) * C1
            second[at : at + C1, :] = jnp.concatenate(columns, axis=1).astype(BF16)
    heads[...] = head_matrix(wh[...])
    b1_col = column(b1[...])
    b2_col = column(b2[...])
    weights = blend_weights(bits)

    def forward(lane, start, count, awaited, group):
        landed(awaited, relayed.at[lane], (relay_send, relay_recv.at[lane, group])).wait_recv()
        part = pl.ds(start, count)
        rows(
            relayed.at[lane, part], arrived.at[part], (relay_send, route_recv), pupils[lane]
        ).start()

    def begin(lane):
        pl.semaphore_wait(mate_ready.at[lane], 1)
        greet_partners(mates_ready.at[lane])
        forward(lane, 0, hubs, hubs - 1, SIDE)

    def finish(lane):
        pl.semaphore_wait(mates_ready.at[lane], 7)
        signal(partners_told, pupils[lane])

    def also(visit, *numbers):
        pl.when(twice)(functools.partial(visit, 1, *numbers))

    @pl.when(early)
    def _():
        also(begin)
        begin(0)
        for y in rows_first:
            group = (hubs + y * others, others, others, y)
            forward(0, *group)
            also(forward, *group)
        landed(blocks - 1, arrived, (route_send, route_recv)).wait_recv()

    @pl.when(jnp.logical_not(early))
    def _():
        landed(blocks, arrived, (route_send, route_recv)).wait_recv()

    volume = unpack_volume(arrived[:, 0, :], expand[...])
    @pl.when(early)
    def _():
        finish(0)
        also(finish)

    one = dot(first[...], conv1_columns(volume, roll)).reshape(TILE, C1, LANES)
    one = jnp.maximum(one + b1_col[None], 0.0).reshape(TILE * C1, LANES)
    for dz, part in enumerate(z_shifted(one, roll)):
        hidden[:, dz] = part.reshape(8, 2 * C1, LANES)
    held = None
    for group in range(8):
        sums = dot(second[...], hidden[group].reshape(6 * C1, LANES)).reshape(4, 3, C1, LANES)
        if held is None:
            partial[0] = sums[1]
        else:
            partial[2 * group - 1] = held[0] + sums[0]
            partial[2 * group] = held[1] + sums[1]
        held = sums[2:]
    partial[TILE - 1] = held[0]
    y = iota((1, 1, LANES), 2) // TILE
    total = partial[:, 1]
    total = total + jnp.where(y > 0, shift_lanes(partial[:, 0].reshape(512, LANES), -TILE, roll).reshape(TILE, C1, LANES), 0.0)
    total = total + jnp.where(y < TILE - 1, shift_lanes(partial[:, 2].reshape(512, LANES), TILE, roll).reshape(TILE, C1, LANES), 0.0)
    two = jnp.maximum(total + b2_col[None], 0.0).reshape(TILE * C1, LANES).astype(BF16)
    logits = dot(heads[...], two)
    pieces = []
    for a in range(AFF):
        pieces.append(jax.nn.sigmoid(logits[a * TILE : a * TILE + TILE] + bh[:, a : a + 1]) * weights)
    blended = jnp.stack(pieces, axis=0)

    tile = [[blended[:, 8 * hx : 8 * hx + 8, 128 * hy : 128 * hy + 128] for hy in range(2)] for hx in range(2)]
    @pl.when(jnp.logical_not(early))
    def _():
        pl.semaphore_wait(partners_told, 1)

    swaps = {}

    def swap(mask, source, target):
        swaps[mask] = pltpu.make_async_remote_copy(
            src_ref=source,
            dst_ref=target,
            send_sem=swap_send.at[mask - 1],
            recv_sem=swap_recv.at[mask - 1],
            device_id={"octant": partner(mask)},
            device_id_type=MESH,
        )
        swaps[mask].start()

    z_out[:, :8] = pack_z(tile[0][0], tile[0][1], bits[2], roll)
    z_out[:, 8:] = pack_z(tile[1][0], tile[1][1], bits[2], roll)
    swap(4, z_out, z_in)
    at_x = [move_x(tile[0][hy], tile[1][hy], bits[0], roll) for hy in range(2)]
    e_out[1] = pack_z(at_x[0], at_x[1], bits[2], roll)
    swap(5, e_out.at[1], e_in.at[1])
    at_y = [move_y(tile[hx][0], tile[hx][1], bits[1], roll) for hx in range(2)]
    y_out[:, :8] = at_y[0]
    y_out[:, 8:] = at_y[1]
    swap(2, y_out, y_in)
    e_out[2] = pack_z(at_y[0], at_y[1], bits[2], roll)
    swap(6, e_out.at[2], e_in.at[2])
    at_xy = move_y(at_x[0], at_x[1], bits[1], roll)
    e_out[0] = at_xy
    swap(3, e_out.at[0], e_in.at[0])
    e_out[3] = pack_z(at_xy, at_xy, bits[2], roll)
    swap(7, e_out.at[3], e_in.at[3])
    x_out[:, :, :128] = at_x[0]
    x_out[:, :, 128:] = at_x[1]
    swap(1, x_out, x_in)

    plane = [[tile[hx][hy] for hy in range(2)] for hx in range(2)]

    def add(hx, hy, value):
        plane[hx][hy] = plane[hx][hy] + value

    def is_half(bit, half, value):
        return jnp.where(bit == 1 - half, value, 0.0)

    swaps[1].wait_recv()
    for hy in range(2):
        value = x_in[:, :, 128 * hy : 128 * hy + 128]
        for hx in range(2):
            add(hx, hy, is_half(bits[0], hx, value))
    swaps[2].wait_recv()
    for hx in range(2):
        value = y_in[:, 8 * hx : 8 * hx + 8]
        for hy in range(2):
            add(hx, hy, is_half(bits[1], hy, value))
    swaps[3].wait_recv()
    swaps[7].wait_recv()
    corner = e_in[0] + unpack_z(e_in[3], bits[2], roll)[0]
    for hx in range(2):
        for hy in range(2):
            add(hx, hy, is_half(bits[0], hx, is_half(bits[1], hy, corner)))
    swaps[6].wait_recv()
    parts = unpack_z(e_in[2], bits[2], roll)
    for hx in range(2):
        for hy in range(2):
            add(hx, hy, is_half(bits[1], hy, parts[hx]))
    swaps[5].wait_recv()
    parts = unpack_z(e_in[1], bits[2], roll)
    for hx in range(2):
        for hy in range(2):
            add(hx, hy, is_half(bits[0], hx, parts[hy]))
    swaps[4].wait_recv()
    for hx in range(2):
        parts = unpack_z(z_in[:, 8 * hx : 8 * hx + 8], bits[2], roll)
        for hy in range(2):
            add(hx, hy, parts[hy])
    for hx in range(2):
        for hy in range(2):
            out_ref[:, pl.ds(TILE * hx + hy, 8, stride=2), :] = plane[hx][hy]
    for copy in swaps.values():
        copy.wait_send()

    @pl.when(early)
    def _():
        landed(blocks - 3, arrived, (route_send, route_recv)).wait_send()
        landed(blocks, arrived, (relay_send, route_recv)).wait_send()

    @pl.when(twice)
    def _():
        landed(blocks, arrived, (relay_send, route_recv)).wait_send()

    @pl.when(mz == HUBS - 1)
    def _():
        landed(1, arrived, (route_send, route_recv)).wait_send()

    @pl.when(jnp.logical_not(early))
    def _():
        landed(blocks, arrived, (route_send, route_recv)).wait_send()


def shards(em_store, route_block, route_slot, conv1_w, conv1_b, conv2_w, conv2_b, head_w, head_b):
    operands = (
        em_store, route_block, route_slot, conv1_w, conv1_b.reshape(1, C1), conv2_w,
        conv2_b.reshape(1, C1), head_w, head_b.reshape(1, AFF),
    )
    operands = tuple(pltpu.with_memory_space_constraint(value, pltpu.HBM) for value in operands)
    vmem = pltpu.VMEM
    result = pl.pallas_call(
        kernel,
        out_shape=jax.ShapeDtypeStruct((AFF, 2 * TILE, 128), F32),
        in_specs=[pl.BlockSpec(memory_space=pltpu.HBM)] * len(operands),
        out_specs=pl.BlockSpec(memory_space=vmem),
        scratch_shapes=[vmem(value.shape, value.dtype) for value in operands]
        + [
            vmem((64, 1, 256), F32),
            vmem((64, 1, 256), F32),
            vmem((128, 4 * 128), BF16),
            vmem((TILE * C1, LANES), BF16),
            vmem((12 * C1, 6 * C1), BF16),
            vmem((AFF * TILE, TILE * C1), BF16),
            vmem((8, 3, 2 * C1, LANES), BF16),
            vmem((TILE, 3, C1, LANES), F32),
        ]
        + [
            vmem((AFF, 8, 256), F32),
            vmem((AFF, 16, 128), F32),
            vmem((AFF, 16, 128), F32),
            vmem((4, AFF, 8, 128), F32),
        ]
        * 2
        + [
            pltpu.SemaphoreType.DMA((len(operands),)),
            pltpu.SemaphoreType.DMA,
            pltpu.SemaphoreType.DMA,
            pltpu.SemaphoreType.DMA((7,)),
            pltpu.SemaphoreType.DMA((7,)),
        ]
        + [
            vmem((2, 64, 1, 256), F32),
            pltpu.SemaphoreType.DMA,
            pltpu.SemaphoreType.DMA((2, SIDE + 1)),
            pltpu.SemaphoreType.REGULAR((2,)),
            pltpu.SemaphoreType.REGULAR((2,)),
            pltpu.SemaphoreType.REGULAR,
        ],
        compiler_params=pltpu.CompilerParams(
            collective_id=0, has_side_effects=True, vmem_limit_bytes=32 * 1024 * 1024
        ),
    )(*operands)
    return result.reshape(1, 1, AFF, TILE * LANES)


def solution(mesh):
    in_specs = (P("octant", "blocks", None), P("octant", "blocks"), P("octant", "blocks")) + (P(),) * 6
    out_specs = P("octant", "blocks", None, None)
    return jax.shard_map(shards, mesh=mesh, in_specs=in_specs, out_specs=out_specs, check_vma=False)
```

```python
import functools

import jax
import jax.numpy as jnp
from jax import lax
from jax.experimental import pallas as pl
from jax.experimental.pallas import tpu as pltpu
from jax.sharding import PartitionSpec as P

TILE = 16
OVL = 6
LANES = TILE * TILE
C1 = 32
SIDE = 8
HUBS = 3
RELAYS = {7: (0, 0), 6: (1, 0), 5: (2, 0), 4: (1, 1), 3: (0, 1)}
AFF = 3
MESH = pl.DeviceIdType.MESH
F32 = jnp.float32
BF16 = jnp.bfloat16


def iota(shape, dim):
    return lax.broadcasted_iota(jnp.int32, shape, dim)


def dot(a, b):
    return jnp.dot(a, b, preferred_element_type=F32)


def column(row):
    n = row.shape[1]
    return jnp.sum(jnp.where(iota((n, n), 0) == iota((n, n), 1), row, 0.0), axis=1, keepdims=True)


def pack_rows(em, targets, slots):
    n = em.shape[0]
    target_row = targets.astype(F32)
    target_col = column(target_row)
    earlier = (target_col == target_row) & (iota((n, n), 0) < iota((n, n), 1))
    rank_row = jnp.sum(jnp.where(earlier, 1.0, 0.0), axis=0, keepdims=True)
    slot_row = slots
    i_col = column((slot_row // 16 + 1).astype(F32))
    jk_col = column((slot_row % 16).astype(F32))
    lane = iota((n, 64), 1)
    labels = jnp.where(lane == 0, i_col, jnp.where(lane == 1, jk_col, 0.0)).astype(BF16)
    wide = jnp.concatenate([em, labels], axis=1)
    row = iota((128, n), 0)
    here = ((row % 64).astype(F32) == target_row) & ((row // 64).astype(F32) == rank_row)
    return dot(here.astype(F32).astype(BF16), wide)


def expander():
    row = iota((128, 4 * 128), 0)
    col = iota((128, 4 * 128), 1)
    wanted = (col // 128) * 16 + (col // 16 % 4) * 4 + col % 4
    return (row == wanted).astype(F32).astype(BF16)


def unpack_volume(arrived, expand):
    rows = jnp.concatenate([arrived[:, :128], arrived[:, 128:]], axis=0)
    i_col = rows[:, 64:65]
    jk_col = rows[:, 65:66]
    eye = iota((128, 128), 0) == iota((128, 128), 1)
    i_row = jnp.sum(jnp.where(eye, i_col, 0.0), axis=0, keepdims=True)
    lane = iota((128, LANES), 1)
    lane_jk = (lane // 64 * 4 + lane // 4 % 4).astype(F32)
    inside = lane_jk == jk_col
    spread = dot(rows.astype(BF16), expand)
    x_row = iota((TILE, 128), 0)
    volume = jnp.zeros((TILE, LANES), F32)
    for a in range(4):
        part = spread[:, a * 128 : a * 128 + 128]
        masked = jnp.where(inside, jnp.concatenate([part, part], axis=1), 0.0).astype(BF16)
        wanted = (x_row % 4 == a) & ((x_row // 4 + 1).astype(F32) == i_row)
        volume = volume + dot(wanted.astype(F32).astype(BF16), masked)
    return volume


def first_matrix(conv1_w):
    tap = iota((27, LANES), 0)
    col = iota((27, LANES), 1)
    x_in = iota((TILE, C1, LANES), 2) % TILE
    x_out = iota((TILE, C1, LANES), 0)
    total = jnp.zeros((TILE, C1, LANES), F32)
    for dx in range(3):
        spread = ((tap == 9 * dx + col // TILE) & (col < 9 * TILE)).astype(F32).astype(BF16)
        rows = dot(conv1_w, spread)
        total = jnp.where(x_in == x_out + dx - 1, rows[None], total)
    return total.reshape(TILE * C1, LANES).astype(BF16)


def replicated(weights, count):
    shape = (C1, count * C1)
    return dot(weights, (iota(shape, 0) == iota(shape, 1) % C1).astype(F32).astype(BF16))


def shift_lanes(value, by, roll):
    return roll(value, (-by) % value.shape[-1], value.ndim - 1)


def conv1_columns(volume, roll):
    lane = iota((TILE, LANES), 1)
    y, z = lane // TILE, lane % TILE
    rows = []
    for dy in (-1, 0, 1):
        for dz in (-1, 0, 1):
            moved = volume
            if dy or dz:
                moved = shift_lanes(volume, dy * TILE + dz, roll)
                keep = (y + dy >= 0) & (y + dy < TILE) & (z + dz >= 0) & (z + dz < TILE)
                moved = jnp.where(keep, moved, 0.0)
            rows.append(moved)
    rows.append(jnp.zeros((LANES - 9 * TILE, LANES), F32))
    return jnp.concatenate(rows, axis=0).astype(BF16)


def z_shifted(value, roll):
    z = iota((1, LANES), 1) % TILE
    value = value.astype(BF16)
    before = shift_lanes(value, -1, roll) * jnp.where(z > 0, 1.0, 0.0).astype(BF16)
    after = shift_lanes(value, 1, roll) * jnp.where(z < TILE - 1, 1.0, 0.0).astype(BF16)
    return [before, value, after]


def head_matrix(head_w):
    wide = replicated(head_w, TILE)
    x_in = iota((TILE, TILE * C1), 1) // C1
    x_out = iota((TILE, TILE * C1), 0)
    rows = [jnp.where(x_in == x_out, wide[a : a + 1], 0.0) for a in range(AFF)]
    return jnp.concatenate(rows, axis=0).astype(BF16)


def ramp(position, bit):
    lower = jnp.minimum((TILE - position - 0.5) / OVL, 1.0)
    upper = jnp.minimum((position + 0.5) / OVL, 1.0)
    return jnp.where(bit == 1, upper, lower)


def blend_weights(bits):
    lane = iota((TILE, LANES), 1)
    x = iota((TILE, LANES), 0).astype(F32)
    y = (lane // TILE).astype(F32)
    z = (lane % TILE).astype(F32)
    return ramp(x, bits[0]) * (ramp(y, bits[1]) * ramp(z, bits[2]))


def move_x(low, high, bit, roll):
    row = iota(low.shape, 1)
    from_high = jnp.where(row < OVL, roll(high, 6, 1), 0.0)
    from_low = jnp.where(row >= 8 - OVL, roll(low, 2, 1), 0.0)
    return jnp.where(bit == 0, from_high, from_low)


def move_y(low, high, bit, roll):
    lane = iota(low.shape, 2)
    from_high = jnp.where(lane < OVL * TILE, roll(high, 96, 2), 0.0)
    from_low = jnp.where(lane >= 128 - OVL * TILE, roll(low, 32, 2), 0.0)
    return jnp.where(bit == 0, from_high, from_low)


def pack_z(first, second, bit, roll):
    z = iota(first.shape, 2) % TILE
    head = jnp.where(bit == 0, roll(first, 128 - 10, 2), first)
    tail = jnp.where(bit == 0, roll(second, 128 - 2, 2), roll(second, 8, 2))
    return jnp.where(z < 8, head, tail)


def unpack_z(packed, bit, roll):
    z = iota(packed.shape, 2) % TILE
    keep = jnp.where(bit == 0, z - 10, 5 - z) >= 0
    head = jnp.where(bit == 0, roll(packed, 10, 2), packed)
    tail = jnp.where(bit == 0, roll(packed, 2, 2), roll(packed, 128 - 8, 2))
    return jnp.where(keep, head, 0.0), jnp.where(keep, tail, 0.0)


def kernel(
    em_ref, block_ref, slot_ref, w1_ref, b1_ref, w2_ref, b2_ref, wh_ref, bh_ref,
    out_ref,
    em, block, slot, w1, b1, w2, b2, wh, bh,
    sent, arrived, expand, first, second, heads, hidden, two,
    x_out, y_out, z_out, e_out, x_in, y_in, z_in, e_in,
    load_sems, route_send, route_recv, swap_send, swap_recv,
    relayed, relay_send, relay_recv, mate_ready, mates_ready, partners_told,
):
    roll = pltpu.roll
    blocks = SIDE * SIDE
    me = lax.axis_index("blocks")
    own = lax.axis_index("octant")
    bits = [own % 2, own // 2 % 2, own // 4]

    def partner(mask):
        total = 0
        for d in range(3):
            total = total + (1 - bits[d] if mask >> d & 1 else bits[d]) * 2**d
        return total

    my, mz = me // SIDE, me % SIDE
    early = mz < HUBS
    twice = mz < 2
    hubs, others = HUBS * SIDE, SIDE - HUBS
    slot_me = jnp.where(early, my * HUBS + mz, hubs + my * others + mz - HUBS)
    group_me = jnp.where(early, SIDE, my)
    pupils = [my * SIDE + SIDE - 1 - mz, my * SIDE + HUBS + mz]
    relay = my * SIDE + jnp.where(mz >= SIDE - HUBS, SIDE - 1 - mz, mz - HUBS)
    lane_me = jnp.where(mz >= SIDE - HUBS, 0, 1)
    spans = (4, 3, 5, 2, 6, 1, 7, 0)
    rows_first = (0, 1, 7, 2, 6, 3, 5, 4)

    def signal(semaphore, target):
        pl.semaphore_signal(
            semaphore, inc=1, device_id={"blocks": target}, device_id_type=MESH
        )

    def unless(condition, visit):
        if condition is None:
            visit()
        else:
            pl.when(jnp.logical_not(condition))(visit)

    def greet(span, z):
        target = (my + span) % SIDE * SIDE + z
        unless(mz == z if span == 0 and z < HUBS else None, lambda: signal(barrier, target))

    def rows(source, target, semaphores, device):
        return pltpu.make_async_remote_copy(
            src_ref=source,
            dst_ref=target,
            send_sem=semaphores[0],
            recv_sem=semaphores[1],
            device_id={"blocks": device},
            device_id_type=MESH,
        )

    def send(y, z):
        target = y * SIDE + z
        if z < HUBS:
            device, place, semaphore = target, arrived, route_recv
        else:
            hub, lane = RELAYS[z]
            device, place = y * SIDE + hub, relayed.at[lane]
            semaphore = relay_recv.at[lane, group_me]
        copy = rows(sent.at[target], place.at[slot_me], (route_send, semaphore), device)
        unless(me == device, copy.start)

    def landed(count, place, semaphores):
        return rows(place.at[pl.ds(0, count)], place.at[pl.ds(0, count)], semaphores, (me + 1) % blocks)

    loads = [
        pltpu.make_async_copy(source, target, load_sems.at[index])
        for index, (source, target) in enumerate(
            [
                (block_ref, block), (slot_ref, slot), (em_ref, em),
                (w1_ref, w1), (b1_ref, b1), (w2_ref, w2), (b2_ref, b2), (wh_ref, wh), (bh_ref, bh),
            ]
        )
    ]
    barrier = pltpu.get_barrier_semaphore()

    def greet_partners(semaphore):
        for mask in range(1, 8):
            pl.semaphore_signal(
                semaphore, inc=1, device_id={"octant": partner(mask)}, device_id_type=MESH
            )


    @pl.when(early)
    def _():
        for span in spans:
            for z in (6, 5, 7, 4, 0, 3, 1, 2):
                greet(span, z)
        greet_partners(barrier)

    for load in loads[:3]:
        load.start()
    for load in loads[:3]:
        load.wait()
    packed = pack_rows(em[0], block[...], slot[...])
    sent[:, 0, :128] = packed[:64]
    sent[:, 0, 128:] = packed[64:]

    @pl.when(early)
    def _():
        pl.semaphore_wait(barrier, 7 + hubs - 1)
        arrived[slot_me] = sent[me]
        relayed[0, slot_me] = sent[pupils[0]]
        relayed[1, slot_me] = sent[pupils[1]]

    @pl.when(jnp.logical_not(early))
    def _():
        pl.semaphore_wait(barrier, hubs)
        signal(mate_ready.at[lane_me], relay)

    for y in rows_first:
        for z in range(SIDE):
            send(y, z)

    for load in loads[3:]:
        load.start()
    for load in loads[3:]:
        load.wait()
    expand[...] = expander()
    first[...] = first_matrix(w1[...])
    wide = replicated(w2[...].reshape(27 * C1, C1), 2)
    x_inner = iota((C1, 2 * C1), 1) // C1
    for x in range(4):
        for dy in range(3):
            columns = []
            for dz in range(3):
                block_rows = jnp.zeros((C1, 2 * C1), F32)
                for dx in range(3):
                    if 0 <= x + dx - 2 < 2:
                        at = (9 * dx + 3 * dy + dz) * C1
                        block_rows = jnp.where(
                            x_inner == x + dx - 2, wide[at : at + C1], block_rows
                        )
                columns.append(block_rows)
            at = (x * 3 + dy) * C1
            second[at : at + C1, :] = jnp.concatenate(columns, axis=1).astype(BF16)
    heads[...] = head_matrix(wh[...])
    b1_col = column(b1[...])
    b2_col = column(b2[...])
    weights = blend_weights(bits)

    def forward(lane, start, count, awaited, group):
        landed(awaited, relayed.at[lane], (relay_send, relay_recv.at[lane, group])).wait_recv()
        part = pl.ds(start, count)
        rows(
            relayed.at[lane, part], arrived.at[part], (relay_send, route_recv), pupils[lane]
        ).start()

    def begin(lane):
        pl.semaphore_wait(mate_ready.at[lane], 1)
        greet_partners(mates_ready.at[lane])
        forward(lane, 0, hubs, hubs - 1, SIDE)

    def finish(lane):
        pl.semaphore_wait(mates_ready.at[lane], 7)
        signal(partners_told, pupils[lane])

    def also(visit, *numbers):
        pl.when(twice)(functools.partial(visit, 1, *numbers))

    @pl.when(early)
    def _():
        also(begin)
        begin(0)
        for y in rows_first:
            group = (hubs + y * others, others, others, y)
            forward(0, *group)
            also(forward, *group)
        landed(blocks - 1, arrived, (route_send, route_recv)).wait_recv()

    @pl.when(jnp.logical_not(early))
    def _():
        landed(blocks, arrived, (route_send, route_recv)).wait_recv()

    volume = unpack_volume(arrived[:, 0, :], expand[...])
    @pl.when(early)
    def _():
        finish(0)
        also(finish)

    one = dot(first[...], conv1_columns(volume, roll)).reshape(TILE, C1, LANES)
    one = jnp.maximum(one + b1_col[None], 0.0).reshape(TILE * C1, LANES)
    for dz, part in enumerate(z_shifted(one, roll)):
        hidden[:, dz] = part.reshape(8, 2 * C1, LANES)
    y = iota((1, LANES), 1) // TILE

    def complete(x, sums):
        total = sums[1]
        total = total + jnp.where(y > 0, shift_lanes(sums[0], -TILE, roll), 0.0)
        total = total + jnp.where(y < TILE - 1, shift_lanes(sums[2], TILE, roll), 0.0)
        two[x * C1 : x * C1 + C1, :] = jnp.maximum(total + b2_col, 0.0).astype(BF16)

    held = None
    for group in range(8):
        sums = dot(second[...], hidden[group].reshape(6 * C1, LANES)).reshape(4, 3, C1, LANES)
        if held is None:
            complete(0, sums[1])
        else:
            complete(2 * group - 1, held[0] + sums[0])
            complete(2 * group, held[1] + sums[1])
        held = sums[2:]
    complete(TILE - 1, held[0])
    logits = dot(heads[...], two[...])
    pieces = []
    for a in range(AFF):
        pieces.append(jax.nn.sigmoid(logits[a * TILE : a * TILE + TILE] + bh[:, a : a + 1]) * weights)
    blended = jnp.stack(pieces, axis=0)

    tile = [[blended[:, 8 * hx : 8 * hx + 8, 128 * hy : 128 * hy + 128] for hy in range(2)] for hx in range(2)]
    @pl.when(jnp.logical_not(early))
    def _():
        pl.semaphore_wait(partners_told, 1)

    swaps = {}

    def swap(mask, source, target):
        swaps[mask] = pltpu.make_async_remote_copy(
            src_ref=source,
            dst_ref=target,
            send_sem=swap_send.at[mask - 1],
            recv_sem=swap_recv.at[mask - 1],
            device_id={"octant": partner(mask)},
            device_id_type=MESH,
        )
        swaps[mask].start()

    z_out[:, :8] = pack_z(tile[0][0], tile[0][1], bits[2], roll)
    z_out[:, 8:] = pack_z(tile[1][0], tile[1][1], bits[2], roll)
    swap(4, z_out, z_in)
    at_x = [move_x(tile[0][hy], tile[1][hy], bits[0], roll) for hy in range(2)]
    e_out[1] = pack_z(at_x[0], at_x[1], bits[2], roll)
    swap(5, e_out.at[1], e_in.at[1])
    at_y = [move_y(tile[hx][0], tile[hx][1], bits[1], roll) for hx in range(2)]
    y_out[:, :8] = at_y[0]
    y_out[:, 8:] = at_y[1]
    swap(2, y_out, y_in)
    e_out[2] = pack_z(at_y[0], at_y[1], bits[2], roll)
    swap(6, e_out.at[2], e_in.at[2])
    at_xy = move_y(at_x[0], at_x[1], bits[1], roll)
    e_out[0] = at_xy
    swap(3, e_out.at[0], e_in.at[0])
    e_out[3] = pack_z(at_xy, at_xy, bits[2], roll)
    swap(7, e_out.at[3], e_in.at[3])
    x_out[:, :, :128] = at_x[0]
    x_out[:, :, 128:] = at_x[1]
    swap(1, x_out, x_in)

    plane = [[tile[hx][hy] for hy in range(2)] for hx in range(2)]

    def add(hx, hy, value):
        plane[hx][hy] = plane[hx][hy] + value

    def is_half(bit, half, value):
        return jnp.where(bit == 1 - half, value, 0.0)

    swaps[1].wait_recv()
    for hy in range(2):
        value = x_in[:, :, 128 * hy : 128 * hy + 128]
        for hx in range(2):
            add(hx, hy, is_half(bits[0], hx, value))
    swaps[2].wait_recv()
    for hx in range(2):
        value = y_in[:, 8 * hx : 8 * hx + 8]
        for hy in range(2):
            add(hx, hy, is_half(bits[1], hy, value))
    swaps[3].wait_recv()
    swaps[7].wait_recv()
    corner = e_in[0] + unpack_z(e_in[3], bits[2], roll)[0]
    for hx in range(2):
        for hy in range(2):
            add(hx, hy, is_half(bits[0], hx, is_half(bits[1], hy, corner)))
    swaps[6].wait_recv()
    parts = unpack_z(e_in[2], bits[2], roll)
    for hx in range(2):
        for hy in range(2):
            add(hx, hy, is_half(bits[1], hy, parts[hx]))
    swaps[5].wait_recv()
    parts = unpack_z(e_in[1], bits[2], roll)
    for hx in range(2):
        for hy in range(2):
            add(hx, hy, is_half(bits[0], hx, parts[hy]))
    swaps[4].wait_recv()
    for hx in range(2):
        parts = unpack_z(z_in[:, 8 * hx : 8 * hx + 8], bits[2], roll)
        for hy in range(2):
            add(hx, hy, parts[hy])
    for hx in range(2):
        for hy in range(2):
            out_ref[:, pl.ds(TILE * hx + hy, 8, stride=2), :] = plane[hx][hy]
    for copy in swaps.values():
        copy.wait_send()

    @pl.when(early)
    def _():
        landed(blocks - 3, arrived, (route_send, route_recv)).wait_send()
        landed(blocks, arrived, (relay_send, route_recv)).wait_send()

    @pl.when(twice)
    def _():
        landed(blocks, arrived, (relay_send, route_recv)).wait_send()

    @pl.when(mz == HUBS - 1)
    def _():
        landed(1, arrived, (route_send, route_recv)).wait_send()

    @pl.when(jnp.logical_not(early))
    def _():
        landed(blocks, arrived, (route_send, route_recv)).wait_send()


def shards(em_store, route_block, route_slot, conv1_w, conv1_b, conv2_w, conv2_b, head_w, head_b):
    operands = (
        em_store, route_block, route_slot, conv1_w, conv1_b.reshape(1, C1), conv2_w,
        conv2_b.reshape(1, C1), head_w, head_b.reshape(1, AFF),
    )
    operands = tuple(pltpu.with_memory_space_constraint(value, pltpu.HBM) for value in operands)
    vmem = pltpu.VMEM
    result = pl.pallas_call(
        kernel,
        out_shape=jax.ShapeDtypeStruct((AFF, 2 * TILE, 128), F32),
        in_specs=[pl.BlockSpec(memory_space=pltpu.HBM)] * len(operands),
        out_specs=pl.BlockSpec(memory_space=vmem),
        scratch_shapes=[vmem(value.shape, value.dtype) for value in operands]
        + [
            vmem((64, 1, 256), F32),
            vmem((64, 1, 256), F32),
            vmem((128, 4 * 128), BF16),
            vmem((TILE * C1, LANES), BF16),
            vmem((12 * C1, 6 * C1), BF16),
            vmem((AFF * TILE, TILE * C1), BF16),
            vmem((8, 3, 2 * C1, LANES), BF16),
            vmem((TILE * C1, LANES), BF16),
        ]
        + [
            vmem((AFF, 8, 256), F32),
            vmem((AFF, 16, 128), F32),
            vmem((AFF, 16, 128), F32),
            vmem((4, AFF, 8, 128), F32),
        ]
        * 2
        + [
            pltpu.SemaphoreType.DMA((len(operands),)),
            pltpu.SemaphoreType.DMA,
            pltpu.SemaphoreType.DMA,
            pltpu.SemaphoreType.DMA((7,)),
            pltpu.SemaphoreType.DMA((7,)),
        ]
        + [
            vmem((2, 64, 1, 256), F32),
            pltpu.SemaphoreType.DMA,
            pltpu.SemaphoreType.DMA((2, SIDE + 1)),
            pltpu.SemaphoreType.REGULAR((2,)),
            pltpu.SemaphoreType.REGULAR((2,)),
            pltpu.SemaphoreType.REGULAR,
        ],
        compiler_params=pltpu.CompilerParams(
            collective_id=0, has_side_effects=True, vmem_limit_bytes=32 * 1024 * 1024
        ),
    )(*operands)
    return result.reshape(1, 1, AFF, TILE * LANES)


def solution(mesh):
    in_specs = (P("octant", "blocks", None), P("octant", "blocks"), P("octant", "blocks")) + (P(),) * 6
    out_specs = P("octant", "blocks", None, None)
    return jax.shard_map(shards, mesh=mesh, in_specs=in_specs, out_specs=out_specs, check_vma=False)
```

```python
import functools

import jax
import jax.numpy as jnp
from jax import lax
from jax.experimental import pallas as pl
from jax.experimental.pallas import tpu as pltpu
from jax.sharding import PartitionSpec as P

TILE = 16
OVL = 6
LANES = TILE * TILE
C1 = 32
SIDE = 8
HUBS = 3
RELAYS = {7: (0, 0), 6: (1, 0), 5: (2, 0), 4: (1, 1), 3: (0, 1)}
AFF = 3
MESH = pl.DeviceIdType.MESH
F32 = jnp.float32
BF16 = jnp.bfloat16


def iota(shape, dim):
    return lax.broadcasted_iota(jnp.int32, shape, dim)


def dot(a, b):
    return jnp.dot(a, b, preferred_element_type=F32)


def column(row):
    n = row.shape[1]
    return jnp.sum(jnp.where(iota((n, n), 0) == iota((n, n), 1), row, 0.0), axis=1, keepdims=True)


def pack_rows(em, targets, slots):
    n = em.shape[0]
    target_row = targets.astype(F32)
    target_col = column(target_row)
    earlier = (target_col == target_row) & (iota((n, n), 0) < iota((n, n), 1))
    rank_row = jnp.sum(jnp.where(earlier, 1.0, 0.0), axis=0, keepdims=True)
    slot_row = slots
    i_col = column((slot_row // 16 + 1).astype(F32))
    jk_col = column((slot_row % 16).astype(F32))
    lane = iota((n, 64), 1)
    labels = jnp.where(lane == 0, i_col, jnp.where(lane == 1, jk_col, 0.0)).astype(BF16)
    wide = jnp.concatenate([em, labels], axis=1)
    row = iota((128, n), 0)
    here = ((row % 64).astype(F32) == target_row) & ((row // 64).astype(F32) == rank_row)
    return dot(here.astype(F32).astype(BF16), wide)


def expander():
    row = iota((128, 4 * 128), 0)
    col = iota((128, 4 * 128), 1)
    wanted = (col // 128) * 16 + (col // 16 % 4) * 4 + col % 4
    return (row == wanted).astype(F32).astype(BF16)


def unpack_volume(arrived, expand):
    rows = jnp.concatenate([arrived[:, :128], arrived[:, 128:]], axis=0)
    i_col = rows[:, 64:65]
    jk_col = rows[:, 65:66]
    eye = iota((128, 128), 0) == iota((128, 128), 1)
    i_row = jnp.sum(jnp.where(eye, i_col, 0.0), axis=0, keepdims=True)
    lane = iota((128, LANES), 1)
    lane_jk = (lane // 64 * 4 + lane // 4 % 4).astype(F32)
    inside = lane_jk == jk_col
    spread = dot(rows.astype(BF16), expand)
    x_row = iota((TILE, 128), 0)
    volume = jnp.zeros((TILE, LANES), F32)
    for a in range(4):
        part = spread[:, a * 128 : a * 128 + 128]
        masked = jnp.where(inside, jnp.concatenate([part, part], axis=1), 0.0).astype(BF16)
        wanted = (x_row % 4 == a) & ((x_row // 4 + 1).astype(F32) == i_row)
        volume = volume + dot(wanted.astype(F32).astype(BF16), masked)
    return volume


def first_matrix(conv1_w):
    tap = iota((27, LANES), 0)
    col = iota((27, LANES), 1)
    x_in = iota((TILE, C1, LANES), 2) % TILE
    x_out = iota((TILE, C1, LANES), 0)
    total = jnp.zeros((TILE, C1, LANES), F32)
    for dx in range(3):
        spread = ((tap == 9 * dx + col // TILE) & (col < 9 * TILE)).astype(F32).astype(BF16)
        rows = dot(conv1_w, spread)
        total = jnp.where(x_in == x_out + dx - 1, rows[None], total)
    return total.reshape(TILE * C1, LANES).astype(BF16)


def replicated(weights, count):
    shape = (C1, count * C1)
    return dot(weights, (iota(shape, 0) == iota(shape, 1) % C1).astype(F32).astype(BF16))


def shift_lanes(value, by, roll):
    return roll(value, (-by) % value.shape[-1], value.ndim - 1)


def conv1_columns(volume, roll):
    lane = iota((TILE, LANES), 1)
    y, z = lane // TILE, lane % TILE
    rows = []
    for dy in (-1, 0, 1):
        for dz in (-1, 0, 1):
            moved = volume
            if dy or dz:
                moved = shift_lanes(volume, dy * TILE + dz, roll)
                keep = (y + dy >= 0) & (y + dy < TILE) & (z + dz >= 0) & (z + dz < TILE)
                moved = jnp.where(keep, moved, 0.0)
            rows.append(moved)
    rows.append(jnp.zeros((LANES - 9 * TILE, LANES), F32))
    return jnp.concatenate(rows, axis=0).astype(BF16)


def z_shifted(value, roll):
    z = iota((1, LANES), 1) % TILE
    value = value.astype(BF16)
    before = shift_lanes(value, -1, roll) * jnp.where(z > 0, 1.0, 0.0).astype(BF16)
    after = shift_lanes(value, 1, roll) * jnp.where(z < TILE - 1, 1.0, 0.0).astype(BF16)
    return [before, value, after]


def head_matrix(head_w):
    wide = replicated(head_w, TILE)
    x_in = iota((TILE, TILE * C1), 1) // C1
    x_out = iota((TILE, TILE * C1), 0)
    rows = [jnp.where(x_in == x_out, wide[a : a + 1], 0.0) for a in range(AFF)]
    return jnp.concatenate(rows, axis=0).astype(BF16)


def ramp(position, bit):
    lower = jnp.minimum((TILE - position - 0.5) / OVL, 1.0)
    upper = jnp.minimum((position + 0.5) / OVL, 1.0)
    return jnp.where(bit == 1, upper, lower)


def blend_weights(bits):
    lane = iota((TILE, LANES), 1)
    x = iota((TILE, LANES), 0).astype(F32)
    y = (lane // TILE).astype(F32)
    z = (lane % TILE).astype(F32)
    return ramp(x, bits[0]) * (ramp(y, bits[1]) * ramp(z, bits[2]))


def move_x(low, high, bit, roll):
    row = iota(low.shape, 1)
    from_high = jnp.where(row < OVL, roll(high, 6, 1), 0.0)
    from_low = jnp.where(row >= 8 - OVL, roll(low, 2, 1), 0.0)
    return jnp.where(bit == 0, from_high, from_low)


def move_y(low, high, bit, roll):
    lane = iota(low.shape, 2)
    from_high = jnp.where(lane < OVL * TILE, roll(high, 96, 2), 0.0)
    from_low = jnp.where(lane >= 128 - OVL * TILE, roll(low, 32, 2), 0.0)
    return jnp.where(bit == 0, from_high, from_low)


def pack_z(first, second, bit, roll):
    z = iota(first.shape, 2) % TILE
    head = jnp.where(bit == 0, roll(first, 128 - 10, 2), first)
    tail = jnp.where(bit == 0, roll(second, 128 - 2, 2), roll(second, 8, 2))
    return jnp.where(z < 8, head, tail)


def unpack_z(packed, bit, roll):
    z = iota(packed.shape, 2) % TILE
    keep = jnp.where(bit == 0, z - 10, 5 - z) >= 0
    head = jnp.where(bit == 0, roll(packed, 10, 2), packed)
    tail = jnp.where(bit == 0, roll(packed, 2, 2), roll(packed, 128 - 8, 2))
    return jnp.where(keep, head, 0.0), jnp.where(keep, tail, 0.0)


def kernel(
    em_ref, block_ref, slot_ref, w1_ref, b1_ref, w2_ref, b2_ref, wh_ref, bh_ref,
    out_ref,
    em, block, slot, w1, b1, w2, b2, wh, bh,
    sent, arrived, expand, first, second, heads, hidden, two,
    x_out, y_out, z_out, e_out, x_in, y_in, z_in, e_in,
    load_sems, route_send, route_recv, swap_send, swap_recv,
    relayed, relay_send, relay_recv, mate_ready, mates_ready, partners_told,
):
    roll = pltpu.roll
    blocks = SIDE * SIDE
    me = lax.axis_index("blocks")
    own = lax.axis_index("octant")
    bits = [own % 2, own // 2 % 2, own // 4]

    def partner(mask):
        total = 0
        for d in range(3):
            total = total + (1 - bits[d] if mask >> d & 1 else bits[d]) * 2**d
        return total

    my, mz = me // SIDE, me % SIDE
    early = mz < HUBS
    twice = mz < 2
    hubs, others = HUBS * SIDE, SIDE - HUBS
    slot_me = jnp.where(early, my * HUBS + mz, hubs + my * others + mz - HUBS)
    group_me = jnp.where(early, SIDE, my)
    pupils = [my * SIDE + SIDE - 1 - mz, my * SIDE + HUBS + mz]
    relay = my * SIDE + jnp.where(mz >= SIDE - HUBS, SIDE - 1 - mz, mz - HUBS)
    lane_me = jnp.where(mz >= SIDE - HUBS, 0, 1)
    spans = (4, 3, 5, 2, 6, 1, 7, 0)
    rows_first = (0, 1, 7, 2, 6, 3, 5, 4)

    def signal(semaphore, target):
        pl.semaphore_signal(
            semaphore, inc=1, device_id={"blocks": target}, device_id_type=MESH
        )

    def unless(condition, visit):
        if condition is None:
            visit()
        else:
            pl.when(jnp.logical_not(condition))(visit)

    def greet(span, z):
        target = (my + span) % SIDE * SIDE + z
        unless(mz == z if span == 0 and z < HUBS else None, lambda: signal(barrier, target))

    def rows(source, target, semaphores, device):
        return pltpu.make_async_remote_copy(
            src_ref=source,
            dst_ref=target,
            send_sem=semaphores[0],
            recv_sem=semaphores[1],
            device_id={"blocks": device},
            device_id_type=MESH,
        )

    def send(y, z):
        target = y * SIDE + z
        if z < HUBS:
            device, place, semaphore = target, arrived, route_recv
        else:
            hub, lane = RELAYS[z]
            device, place = y * SIDE + hub, relayed.at[lane]
            semaphore = relay_recv.at[lane, group_me]
        copy = rows(sent.at[target], place.at[slot_me], (route_send, semaphore), device)
        unless(me == device, copy.start)

    def landed(count, place, semaphores):
        return rows(place.at[pl.ds(0, count)], place.at[pl.ds(0, count)], semaphores, (me + 1) % blocks)

    loads = [
        pltpu.make_async_copy(source, target, load_sems.at[index])
        for index, (source, target) in enumerate(
            [
                (block_ref, block), (slot_ref, slot), (em_ref, em),
                (w1_ref, w1), (b1_ref, b1), (w2_ref, w2), (b2_ref, b2), (wh_ref, wh), (bh_ref, bh),
            ]
        )
    ]
    barrier = pltpu.get_barrier_semaphore()

    def greet_partners(semaphore):
        for mask in range(1, 8):
            pl.semaphore_signal(
                semaphore, inc=1, device_id={"octant": partner(mask)}, device_id_type=MESH
            )


    @pl.when(early)
    def _():
        for span in spans:
            for z in (6, 5, 7, 4, 0, 3, 1, 2):
                greet(span, z)
        greet_partners(barrier)

    for load in loads[:3]:
        load.start()
    for load in loads[:3]:
        load.wait()
    packed = pack_rows(em[0], block[...], slot[...])
    sent[:, 0, :128] = packed[:64]
    sent[:, 0, 128:] = packed[64:]

    @pl.when(early)
    def _():
        pl.semaphore_wait(barrier, 7 + hubs - 1)
        arrived[slot_me] = sent[me]
        relayed[0, slot_me] = sent[pupils[0]]
        relayed[1, slot_me] = sent[pupils[1]]

    @pl.when(jnp.logical_not(early))
    def _():
        pl.semaphore_wait(barrier, hubs)
        signal(mate_ready.at[lane_me], relay)

    for y in rows_first:
        for z in range(SIDE):
            send(y, z)

    for load in loads[3:]:
        load.start()
    for load in loads[3:]:
        load.wait()
    expand[...] = expander()
    first[...] = first_matrix(w1[...])
    wide = replicated(w2[...].reshape(27 * C1, C1), 2)
    x_inner = iota((C1, 2 * C1), 1) // C1
    for x in range(4):
        for dy in range(3):
            columns = []
            for dz in range(3):
                block_rows = jnp.zeros((C1, 2 * C1), F32)
                for dx in range(3):
                    if 0 <= x + dx - 2 < 2:
                        at = (9 * dx + 3 * dy + dz) * C1
                        block_rows = jnp.where(
                            x_inner == x + dx - 2, wide[at : at + C1], block_rows
                        )
                columns.append(block_rows)
            at = (x * 3 + dy) * C1
            second[at : at + C1, :] = jnp.concatenate(columns, axis=1).astype(BF16)
    heads[...] = head_matrix(wh[...])
    b1_col = column(b1[...])
    b2_col = column(b2[...])
    weights = blend_weights(bits)

    def forward(lane, start, count, awaited, group):
        landed(awaited, relayed.at[lane], (relay_send, relay_recv.at[lane, group])).wait_recv()
        part = pl.ds(start, count)
        rows(
            relayed.at[lane, part], arrived.at[part], (relay_send, route_recv), pupils[lane]
        ).start()

    def begin(lane):
        pl.semaphore_wait(mate_ready.at[lane], 1)
        greet_partners(mates_ready.at[lane])
        forward(lane, 0, hubs, hubs - 1, SIDE)

    def finish(lane):
        pl.semaphore_wait(mates_ready.at[lane], 7)
        signal(partners_told, pupils[lane])

    def also(visit, *numbers):
        pl.when(twice)(functools.partial(visit, 1, *numbers))

    @pl.when(early)
    def _():
        also(begin)
        begin(0)
        for y in rows_first:
            group = (hubs + y * others, others, others, y)
            forward(0, *group)
            also(forward, *group)
        landed(blocks - 1, arrived, (route_send, route_recv)).wait_recv()

    @pl.when(jnp.logical_not(early))
    def _():
        landed(blocks, arrived, (route_send, route_recv)).wait_recv()

    volume = unpack_volume(arrived[:, 0, :], expand[...])
    @pl.when(early)
    def _():
        finish(0)
        also(finish)

    one = dot(first[...], conv1_columns(volume, roll)).reshape(TILE, C1, LANES)
    one = jnp.maximum(one + b1_col[None], 0.0).reshape(TILE * C1, LANES)
    for dz, part in enumerate(z_shifted(one, roll)):
        hidden[:, dz] = part.reshape(8, 2 * C1, LANES)
    y = iota((1, LANES), 1) // TILE

    def complete(x, sums):
        total = sums[1]
        total = total + jnp.where(y > 0, shift_lanes(sums[0], -TILE, roll), 0.0)
        total = total + jnp.where(y < TILE - 1, shift_lanes(sums[2], TILE, roll), 0.0)
        two[x * C1 : x * C1 + C1, :] = jnp.maximum(total + b2_col, 0.0).astype(BF16)

    held = None
    for group in range(8):
        sums = dot(second[...], hidden[group].reshape(6 * C1, LANES)).reshape(4, 3, C1, LANES)
        if held is None:
            complete(0, sums[1])
        else:
            complete(2 * group - 1, held[0] + sums[0])
            complete(2 * group, held[1] + sums[1])
        held = sums[2:]
    complete(TILE - 1, held[0])
    logits = dot(heads[...], two[...])
    pieces = []
    for a in range(AFF):
        pieces.append(jax.nn.sigmoid(logits[a * TILE : a * TILE + TILE] + bh[:, a : a + 1]) * weights)
    blended = jnp.stack(pieces, axis=0)

    tile = [[blended[:, 8 * hx : 8 * hx + 8, 128 * hy : 128 * hy + 128] for hy in range(2)] for hx in range(2)]
    @pl.when(jnp.logical_not(early))
    def _():
        pl.semaphore_wait(partners_told, 1)

    swaps = {}

    def swap(mask, source, target):
        swaps[mask] = pltpu.make_async_remote_copy(
            src_ref=source,
            dst_ref=target,
            send_sem=swap_send.at[mask - 1],
            recv_sem=swap_recv.at[mask - 1],
            device_id={"octant": partner(mask)},
            device_id_type=MESH,
        )
        swaps[mask].start()

    at_x = [move_x(tile[0][hy], tile[1][hy], bits[0], roll) for hy in range(2)]
    e_out[1] = pack_z(at_x[0], at_x[1], bits[2], roll)
    swap(5, e_out.at[1], e_in.at[1])
    at_xy = move_y(at_x[0], at_x[1], bits[1], roll)
    e_out[3] = pack_z(at_xy, at_xy, bits[2], roll)
    swap(7, e_out.at[3], e_in.at[3])
    z_out[:, :8] = pack_z(tile[0][0], tile[0][1], bits[2], roll)
    z_out[:, 8:] = pack_z(tile[1][0], tile[1][1], bits[2], roll)
    swap(4, z_out, z_in)
    at_y = [move_y(tile[hx][0], tile[hx][1], bits[1], roll) for hx in range(2)]
    e_out[2] = pack_z(at_y[0], at_y[1], bits[2], roll)
    swap(6, e_out.at[2], e_in.at[2])
    y_out[:, :8] = at_y[0]
    y_out[:, 8:] = at_y[1]
    swap(2, y_out, y_in)
    e_out[0] = at_xy
    swap(3, e_out.at[0], e_in.at[0])
    x_out[:, :, :128] = at_x[0]
    x_out[:, :, 128:] = at_x[1]
    swap(1, x_out, x_in)

    plane = [[tile[hx][hy] for hy in range(2)] for hx in range(2)]

    def add(hx, hy, value):
        plane[hx][hy] = plane[hx][hy] + value

    def is_half(bit, half, value):
        return jnp.where(bit == 1 - half, value, 0.0)

    swaps[1].wait_recv()
    for hy in range(2):
        value = x_in[:, :, 128 * hy : 128 * hy + 128]
        for hx in range(2):
            add(hx, hy, is_half(bits[0], hx, value))
    swaps[2].wait_recv()
    for hx in range(2):
        value = y_in[:, 8 * hx : 8 * hx + 8]
        for hy in range(2):
            add(hx, hy, is_half(bits[1], hy, value))
    swaps[3].wait_recv()
    swaps[7].wait_recv()
    corner = e_in[0] + unpack_z(e_in[3], bits[2], roll)[0]
    for hx in range(2):
        for hy in range(2):
            add(hx, hy, is_half(bits[0], hx, is_half(bits[1], hy, corner)))
    swaps[6].wait_recv()
    parts = unpack_z(e_in[2], bits[2], roll)
    for hx in range(2):
        for hy in range(2):
            add(hx, hy, is_half(bits[1], hy, parts[hx]))
    swaps[5].wait_recv()
    parts = unpack_z(e_in[1], bits[2], roll)
    for hx in range(2):
        for hy in range(2):
            add(hx, hy, is_half(bits[0], hx, parts[hy]))
    swaps[4].wait_recv()
    for hx in range(2):
        parts = unpack_z(z_in[:, 8 * hx : 8 * hx + 8], bits[2], roll)
        for hy in range(2):
            add(hx, hy, parts[hy])
    for hx in range(2):
        for hy in range(2):
            out_ref[:, pl.ds(TILE * hx + hy, 8, stride=2), :] = plane[hx][hy]
    for copy in swaps.values():
        copy.wait_send()

    @pl.when(early)
    def _():
        landed(blocks - 3, arrived, (route_send, route_recv)).wait_send()
        landed(blocks, arrived, (relay_send, route_recv)).wait_send()

    @pl.when(twice)
    def _():
        landed(blocks, arrived, (relay_send, route_recv)).wait_send()

    @pl.when(mz == HUBS - 1)
    def _():
        landed(1, arrived, (route_send, route_recv)).wait_send()

    @pl.when(jnp.logical_not(early))
    def _():
        landed(blocks, arrived, (route_send, route_recv)).wait_send()


def shards(em_store, route_block, route_slot, conv1_w, conv1_b, conv2_w, conv2_b, head_w, head_b):
    operands = (
        em_store, route_block, route_slot, conv1_w, conv1_b.reshape(1, C1), conv2_w,
        conv2_b.reshape(1, C1), head_w, head_b.reshape(1, AFF),
    )
    operands = tuple(pltpu.with_memory_space_constraint(value, pltpu.HBM) for value in operands)
    vmem = pltpu.VMEM
    result = pl.pallas_call(
        kernel,
        out_shape=jax.ShapeDtypeStruct((AFF, 2 * TILE, 128), F32),
        in_specs=[pl.BlockSpec(memory_space=pltpu.HBM)] * len(operands),
        out_specs=pl.BlockSpec(memory_space=vmem),
        scratch_shapes=[vmem(value.shape, value.dtype) for value in operands]
        + [
            vmem((64, 1, 256), F32),
            vmem((64, 1, 256), F32),
            vmem((128, 4 * 128), BF16),
            vmem((TILE * C1, LANES), BF16),
            vmem((12 * C1, 6 * C1), BF16),
            vmem((AFF * TILE, TILE * C1), BF16),
            vmem((8, 3, 2 * C1, LANES), BF16),
            vmem((TILE * C1, LANES), BF16),
        ]
        + [
            vmem((AFF, 8, 256), F32),
            vmem((AFF, 16, 128), F32),
            vmem((AFF, 16, 128), F32),
            vmem((4, AFF, 8, 128), F32),
        ]
        * 2
        + [
            pltpu.SemaphoreType.DMA((len(operands),)),
            pltpu.SemaphoreType.DMA,
            pltpu.SemaphoreType.DMA,
            pltpu.SemaphoreType.DMA((7,)),
            pltpu.SemaphoreType.DMA((7,)),
        ]
        + [
            vmem((2, 64, 1, 256), F32),
            pltpu.SemaphoreType.DMA,
            pltpu.SemaphoreType.DMA((2, SIDE + 1)),
            pltpu.SemaphoreType.REGULAR((2,)),
            pltpu.SemaphoreType.REGULAR((2,)),
            pltpu.SemaphoreType.REGULAR,
        ],
        compiler_params=pltpu.CompilerParams(
            collective_id=0, has_side_effects=True, vmem_limit_bytes=32 * 1024 * 1024
        ),
    )(*operands)
    return result.reshape(1, 1, AFF, TILE * LANES)


def solution(mesh):
    in_specs = (P("octant", "blocks", None), P("octant", "blocks"), P("octant", "blocks")) + (P(),) * 6
    out_specs = P("octant", "blocks", None, None)
    return jax.shard_map(shards, mesh=mesh, in_specs=in_specs, out_specs=out_specs, check_vma=False)
```

```python
import functools

import jax
import jax.numpy as jnp
from jax import lax
from jax.experimental import pallas as pl
from jax.experimental.pallas import tpu as pltpu
from jax.sharding import PartitionSpec as P

TILE = 16
OVL = 6
LANES = TILE * TILE
C1 = 32
SIDE = 8
HUBS = 3
RELAYS = {7: (0, 0), 6: (1, 0), 5: (2, 0), 4: (1, 1), 3: (0, 1)}
AFF = 3
MESH = pl.DeviceIdType.MESH
F32 = jnp.float32
BF16 = jnp.bfloat16


def iota(shape, dim):
    return lax.broadcasted_iota(jnp.int32, shape, dim)


def dot(a, b):
    return jnp.dot(a, b, preferred_element_type=F32)


def column(row):
    n = row.shape[1]
    return jnp.sum(jnp.where(iota((n, n), 0) == iota((n, n), 1), row, 0.0), axis=1, keepdims=True)


def pack_rows(em, targets, slots):
    n = em.shape[0]
    target_row = targets.astype(F32)
    target_col = column(target_row)
    earlier = (target_col == target_row) & (iota((n, n), 0) < iota((n, n), 1))
    rank_row = jnp.sum(jnp.where(earlier, 1.0, 0.0), axis=0, keepdims=True)
    slot_row = slots
    i_col = column((slot_row // 16 + 1).astype(F32))
    jk_col = column((slot_row % 16).astype(F32))
    lane = iota((n, 64), 1)
    labels = jnp.where(lane == 0, i_col, jnp.where(lane == 1, jk_col, 0.0)).astype(BF16)
    wide = jnp.concatenate([em, labels], axis=1)
    row = iota((128, n), 0)
    here = ((row % 64).astype(F32) == target_row) & ((row // 64).astype(F32) == rank_row)
    return dot(here.astype(F32).astype(BF16), wide)


def expander():
    row = iota((128, 4 * 128), 0)
    col = iota((128, 4 * 128), 1)
    wanted = (col // 128) * 16 + (col // 16 % 4) * 4 + col % 4
    return (row == wanted).astype(F32).astype(BF16)


def unpack_volume(arrived, expand):
    rows = jnp.concatenate([arrived[:, :128], arrived[:, 128:]], axis=0)
    i_col = rows[:, 64:65]
    jk_col = rows[:, 65:66]
    eye = iota((128, 128), 0) == iota((128, 128), 1)
    i_row = jnp.sum(jnp.where(eye, i_col, 0.0), axis=0, keepdims=True)
    lane = iota((128, LANES), 1)
    lane_jk = (lane // 64 * 4 + lane // 4 % 4).astype(F32)
    inside = lane_jk == jk_col
    spread = dot(rows.astype(BF16), expand)
    x_row = iota((TILE, 128), 0)
    volume = jnp.zeros((TILE, LANES), F32)
    for a in range(4):
        part = spread[:, a * 128 : a * 128 + 128]
        masked = jnp.where(inside, jnp.concatenate([part, part], axis=1), 0.0).astype(BF16)
        wanted = (x_row % 4 == a) & ((x_row // 4 + 1).astype(F32) == i_row)
        volume = volume + dot(wanted.astype(F32).astype(BF16), masked)
    return volume


def first_matrix(conv1_w):
    tap = iota((27, LANES), 0)
    col = iota((27, LANES), 1)
    x_in = iota((TILE, C1, LANES), 2) % TILE
    x_out = iota((TILE, C1, LANES), 0)
    total = jnp.zeros((TILE, C1, LANES), F32)
    for dx in range(3):
        spread = ((tap == 9 * dx + col // TILE) & (col < 9 * TILE)).astype(F32).astype(BF16)
        rows = dot(conv1_w, spread)
        total = jnp.where(x_in == x_out + dx - 1, rows[None], total)
    return total.reshape(TILE * C1, LANES).astype(BF16)


def replicated(weights, count):
    shape = (C1, count * C1)
    return dot(weights, (iota(shape, 0) == iota(shape, 1) % C1).astype(F32).astype(BF16))


def shift_lanes(value, by, roll):
    return roll(value, (-by) % value.shape[-1], value.ndim - 1)


def conv1_columns(volume, roll):
    lane = iota((TILE, LANES), 1)
    y, z = lane // TILE, lane % TILE
    rows = []
    for dy in (-1, 0, 1):
        for dz in (-1, 0, 1):
            moved = volume
            if dy or dz:
                moved = shift_lanes(volume, dy * TILE + dz, roll)
                keep = (y + dy >= 0) & (y + dy < TILE) & (z + dz >= 0) & (z + dz < TILE)
                moved = jnp.where(keep, moved, 0.0)
            rows.append(moved)
    rows.append(jnp.zeros((LANES - 9 * TILE, LANES), F32))
    return jnp.concatenate(rows, axis=0).astype(BF16)


def z_shifted(value, roll):
    z = iota((1, LANES), 1) % TILE
    value = value.astype(BF16)
    before = shift_lanes(value, -1, roll) * jnp.where(z > 0, 1.0, 0.0).astype(BF16)
    after = shift_lanes(value, 1, roll) * jnp.where(z < TILE - 1, 1.0, 0.0).astype(BF16)
    return [before, value, after]


def head_matrix(head_w):
    wide = replicated(head_w, TILE)
    x_in = iota((TILE, TILE * C1), 1) // C1
    x_out = iota((TILE, TILE * C1), 0)
    rows = [jnp.where(x_in == x_out, wide[a : a + 1], 0.0) for a in range(AFF)]
    return jnp.concatenate(rows, axis=0).astype(BF16)


def ramp(position, bit):
    lower = jnp.minimum((TILE - position - 0.5) / OVL, 1.0)
    upper = jnp.minimum((position + 0.5) / OVL, 1.0)
    return jnp.where(bit == 1, upper, lower)


def blend_weights(bits):
    lane = iota((TILE, LANES), 1)
    x = iota((TILE, LANES), 0).astype(F32)
    y = (lane // TILE).astype(F32)
    z = (lane % TILE).astype(F32)
    return ramp(x, bits[0]) * (ramp(y, bits[1]) * ramp(z, bits[2]))


def move_x(low, high, bit, roll):
    row = iota(low.shape, 1)
    from_high = jnp.where(row < OVL, roll(high, 6, 1), 0.0)
    from_low = jnp.where(row >= 8 - OVL, roll(low, 2, 1), 0.0)
    return jnp.where(bit == 0, from_high, from_low)


def move_y(low, high, bit, roll):
    lane = iota(low.shape, 2)
    from_high = jnp.where(lane < OVL * TILE, roll(high, 96, 2), 0.0)
    from_low = jnp.where(lane >= 128 - OVL * TILE, roll(low, 32, 2), 0.0)
    return jnp.where(bit == 0, from_high, from_low)


def pack_z(first, second, bit, roll):
    z = iota(first.shape, 2) % TILE
    head = jnp.where(bit == 0, roll(first, 128 - 10, 2), first)
    tail = jnp.where(bit == 0, roll(second, 128 - 2, 2), roll(second, 8, 2))
    return jnp.where(z < 8, head, tail)


def unpack_z(packed, bit, roll):
    z = iota(packed.shape, 2) % TILE
    keep = jnp.where(bit == 0, z - 10, 5 - z) >= 0
    head = jnp.where(bit == 0, roll(packed, 10, 2), packed)
    tail = jnp.where(bit == 0, roll(packed, 2, 2), roll(packed, 128 - 8, 2))
    return jnp.where(keep, head, 0.0), jnp.where(keep, tail, 0.0)


def kernel(
    em_ref, block_ref, slot_ref, w1_ref, b1_ref, w2_ref, b2_ref, wh_ref, bh_ref,
    out_ref,
    em, block, slot, w1, b1, w2, b2, wh, bh,
    sent, arrived, expand, first, second, heads, hidden, two,
    x_out, y_out, z_out, e_out, x_in, y_in, z_in, e_in,
    load_sems, route_send, route_recv, swap_send, swap_recv,
    relayed, relay_send, relay_recv, mate_ready, mates_ready, partners_told,
):
    roll = pltpu.roll
    blocks = SIDE * SIDE
    me = lax.axis_index("blocks")
    own = lax.axis_index("octant")
    bits = [own % 2, own // 2 % 2, own // 4]

    def partner(mask):
        total = 0
        for d in range(3):
            total = total + (1 - bits[d] if mask >> d & 1 else bits[d]) * 2**d
        return total

    my, mz = me // SIDE, me % SIDE
    early = mz < HUBS
    twice = mz < 2
    hubs, others = HUBS * SIDE, SIDE - HUBS
    slot_me = jnp.where(early, my * HUBS + mz, hubs + my * others + mz - HUBS)
    group_me = jnp.where(early, SIDE, my)
    pupils = [my * SIDE + SIDE - 1 - mz, my * SIDE + HUBS + mz]
    relay = my * SIDE + jnp.where(mz >= SIDE - HUBS, SIDE - 1 - mz, mz - HUBS)
    lane_me = jnp.where(mz >= SIDE - HUBS, 0, 1)
    spans = (4, 3, 5, 2, 6, 1, 7, 0)
    rows_first = (0, 1, 7, 2, 6, 3, 5, 4)

    def signal(semaphore, target):
        pl.semaphore_signal(
            semaphore, inc=1, device_id={"blocks": target}, device_id_type=MESH
        )

    def unless(condition, visit):
        if condition is None:
            visit()
        else:
            pl.when(jnp.logical_not(condition))(visit)

    def greet(span, z):
        target = (my + span) % SIDE * SIDE + z
        unless(mz == z if span == 0 and z < HUBS else None, lambda: signal(barrier, target))

    def rows(source, target, semaphores, device):
        return pltpu.make_async_remote_copy(
            src_ref=source,
            dst_ref=target,
            send_sem=semaphores[0],
            recv_sem=semaphores[1],
            device_id={"blocks": device},
            device_id_type=MESH,
        )

    def send(y, z):
        target = y * SIDE + z
        if z < HUBS:
            device, place, semaphore = target, arrived, route_recv
        else:
            hub, lane = RELAYS[z]
            device, place = y * SIDE + hub, relayed.at[lane]
            semaphore = relay_recv.at[lane, group_me]
        copy = rows(sent.at[target], place.at[slot_me], (route_send, semaphore), device)
        unless(me == device, copy.start)

    def landed(count, place, semaphores):
        return rows(place.at[pl.ds(0, count)], place.at[pl.ds(0, count)], semaphores, (me + 1) % blocks)

    loads = [
        pltpu.make_async_copy(source, target, load_sems.at[index])
        for index, (source, target) in enumerate(
            [
                (block_ref, block), (slot_ref, slot), (em_ref, em),
                (w1_ref, w1), (b1_ref, b1), (w2_ref, w2), (b2_ref, b2), (wh_ref, wh), (bh_ref, bh),
            ]
        )
    ]
    barrier = pltpu.get_barrier_semaphore()

    def greet_partners(semaphore):
        for mask in range(1, 8):
            pl.semaphore_signal(
                semaphore, inc=1, device_id={"octant": partner(mask)}, device_id_type=MESH
            )


    @pl.when(early)
    def _():
        for span in spans:
            for z in (6, 5, 7, 4, 0, 3, 1, 2):
                greet(span, z)
        greet_partners(barrier)

    for load in loads[:3]:
        load.start()
    for load in loads[:3]:
        load.wait()
    packed = pack_rows(em[0], block[...], slot[...])
    sent[:, 0, :128] = packed[:64]
    sent[:, 0, 128:] = packed[64:]

    @pl.when(early)
    def _():
        pl.semaphore_wait(barrier, 7 + hubs - 1)
        arrived[slot_me] = sent[me]
        relayed[0, slot_me] = sent[pupils[0]]
        relayed[1, slot_me] = sent[pupils[1]]

    @pl.when(jnp.logical_not(early))
    def _():
        pl.semaphore_wait(barrier, hubs)
        signal(mate_ready.at[lane_me], relay)

    for y in rows_first:
        for z in range(SIDE):
            send(y, z)

    for load in loads[3:]:
        load.start()
    for load in loads[3:]:
        load.wait()
    expand[...] = expander()
    first[...] = first_matrix(w1[...])
    wide = replicated(w2[...].reshape(27 * C1, C1), 2)
    x_inner = iota((C1, 2 * C1), 1) // C1
    for x in range(4):
        for dy in range(3):
            columns = []
            for dz in range(3):
                block_rows = jnp.zeros((C1, 2 * C1), F32)
                for dx in range(3):
                    if 0 <= x + dx - 2 < 2:
                        at = (9 * dx + 3 * dy + dz) * C1
                        block_rows = jnp.where(
                            x_inner == x + dx - 2, wide[at : at + C1], block_rows
                        )
                columns.append(block_rows)
            at = (x * 3 + dy) * C1
            second[at : at + C1, :] = jnp.concatenate(columns, axis=1).astype(BF16)
    heads[...] = head_matrix(wh[...])
    b1_col = column(b1[...])
    b2_col = column(b2[...])
    weights = blend_weights(bits)

    def forward(lane, start, count, awaited, group):
        landed(awaited, relayed.at[lane], (relay_send, relay_recv.at[lane, group])).wait_recv()
        part = pl.ds(start, count)
        rows(
            relayed.at[lane, part], arrived.at[part], (relay_send, route_recv), pupils[lane]
        ).start()

    def begin(lane):
        pl.semaphore_wait(mate_ready.at[lane], 1)
        greet_partners(mates_ready.at[lane])
        forward(lane, 0, hubs, hubs - 1, SIDE)

    def finish(lane):
        pl.semaphore_wait(mates_ready.at[lane], 7)
        signal(partners_told, pupils[lane])

    def also(visit, *numbers):
        pl.when(twice)(functools.partial(visit, 1, *numbers))

    @pl.when(early)
    def _():
        also(begin)
        begin(0)
        for y in rows_first:
            group = (hubs + y * others, others, others, y)
            forward(0, *group)
            also(forward, *group)
        landed(blocks - 1, arrived, (route_send, route_recv)).wait_recv()

    @pl.when(jnp.logical_not(early))
    def _():
        landed(blocks, arrived, (route_send, route_recv)).wait_recv()

    volume = unpack_volume(arrived[:, 0, :], expand[...])
    @pl.when(early)
    def _():
        finish(0)
        also(finish)

    one = dot(first[...], conv1_columns(volume, roll)).reshape(TILE, C1, LANES)
    one = jnp.maximum(one + b1_col[None], 0.0).reshape(TILE * C1, LANES)
    for dz, part in enumerate(z_shifted(one, roll)):
        hidden[:, dz] = part.reshape(8, 2 * C1, LANES)
    y = iota((1, LANES), 1) // TILE

    def complete(x, sums):
        total = sums[1]
        total = total + jnp.where(y > 0, shift_lanes(sums[0], -TILE, roll), 0.0)
        total = total + jnp.where(y < TILE - 1, shift_lanes(sums[2], TILE, roll), 0.0)
        two[x * C1 : x * C1 + C1, :] = jnp.maximum(total + b2_col, 0.0).astype(BF16)

    held = None
    for group in range(8):
        sums = dot(second[...], hidden[group].reshape(6 * C1, LANES)).reshape(4, 3, C1, LANES)
        if held is None:
            complete(0, sums[1])
        else:
            complete(2 * group - 1, held[0] + sums[0])
            complete(2 * group, held[1] + sums[1])
        held = sums[2:]
    complete(TILE - 1, held[0])
    logits = dot(heads[...], two[...])
    pieces = []
    for a in range(AFF):
        pieces.append(jax.nn.sigmoid(logits[a * TILE : a * TILE + TILE] + bh[:, a : a + 1]) * weights)
    blended = jnp.stack(pieces, axis=0)

    tile = [[blended[:, 8 * hx : 8 * hx + 8, 128 * hy : 128 * hy + 128] for hy in range(2)] for hx in range(2)]
    @pl.when(jnp.logical_not(early))
    def _():
        pl.semaphore_wait(partners_told, 1)

    swaps = {}

    def swap(mask, source, target):
        swaps[mask] = pltpu.make_async_remote_copy(
            src_ref=source,
            dst_ref=target,
            send_sem=swap_send.at[mask - 1],
            recv_sem=swap_recv.at[mask - 1],
            device_id={"octant": partner(mask)},
            device_id_type=MESH,
        )
        swaps[mask].start()

    at_x = [move_x(tile[0][hy], tile[1][hy], bits[0], roll) for hy in range(2)]
    e_out[1] = pack_z(at_x[0], at_x[1], bits[2], roll)
    swap(5, e_out.at[1], e_in.at[1])
    at_xy = move_y(at_x[0], at_x[1], bits[1], roll)
    e_out[3] = pack_z(at_xy, at_xy, bits[2], roll)
    swap(7, e_out.at[3], e_in.at[3])
    e_out[0] = at_xy
    swap(3, e_out.at[0], e_in.at[0])
    at_y = [move_y(tile[hx][0], tile[hx][1], bits[1], roll) for hx in range(2)]
    e_out[2] = pack_z(at_y[0], at_y[1], bits[2], roll)
    swap(6, e_out.at[2], e_in.at[2])
    z_out[:, :8] = pack_z(tile[0][0], tile[0][1], bits[2], roll)
    z_out[:, 8:] = pack_z(tile[1][0], tile[1][1], bits[2], roll)
    swap(4, z_out, z_in)
    y_out[:, :8] = at_y[0]
    y_out[:, 8:] = at_y[1]
    swap(2, y_out, y_in)
    x_out[:, :, :128] = at_x[0]
    x_out[:, :, 128:] = at_x[1]
    swap(1, x_out, x_in)

    plane = [[tile[hx][hy] for hy in range(2)] for hx in range(2)]

    def add(hx, hy, value):
        plane[hx][hy] = plane[hx][hy] + value

    def is_half(bit, half, value):
        return jnp.where(bit == 1 - half, value, 0.0)

    swaps[1].wait_recv()
    for hy in range(2):
        value = x_in[:, :, 128 * hy : 128 * hy + 128]
        for hx in range(2):
            add(hx, hy, is_half(bits[0], hx, value))
    swaps[2].wait_recv()
    for hx in range(2):
        value = y_in[:, 8 * hx : 8 * hx + 8]
        for hy in range(2):
            add(hx, hy, is_half(bits[1], hy, value))
    swaps[3].wait_recv()
    swaps[7].wait_recv()
    corner = e_in[0] + unpack_z(e_in[3], bits[2], roll)[0]
    for hx in range(2):
        for hy in range(2):
            add(hx, hy, is_half(bits[0], hx, is_half(bits[1], hy, corner)))
    swaps[6].wait_recv()
    parts = unpack_z(e_in[2], bits[2], roll)
    for hx in range(2):
        for hy in range(2):
            add(hx, hy, is_half(bits[1], hy, parts[hx]))
    swaps[5].wait_recv()
    parts = unpack_z(e_in[1], bits[2], roll)
    for hx in range(2):
        for hy in range(2):
            add(hx, hy, is_half(bits[0], hx, parts[hy]))
    swaps[4].wait_recv()
    for hx in range(2):
        parts = unpack_z(z_in[:, 8 * hx : 8 * hx + 8], bits[2], roll)
        for hy in range(2):
            add(hx, hy, parts[hy])
    for hx in range(2):
        for hy in range(2):
            out_ref[:, pl.ds(TILE * hx + hy, 8, stride=2), :] = plane[hx][hy]
    for copy in swaps.values():
        copy.wait_send()

    @pl.when(early)
    def _():
        landed(blocks - 3, arrived, (route_send, route_recv)).wait_send()
        landed(blocks, arrived, (relay_send, route_recv)).wait_send()

    @pl.when(twice)
    def _():
        landed(blocks, arrived, (relay_send, route_recv)).wait_send()

    @pl.when(mz == HUBS - 1)
    def _():
        landed(1, arrived, (route_send, route_recv)).wait_send()

    @pl.when(jnp.logical_not(early))
    def _():
        landed(blocks, arrived, (route_send, route_recv)).wait_send()


def shards(em_store, route_block, route_slot, conv1_w, conv1_b, conv2_w, conv2_b, head_w, head_b):
    operands = (
        em_store, route_block, route_slot, conv1_w, conv1_b.reshape(1, C1), conv2_w,
        conv2_b.reshape(1, C1), head_w, head_b.reshape(1, AFF),
    )
    operands = tuple(pltpu.with_memory_space_constraint(value, pltpu.HBM) for value in operands)
    vmem = pltpu.VMEM
    result = pl.pallas_call(
        kernel,
        out_shape=jax.ShapeDtypeStruct((AFF, 2 * TILE, 128), F32),
        in_specs=[pl.BlockSpec(memory_space=pltpu.HBM)] * len(operands),
        out_specs=pl.BlockSpec(memory_space=vmem),
        scratch_shapes=[vmem(value.shape, value.dtype) for value in operands]
        + [
            vmem((64, 1, 256), F32),
            vmem((64, 1, 256), F32),
            vmem((128, 4 * 128), BF16),
            vmem((TILE * C1, LANES), BF16),
            vmem((12 * C1, 6 * C1), BF16),
            vmem((AFF * TILE, TILE * C1), BF16),
            vmem((8, 3, 2 * C1, LANES), BF16),
            vmem((TILE * C1, LANES), BF16),
        ]
        + [
            vmem((AFF, 8, 256), F32),
            vmem((AFF, 16, 128), F32),
            vmem((AFF, 16, 128), F32),
            vmem((4, AFF, 8, 128), F32),
        ]
        * 2
        + [
            pltpu.SemaphoreType.DMA((len(operands),)),
            pltpu.SemaphoreType.DMA,
            pltpu.SemaphoreType.DMA,
            pltpu.SemaphoreType.DMA((7,)),
            pltpu.SemaphoreType.DMA((7,)),
        ]
        + [
            vmem((2, 64, 1, 256), F32),
            pltpu.SemaphoreType.DMA,
            pltpu.SemaphoreType.DMA((2, SIDE + 1)),
            pltpu.SemaphoreType.REGULAR((2,)),
            pltpu.SemaphoreType.REGULAR((2,)),
            pltpu.SemaphoreType.REGULAR,
        ],
        compiler_params=pltpu.CompilerParams(
            collective_id=0, has_side_effects=True, vmem_limit_bytes=32 * 1024 * 1024
        ),
    )(*operands)
    return result.reshape(1, 1, AFF, TILE * LANES)


def solution(mesh):
    in_specs = (P("octant", "blocks", None), P("octant", "blocks"), P("octant", "blocks")) + (P(),) * 6
    out_specs = P("octant", "blocks", None, None)
    return jax.shard_map(shards, mesh=mesh, in_specs=in_specs, out_specs=out_specs, check_vma=False)
```
